32 devices in a mesh: leaf: 4 (over x, core), oct: 8 (over z, y).
Axes of the slice: x: 2, y: 2, z: 4, core: 2. Of those that a mesh axis runs over, the one named last changes fastest.
Arguments:
- dens_fine: bfloat16 [152, 4608], P(None, ('leaf', 'oct')), may hold values from -6 to 6
- parent: int32 [4608], P(('leaf', 'oct')), may hold values from 0 to 1023, as said below
- child_code: int32 [4608], P(('leaf', 'oct')), may hold values from 0 to 7, as said below
- m2m_ops: bfloat16 [152, 8, 152], replicated, may hold values from -0.15625 to 0.15625
- m2l_ops: bfloat16 [152, 152, 316], replicated, may hold values from -0.02734375 to 0.02734375
- ask_fine: int32 [32, 32, 16], P(('leaf', 'oct')), may hold values from -1 to 143, as said below
- list_fine: int32 [4608, 316], P(('leaf', 'oct')), may hold values from -1 to 655, as said below
- ask_coarse: int32 [32, 32, 8], P(('leaf', 'oct')), may hold values from -1 to 31, as said below
- list_coarse: int32 [1024, 316], P(('leaf', 'oct')), may hold values from -1 to 287, as said below
Outputs:
- pot_fine: float32 [152, 4608], P(None, ('leaf', 'oct'))
- pot_coarse: float32 [152, 1024], P(None, ('leaf', 'oct'))
The draws below stay inside these ranges and needn't reach their ends.
Inputs may be any that keep to these rules, and one draw needn't show every extreme that they name: parent[i] is a coarse octant of the device that holds fine octant i; parents never fall along the array; every coarse octant has 1 to 8 children and some has 8. `child_code`: the children of one coarse octant carry distinct codes, increasing along the array. ask_fine[d, e] lists distinct fine octants of device e, then -1 to the end; row d, d is all -1; some row holds 16 octants. `list_fine`: an entry other than -1 names an own octant (below 144) or a slot of ask_fine[d] that isn't -1; each target has at most 189 entries other than -1, and some target has exactly 189. ask_coarse[d, e] lists distinct coarse octants of device e, then -1 to the end; row d, d is all -1; some row holds 8 octants. `list_coarse`: an entry other than -1 names an own octant (below 32) or a slot of ask_coarse[d] that isn't -1; each target has at most 189 entries other than -1, and some target has exactly 189.
All inputs are finite; a program needn't handle non-finite values.
Results may differ from the reference program's by a relative error of at most 0.0029.
Values may be sent and summed in bfloat16 or wider, within the bound.
No kernel may reach another device: no remote copies, remote signals or barrier semaphores. Data moves between devices by JAX's collectives and lax.ppermute only.
A program may use at most 192 MiB of HBM per device.

```python
import jax
import jax.numpy as jnp
from jax import lax

P_SIZE = 152
OFFS = 316
LIST = 189
COARSE_DEV = 32
FINE_DEV = 144
FINE_CAP = 16
COARSE_CAP = 8
PEERS = 32
FINE_ALL = 4608
COARSE_ALL = 1024


def tree_layout(key):
    key_tree = jax.random.fold_in(key, 101)
    key_slots, key_forced, key_codes = jax.random.split(key_tree, 3)
    slot_total = 7 * COARSE_DEV
    slot_ids = jnp.arange(slot_total, dtype=jnp.int32)
    slot_owner = slot_ids // 7
    forced = jax.random.randint(key_forced, (PEERS,), 0, COARSE_DEV)
    scores = jax.random.randint(key_slots, (PEERS, slot_total), 0, 2 ** 18) * slot_total + slot_ids
    scores = jnp.where(slot_owner[None, :] == forced[:, None], slot_ids[None, :] - slot_total, scores)
    slot_ranks = jnp.argsort(jnp.argsort(scores, axis=1), axis=1)
    slot_taken = (slot_ranks < FINE_DEV - COARSE_DEV).astype(jnp.int32)
    counts = 1 + slot_taken.reshape(PEERS, COARSE_DEV, 7).sum(axis=2)
    parent_ends = jnp.cumsum(counts, axis=1)
    parent_starts = parent_ends - counts
    children = jnp.arange(FINE_DEV, dtype=jnp.int32)
    local_parent = jnp.sum((children[None, :, None] >= parent_ends[:, None, :]).astype(jnp.int32), axis=2)
    rank_inside = children[None, :] - jnp.take_along_axis(parent_starts, local_parent, axis=1)
    code_scores = jax.random.randint(key_codes, (PEERS, COARSE_DEV, 8), 0, 2 ** 18) * 8 + jnp.arange(8, dtype=jnp.int32)
    code_rank = jnp.argsort(jnp.argsort(code_scores, axis=2), axis=2)
    chosen = (code_rank < counts[:, :, None]).astype(jnp.int32)
    order_inside = jnp.cumsum(chosen, axis=2) - 1
    spread_index = jnp.broadcast_to(local_parent[:, :, None], (PEERS, FINE_DEV, 8))
    chosen_child = jnp.take_along_axis(chosen, spread_index, axis=1)
    order_child = jnp.take_along_axis(order_inside, spread_index, axis=1)
    code_match = (chosen_child == 1) & (order_child == rank_inside[:, :, None])
    child_codes = jnp.sum(jnp.where(code_match, jnp.arange(8, dtype=jnp.int32), 0), axis=2)
    parents = jnp.arange(PEERS, dtype=jnp.int32)[:, None] * COARSE_DEV + local_parent
    return (parents.reshape(-1).astype(jnp.int32), child_codes.reshape(-1).astype(jnp.int32))


def fetch_layout(key, salt_value, own_count, capacity):
    key_fetch = jax.random.fold_in(key, salt_value)
    subkeys = jax.random.split(key_fetch, 11)
    asker_ids = jnp.arange(PEERS, dtype=jnp.int32)[:, None]
    theirs = jnp.arange(PEERS, dtype=jnp.int32)[None, :]
    active = jax.random.bernoulli(subkeys[0], 0.8, (PEERS, PEERS))
    wanted = jnp.where(active, jax.random.randint(subkeys[1], (PEERS, PEERS), 1, capacity + 1), 0)
    offset_peer = jax.random.randint(subkeys[2], (PEERS,), 1, PEERS)
    chosen_peer = theirs == (asker_ids + offset_peer[:, None]) % PEERS
    wanted = jnp.where(chosen_peer, jnp.maximum(wanted, 1), wanted)
    full_device = jax.random.randint(subkeys[3], (), 0, PEERS)
    wanted = jnp.where(chosen_peer & (asker_ids == full_device), capacity, wanted)
    wanted = jnp.where(asker_ids == theirs, 0, wanted)
    local_ids = jnp.arange(own_count, dtype=jnp.int32)
    scores = jax.random.randint(subkeys[4], (PEERS, PEERS, own_count), 0, 2 ** 18) * own_count + local_ids
    picked = jnp.argsort(scores, axis=2)[:, :, :capacity].astype(jnp.int32)
    ask_table = jnp.where(jnp.arange(capacity, dtype=jnp.int32) < wanted[:, :, None], picked, -1)
    slot_valid = (ask_table >= 0).reshape(PEERS, PEERS * capacity).astype(jnp.int32)
    valid_order = jnp.argsort(1 - slot_valid, axis=1, stable=True).astype(jnp.int32)
    valid_count = jnp.sum(slot_valid, axis=1)
    draw_shape = (PEERS, own_count, OFFS)
    present_count = jax.random.randint(subkeys[5], (PEERS, own_count), LIST // 2, LIST + 1)
    forced_target = jax.random.randint(subkeys[6], (PEERS,), 0, own_count)
    present_count = jnp.where(local_ids[None, :] == forced_target[:, None], LIST, present_count)
    offset_scores = jax.random.randint(subkeys[7], draw_shape, 0, 2 ** 18) * OFFS + jnp.arange(OFFS, dtype=jnp.int32)
    offset_rank = jnp.argsort(jnp.argsort(offset_scores, axis=2), axis=2)
    present = offset_rank < present_count[:, :, None]
    is_local = jax.random.bernoulli(subkeys[8], 0.65, draw_shape)
    local_pick = jax.random.randint(subkeys[9], draw_shape, 0, own_count)
    remote_pick = jax.random.randint(subkeys[10], draw_shape, 0, valid_count[:, None, None])
    remote_slot = jnp.take_along_axis(valid_order, remote_pick.reshape(PEERS, -1), axis=1).reshape(draw_shape)
    entries = jnp.where(present, jnp.where(is_local, local_pick, own_count + remote_slot), -1)
    return (ask_table.astype(jnp.int32), entries.reshape(PEERS * own_count, OFFS).astype(jnp.int32))


def draw_parent(key, part):
    layout = tree_layout(key)
    return layout[0]


def draw_child_code(key, part):
    layout = tree_layout(key)
    return layout[1]


def draw_ask_fine(key, part):
    layout = fetch_layout(key, 202, FINE_DEV, FINE_CAP)
    return layout[0]


def draw_list_fine(key, part):
    layout = fetch_layout(key, 202, FINE_DEV, FINE_CAP)
    return layout[1]


def draw_ask_coarse(key, part):
    layout = fetch_layout(key, 303, COARSE_DEV, COARSE_CAP)
    return layout[0]


def draw_list_coarse(key, part):
    layout = fetch_layout(key, 303, COARSE_DEV, COARSE_CAP)
    return layout[1]


def shard_levels(stream_key, shape, shards, low, high):
    loudness = 1.0
    for axis_at, parts in shards:
        heights = jax.random.uniform(jax.random.fold_in(jax.random.fold_in(stream_key, 6), axis_at), (parts,), jnp.float32, low / len(shards), high / len(shards))
        loudness = loudness * jnp.repeat(jnp.exp(heights), shape[axis_at] // parts).reshape((-1,) + (1,) * (len(shape) - 1 - axis_at))
    return loudness


def gaussian(stream_key, extent, width, bound, shards=(), kind=jnp.bfloat16):
    loudness = shard_levels(stream_key, extent, shards, -0.22, 0.18) if shards else 1.0
    array = jax.random.normal(stream_key, extent, jnp.float32) * width * loudness
    return jnp.minimum(jnp.maximum(array, -bound), bound).astype(kind)


def setup_inputs(seed: int = 0) -> dict:
    streams_of = jax.random.split(jax.random.key(seed), 10)
    return {
        "dens_fine": gaussian(streams_of[0], (P_SIZE, FINE_ALL), 1.0, 6.0, ((1, 32),)),
        "parent": draw_parent(jax.random.fold_in(streams_of[9], 71), 0),
        "child_code": draw_child_code(jax.random.fold_in(streams_of[9], 71), 0),
        "m2m_ops": gaussian(streams_of[3], (P_SIZE, 8, P_SIZE), (8 * P_SIZE) ** -0.5, 0.15625),
        "m2l_ops": gaussian(streams_of[4], (P_SIZE, P_SIZE, OFFS), (P_SIZE * OFFS) ** -0.5, 0.02734375),
        "ask_fine": draw_ask_fine(jax.random.fold_in(streams_of[9], 71), 0),
        "list_fine": draw_list_fine(jax.random.fold_in(streams_of[9], 71), 0),
        "ask_coarse": draw_ask_coarse(jax.random.fold_in(streams_of[9], 71), 0),
        "list_coarse": draw_list_coarse(jax.random.fold_in(streams_of[9], 71), 0),
    }


def resolve_and_apply(densities, ask_table, lists, own_count, capacity, m2l_ops):
    surface = densities.shape[0]
    all_cols = densities.shape[1]
    padded = jnp.concatenate([densities, jnp.zeros((surface, 1), densities.dtype)], axis=1)
    operators = m2l_ops.astype(jnp.float32)

    def per_device(device):
        entries = lax.dynamic_slice_in_dim(lists, device * own_count, own_count, 0)
        remote = jnp.maximum(entries - own_count, 0)
        source_peer = remote // capacity
        asked_idx = ask_table[device][source_peer, remote % capacity]
        source_cols = jnp.where(entries < 0, all_cols,
                                jnp.where(entries < own_count, device * own_count + entries,
                                          jnp.where(asked_idx < 0, all_cols, source_peer * own_count + asked_idx)))
        gathered = padded[:, source_cols.T].astype(jnp.float32)
        return jnp.einsum("abc,bct->at", operators, gathered, precision=lax.Precision.HIGHEST)

    blocks = lax.map(per_device, jnp.arange(PEERS, dtype=jnp.int32))
    return jnp.transpose(blocks, (1, 0, 2)).reshape(surface, PEERS * own_count)


def reference(dens_fine, parent, child_code, m2m_ops, m2l_ops, ask_fine, list_fine, ask_coarse, list_coarse):
    child_terms = jnp.zeros((P_SIZE, FINE_ALL), jnp.float32)
    for position in range(8):
        selected = jnp.where(child_code[None, :] == position, dens_fine, jnp.zeros((), dens_fine.dtype))
        child_terms = child_terms + jnp.dot(m2m_ops[:, position, :], selected, preferred_element_type=jnp.float32)
    dens_coarse = jax.ops.segment_sum(child_terms.T, parent, num_segments=COARSE_ALL).T.astype(jnp.bfloat16)
    pot_fine = resolve_and_apply(dens_fine, ask_fine, list_fine, FINE_DEV, FINE_CAP, m2l_ops)
    pot_coarse = 0.5 * resolve_and_apply(dens_coarse, ask_coarse, list_coarse, COARSE_DEV, COARSE_CAP, m2l_ops)
    return pot_fine, pot_coarse
```

```python
import functools

import jax
import jax.numpy as jnp
from jax import lax
from jax.experimental import pallas as pl
from jax.experimental.pallas import tpu as pltpu
from jax.sharding import PartitionSpec as P

LANES = 128
BLANK = 1 << 20
AXES = ("leaf", "oct")


def ceil_to(n, m):
    return (n + m - 1) // m * m


def remap(entries, own, cap, shift_ref):
    slot = jnp.maximum(entries - own, 0)
    peer = slot // cap
    at = peer % LANES
    peers = shift_ref.shape[1]
    shift = jnp.zeros_like(entries)
    for k in range(peers // LANES):
        row = jnp.broadcast_to(shift_ref[:, k * LANES : (k + 1) * LANES], entries.shape)
        got = jnp.take_along_axis(row, at, axis=1, mode="promise_in_bounds")
        shift = jnp.where(peer // LANES == k, got, shift)
    column = jnp.where(entries < own, entries, entries - shift)
    return jnp.where(entries < 0, BLANK, column)


def prepare_kernel(
    fine_cap, coarse_cap, m_ref, lf_ref, lc_ref, sf_ref, sc_ref, mr_ref, idx_ref, scr
):
    surface, step_b, offsets = m_ref.shape
    fine_own, coarse_own = lf_ref.shape[0], lc_ref.shape[0]
    width = idx_ref.shape[1]

    @pl.when(pl.program_id(0) == 0)
    def _():
        scr[...] = jnp.zeros_like(scr)
        for first in range(0, offsets, LANES):
            size = min(LANES, offsets - first)
            for ref, own, cap, shift_ref, row in (
                (lf_ref, fine_own, fine_cap, sf_ref, 0),
                (lc_ref, coarse_own, coarse_cap, sc_ref, fine_own),
            ):
                entries = ref[:, first : first + size]
                if size < LANES:
                    blank = jnp.full((own, LANES - size), -1, jnp.int32)
                    entries = jnp.concatenate([entries, blank], axis=1)
                idx_ref[row : row + own, first : first + LANES] = remap(
                    entries, own, cap, shift_ref
                )

    for half in range(step_b // 8):
        for tile, first in enumerate(range(0, offsets, LANES)):
            size = min(LANES, offsets - first)
            block = m_ref[:, half * 8 : half * 8 + 8, first : first + size]
            scr[tile, :, 0:size] = block.astype(jnp.float32).reshape(surface * 8, size)
        for j in range(8):
            pair, side = half * 4 + j // 2, j % 2
            for tile in range(width // LANES):
                rows = scr[tile, pl.ds(j, surface, stride=8), :]
                at = side * width + tile * LANES
                mr_ref[pair, :, at : at + LANES] = rows.astype(jnp.bfloat16)


def prepare(m2l_ops, list_fine, list_coarse, shift_fine, shift_coarse, fine_cap, coarse_cap):
    surface, _, offsets = m2l_ops.shape
    width = ceil_to(offsets, LANES)
    targets = list_fine.shape[0] + list_coarse.shape[0]
    step_b = 16
    whole = lambda x: pl.BlockSpec(x.shape, lambda i: (0,) * x.ndim)
    return pl.pallas_call(
        functools.partial(prepare_kernel, fine_cap, coarse_cap),
        grid=(pl.cdiv(surface, step_b),),
        in_specs=[
            pl.BlockSpec((surface, step_b, offsets), lambda i: (0, i, 0)),
            whole(list_fine),
            whole(list_coarse),
            whole(shift_fine),
            whole(shift_coarse),
        ],
        out_specs=[
            pl.BlockSpec((step_b // 2, surface, 2 * width), lambda i: (i, 0, 0)),
            pl.BlockSpec((targets, width), lambda i: (0, 0)),
        ],
        out_shape=[
            jax.ShapeDtypeStruct((surface // 2, surface, 2 * width), jnp.bfloat16),
            jax.ShapeDtypeStruct((targets, width), jnp.int32),
        ],
        scratch_shapes=[pltpu.VMEM((width // LANES, surface * 8, LANES), jnp.float32)],
        compiler_params=pltpu.CompilerParams(vmem_limit_bytes=32 << 20),
        cost_estimate=pl.CostEstimate(
            flops=0, bytes_accessed=4 * surface * surface * width, transcendentals=0
        ),
        name="prepare",
    )(m2l_ops, list_fine, list_coarse, shift_fine, shift_coarse)


def gathered(idx, table_ref, pair, tiles):
    at = idx & (LANES - 1)
    value = None
    for k in range(tiles):
        row = table_ref[pair : pair + 1, k * LANES : (k + 1) * LANES]
        row = jnp.broadcast_to(row, idx.shape)
        got = jnp.take_along_axis(row, at, axis=1, mode="promise_in_bounds")
        value = got if k == 0 else jnp.where(idx >= k * LANES, got, value)
    return jnp.where(idx >= BLANK, 0, value)


def translate_kernel(fine_own, variants, pick_ref, idx_ref, tf_ref, tc_ref, m_ref, o_ref, g_ref):
    pairs, surface, width2 = m_ref.shape
    width = width2 // 2
    targets = idx_ref.shape[0]
    step = pl.program_id(0)

    @pl.when(step == 0)
    def _():
        o_ref[...] = jnp.zeros_like(o_ref)

    def work(fine_tiles, coarse_tiles):
        for q in range(pairs):
            for first in range(0, width, LANES):
                for low, high, table, tiles in (
                    (0, fine_own, tf_ref, fine_tiles),
                    (fine_own, targets, tc_ref, coarse_tiles),
                ):
                    idx = idx_ref[low:high, first : first + LANES]
                    both = gathered(idx, table, q, tiles)
                    g_ref[q, low:high, first : first + LANES] = (
                        (both << 16).astype(jnp.float32).astype(jnp.bfloat16)
                    )
                    g_ref[q, low:high, width + first : width + first + LANES] = both.astype(
                        jnp.float32
                    ).astype(jnp.bfloat16)
            o_ref[...] += lax.dot_general(
                m_ref[q],
                g_ref[q],
                (((1,), (1,)), ((), ())),
                preferred_element_type=jnp.float32,
            )

    for at, (fine_tiles, coarse_tiles) in enumerate(variants):
        pl.when(pick_ref[0] == at)(functools.partial(work, fine_tiles, coarse_tiles))


def translate(operators, idx, table_fine, table_coarse, pick, variants, fine_own):
    pairs_all, surface, width2 = operators.shape
    targets, width = idx.shape
    pairs = 4 if pairs_all % 4 == 0 else 1
    table_fine = table_fine.reshape(-1, pairs, table_fine.shape[1])
    table_coarse = table_coarse.reshape(-1, pairs, table_coarse.shape[1])
    whole = lambda x: pl.BlockSpec(x.shape, lambda i, s: (0,) * x.ndim)
    rows = lambda x: pl.BlockSpec((None,) + x.shape[1:], lambda i, s: (i, 0, 0))
    return pl.pallas_call(
        functools.partial(translate_kernel, fine_own, variants),
        grid_spec=pltpu.PrefetchScalarGridSpec(
            num_scalar_prefetch=1,
            grid=(pairs_all // pairs,),
            in_specs=[
                whole(idx),
                rows(table_fine),
                rows(table_coarse),
                pl.BlockSpec((pairs, surface, width2), lambda i, s: (i, 0, 0)),
            ],
            out_specs=pl.BlockSpec((surface, targets), lambda i, s: (0, 0)),
            scratch_shapes=[pltpu.VMEM((pairs, targets, width2), jnp.bfloat16)],
        ),
        out_shape=jax.ShapeDtypeStruct((surface, targets), jnp.float32),
        compiler_params=pltpu.CompilerParams(vmem_limit_bytes=32 << 20),
        cost_estimate=pl.CostEstimate(
            flops=2 * pairs_all * surface * targets * width2,
            bytes_accessed=2 * pairs_all * surface * width2,
            transcendentals=0,
        ),
        name="translate",
    )(pick, idx, table_fine, table_coarse, operators)


def offsets_of(asks):
    peers, cap = asks.shape
    counts = jnp.sum((asks >= 0).astype(jnp.int32), axis=1)
    order = jnp.arange(peers, dtype=jnp.int32)
    before = jnp.sum(jnp.where(order[None, :] < order[:, None], counts[None, :], 0), axis=1)
    shift = order * cap - before
    place = before[:, None] + jnp.arange(cap, dtype=jnp.int32)[None, :]
    place = jnp.where(asks >= 0, place, -1).reshape(-1)
    padded = jnp.pad(shift, (0, ceil_to(peers, LANES) - peers))[None, :]
    return padded, place, jnp.sum(counts)


def select_columns(arrived, place, count):
    hot = (place[:, None] == jnp.arange(count, dtype=jnp.int32)[None, :]).astype(jnp.bfloat16)
    return lax.dot_general(
        arrived, hot, (((0,), (0,)), ((), ())), preferred_element_type=jnp.float32
    )


def pack(table):
    surface, count = table.shape
    table = jnp.pad(table, ((0, 0), (0, ceil_to(count, LANES) - count)))
    peak = jnp.maximum(jnp.max(jnp.abs(table)), 1e-30)
    level = jnp.floor(jnp.log2(peak))
    fixed = jnp.round(table * jnp.exp2(13.0 - level)).astype(jnp.int32)
    fixed = fixed.reshape(surface // 2, 2, -1)
    return fixed[:, 1] * 65536 + fixed[:, 0], jnp.exp2(level - 29.0)


def exchange(x):
    return lax.all_to_all(x, AXES, split_axis=0, concat_axis=0, tiled=True)


def body(
    dens_fine, parent, child_code, m2m_ops, m2l_ops, ask_fine, list_fine, ask_coarse, list_coarse
):
    surface, fine_own = dens_fine.shape
    coarse_own = list_coarse.shape[0]
    asks_fine, asks_coarse = ask_fine[0], ask_coarse[0]
    peers, fine_cap = asks_fine.shape
    coarse_cap = asks_coarse.shape[1]
    wanted = exchange(
        jnp.concatenate(
            [asks_fine, jnp.where(asks_coarse < 0, -1, asks_coarse + fine_own)], axis=1
        )
    )

    shift_fine, place_fine, used_fine = offsets_of(asks_fine)
    shift_coarse, place_coarse, used_coarse = offsets_of(asks_coarse)
    operators, idx = prepare(
        m2l_ops, list_fine, list_coarse, shift_fine, shift_coarse, fine_cap, coarse_cap
    )

    positions = jnp.arange(8, dtype=jnp.int32)
    spread = jnp.where(
        (child_code[None, :] == positions[:, None])[:, None, :],
        dens_fine[None],
        jnp.zeros((), jnp.bfloat16),
    )
    child_terms = jnp.dot(
        m2m_ops.reshape(surface, 8 * surface),
        spread.reshape(8 * surface, fine_own),
        preferred_element_type=jnp.float32,
    )
    local_parent = parent - lax.axis_index(AXES) * coarse_own
    members = (local_parent[:, None] == jnp.arange(coarse_own, dtype=jnp.int32)[None, :]).astype(
        jnp.float32
    )
    dens_coarse = jnp.dot(child_terms, members, precision=lax.Precision.HIGHEST).astype(
        jnp.bfloat16
    )

    own = jnp.concatenate([dens_fine, dens_coarse], axis=1)
    picked = (
        wanted.reshape(-1)[:, None] == jnp.arange(fine_own + coarse_own, dtype=jnp.int32)[None, :]
    ).astype(jnp.bfloat16)
    outgoing = lax.dot_general(
        picked, own, (((1,), (1,)), ((), ())), preferred_element_type=jnp.float32
    ).astype(jnp.bfloat16)
    arrived = exchange(outgoing.reshape(peers, fine_cap + coarse_cap, surface))

    remote_fine = (peers - 1) * fine_cap
    remote_coarse = (peers - 1) * coarse_cap
    came_fine = select_columns(
        arrived[:, :fine_cap].reshape(-1, surface), place_fine, remote_fine
    )
    came_coarse = select_columns(
        arrived[:, fine_cap:].reshape(-1, surface), place_coarse, remote_coarse
    )
    table_fine, unit_fine = pack(
        jnp.concatenate([dens_fine.astype(jnp.float32), came_fine], axis=1)
    )
    table_coarse, unit_coarse = pack(
        jnp.concatenate([dens_coarse.astype(jnp.float32), came_coarse], axis=1)
    )
    all_fine = table_fine.shape[1] // LANES
    all_coarse = table_coarse.shape[1] // LANES
    need_fine = (fine_own + used_fine + LANES - 1) // LANES
    need_coarse = (coarse_own + used_coarse + LANES - 1) // LANES
    variants = [(min(3, all_fine), min(2, all_coarse)), (min(4, all_fine), min(2, all_coarse))]
    variants = variants + [(all_fine, all_coarse)]
    pick = jnp.int32(len(variants) - 1)
    for at in reversed(range(len(variants) - 1)):
        fits = (need_fine <= variants[at][0]) & (need_coarse <= variants[at][1])
        pick = jnp.where(fits, at, pick)
    both = translate(
        operators, idx, table_fine, table_coarse, pick.reshape(1), variants, fine_own
    )
    return both[:, :fine_own] * unit_fine, both[:, fine_own:] * (0.5 * unit_coarse)


def solution(mesh):
    return jax.shard_map(
        body,
        mesh=mesh,
        in_specs=(
            P(None, AXES),
            P(AXES),
            P(AXES),
            P(),
            P(),
            P(AXES, None, None),
            P(AXES, None),
            P(AXES, None, None),
            P(AXES, None),
        ),
        out_specs=(P(None, AXES), P(None, AXES)),
        check_vma=False,
    )
```

```python
import functools

import jax
import jax.numpy as jnp
from jax import lax
from jax.experimental import pallas as pl
from jax.experimental.pallas import tpu as pltpu
from jax.sharding import PartitionSpec as P

LANES = 128
CHUNK = 16
BLANK = 1 << 20
AXES = ("leaf", "oct")


def ceil_to(n, m):
    return (n + m - 1) // m * m


def remap(entries, own, cap, shift_ref):
    slot = jnp.maximum(entries - own, 0)
    peer = slot // cap
    at = peer % LANES
    peers = shift_ref.shape[1]
    shift = jnp.zeros_like(entries)
    for k in range(peers // LANES):
        row = jnp.broadcast_to(shift_ref[:, k * LANES : (k + 1) * LANES], entries.shape)
        got = jnp.take_along_axis(row, at, axis=1, mode="promise_in_bounds")
        shift = jnp.where(peer // LANES == k, got, shift)
    column = jnp.where(entries < own, entries, entries - shift)
    return jnp.where(entries < 0, BLANK, column)


def prepare_kernel(
    fine_cap, coarse_cap, m_ref, lf_ref, lc_ref, sf_ref, sc_ref, mr_ref, idx_ref, scr
):
    surface, step_b, offsets = m_ref.shape
    fine_own, coarse_own = lf_ref.shape[0], lc_ref.shape[0]
    width = idx_ref.shape[1]

    @pl.when(pl.program_id(0) == 0)
    def _():
        scr[...] = jnp.zeros_like(scr)
        for first in range(0, offsets, LANES):
            size = min(LANES, offsets - first)
            for ref, own, cap, shift_ref, row in (
                (lf_ref, fine_own, fine_cap, sf_ref, 0),
                (lc_ref, coarse_own, coarse_cap, sc_ref, fine_own),
            ):
                entries = ref[:, first : first + size]
                if size < LANES:
                    blank = jnp.full((own, LANES - size), -1, jnp.int32)
                    entries = jnp.concatenate([entries, blank], axis=1)
                idx_ref[row : row + own, first : first + LANES] = remap(
                    entries, own, cap, shift_ref
                )

    for half in range(step_b // 8):
        for tile, first in enumerate(range(0, offsets, LANES)):
            size = min(LANES, offsets - first)
            block = m_ref[:, half * 8 : half * 8 + 8, first : first + size]
            scr[tile, :, 0:size] = block.astype(jnp.float32).reshape(surface * 8, size)
        for j in range(8):
            for tile in range(width // LANES):
                rows = scr[tile, pl.ds(j, surface, stride=8), :]
                at = j * width + tile * LANES
                mr_ref[half, :, at : at + LANES] = rows.astype(jnp.bfloat16)


def prepare(m2l_ops, list_fine, list_coarse, shift_fine, shift_coarse, fine_cap, coarse_cap):
    surface, _, offsets = m2l_ops.shape
    width = ceil_to(offsets, LANES)
    targets = list_fine.shape[0] + list_coarse.shape[0]
    step_b = 16
    whole = lambda x: pl.BlockSpec(x.shape, lambda i: (0,) * x.ndim)
    return pl.pallas_call(
        functools.partial(prepare_kernel, fine_cap, coarse_cap),
        grid=(pl.cdiv(surface, step_b),),
        in_specs=[
            pl.BlockSpec((surface, step_b, offsets), lambda i: (0, i, 0)),
            whole(list_fine),
            whole(list_coarse),
            whole(shift_fine),
            whole(shift_coarse),
        ],
        out_specs=[
            pl.BlockSpec((step_b // 8, surface, 8 * width), lambda i: (i, 0, 0)),
            pl.BlockSpec((targets, width), lambda i: (0, 0)),
        ],
        out_shape=[
            jax.ShapeDtypeStruct((surface // 8, surface, 8 * width), jnp.bfloat16),
            jax.ShapeDtypeStruct((targets, width), jnp.int32),
        ],
        scratch_shapes=[pltpu.VMEM((width // LANES, surface * 8, LANES), jnp.float32)],
        compiler_params=pltpu.CompilerParams(vmem_limit_bytes=56 << 20),
        cost_estimate=pl.CostEstimate(
            flops=0, bytes_accessed=4 * surface * surface * width, transcendentals=0
        ),
        name="prepare",
    )(m2l_ops, list_fine, list_coarse, shift_fine, shift_coarse)


def translate_kernel(fine_own, variants, pick_ref, idx_ref, tf_ref, tc_ref, m_ref, o_ref, g_ref):
    targets, width = idx_ref.shape
    pairs = m_ref.shape[1] // (2 * width)
    step = pl.program_id(0)

    @pl.when(step == 0)
    def _():
        o_ref[...] = jnp.zeros_like(o_ref)

    def work(fine_tiles, coarse_tiles):
        for first in range(0, width, LANES):
            for low in range(0, targets, CHUNK):
                table, tiles = (tf_ref, fine_tiles) if low < fine_own else (tc_ref, coarse_tiles)
                idx = idx_ref[low : low + CHUNK, first : first + LANES]
                at = idx & (LANES - 1)
                later = [idx >= k * LANES for k in range(1, tiles)]
                blank = idx >= BLANK
                for q in range(pairs):
                    value = None
                    for k in range(tiles):
                        row = table[q : q + 1, k * LANES : (k + 1) * LANES]
                        row = jnp.broadcast_to(row, idx.shape)
                        got = jnp.take_along_axis(row, at, axis=1, mode="promise_in_bounds")
                        value = got if k == 0 else jnp.where(later[k - 1], got, value)
                    value = jnp.where(blank, 0, value)
                    to = 2 * q * width + first
                    g_ref[low : low + CHUNK, to : to + LANES] = (
                        (value << 16).astype(jnp.float32).astype(jnp.bfloat16)
                    )
                    to = to + width
                    g_ref[low : low + CHUNK, to : to + LANES] = value.astype(jnp.float32).astype(
                        jnp.bfloat16
                    )
        o_ref[...] += lax.dot_general(
            m_ref[...],
            g_ref[...],
            (((1,), (1,)), ((), ())),
            preferred_element_type=jnp.float32,
        )

    for at, (fine_tiles, coarse_tiles) in enumerate(variants):
        pl.when(pick_ref[0] == at)(functools.partial(work, fine_tiles, coarse_tiles))


def translate(operators, idx, table_fine, table_coarse, pick, variants, fine_own):
    blocks, surface, depth = operators.shape
    targets, width = idx.shape
    pairs = depth // (2 * width)
    table_fine = table_fine.reshape(blocks, pairs, table_fine.shape[1])
    table_coarse = table_coarse.reshape(blocks, pairs, table_coarse.shape[1])
    whole = lambda x: pl.BlockSpec(x.shape, lambda i, s: (0,) * x.ndim)
    rows = lambda x: pl.BlockSpec((None,) + x.shape[1:], lambda i, s: (i, 0, 0))
    return pl.pallas_call(
        functools.partial(translate_kernel, fine_own, variants),
        grid_spec=pltpu.PrefetchScalarGridSpec(
            num_scalar_prefetch=1,
            grid=(blocks,),
            in_specs=[whole(idx), rows(table_fine), rows(table_coarse), rows(operators)],
            out_specs=pl.BlockSpec((surface, targets), lambda i, s: (0, 0)),
            scratch_shapes=[pltpu.VMEM((targets, depth), jnp.bfloat16)],
        ),
        out_shape=jax.ShapeDtypeStruct((surface, targets), jnp.float32),
        compiler_params=pltpu.CompilerParams(vmem_limit_bytes=56 << 20),
        cost_estimate=pl.CostEstimate(
            flops=2 * blocks * surface * targets * depth,
            bytes_accessed=2 * blocks * surface * depth,
            transcendentals=0,
        ),
        name="translate",
    )(pick, idx, table_fine, table_coarse, operators)


def offsets_of(asks):
    peers, cap = asks.shape
    counts = jnp.sum((asks >= 0).astype(jnp.int32), axis=1)
    order = jnp.arange(peers, dtype=jnp.int32)
    before = jnp.sum(jnp.where(order[None, :] < order[:, None], counts[None, :], 0), axis=1)
    shift = order * cap - before
    place = before[:, None] + jnp.arange(cap, dtype=jnp.int32)[None, :]
    place = jnp.where(asks >= 0, place, -1).reshape(-1)
    padded = jnp.pad(shift, (0, ceil_to(peers, LANES) - peers))[None, :]
    return padded, place, jnp.sum(counts)


def select_columns(arrived, place, count):
    hot = (place[:, None] == jnp.arange(count, dtype=jnp.int32)[None, :]).astype(jnp.bfloat16)
    return lax.dot_general(
        arrived, hot, (((0,), (0,)), ((), ())), preferred_element_type=jnp.float32
    )


def pack(table):
    surface, count = table.shape
    table = jnp.pad(table, ((0, 0), (0, ceil_to(count, LANES) - count)))
    peak = jnp.maximum(jnp.max(jnp.abs(table)), 1e-30)
    level = jnp.floor(jnp.log2(peak))
    fixed = jnp.round(table * jnp.exp2(13.0 - level)).astype(jnp.int32)
    fixed = fixed.reshape(surface // 2, 2, -1)
    return fixed[:, 1] * 65536 + fixed[:, 0], jnp.exp2(level - 29.0)


def exchange(x):
    return lax.all_to_all(x, AXES, split_axis=0, concat_axis=0, tiled=True)


def body(
    dens_fine, parent, child_code, m2m_ops, m2l_ops, ask_fine, list_fine, ask_coarse, list_coarse
):
    surface, fine_own = dens_fine.shape
    coarse_own = list_coarse.shape[0]
    asks_fine, asks_coarse = ask_fine[0], ask_coarse[0]
    peers, fine_cap = asks_fine.shape
    coarse_cap = asks_coarse.shape[1]
    wanted = exchange(
        jnp.concatenate(
            [asks_fine, jnp.where(asks_coarse < 0, -1, asks_coarse + fine_own)], axis=1
        )
    )

    shift_fine, place_fine, used_fine = offsets_of(asks_fine)
    shift_coarse, place_coarse, used_coarse = offsets_of(asks_coarse)
    operators, idx = prepare(
        m2l_ops, list_fine, list_coarse, shift_fine, shift_coarse, fine_cap, coarse_cap
    )

    positions = jnp.arange(8, dtype=jnp.int32)
    spread = jnp.where(
        (child_code[None, :] == positions[:, None])[:, None, :],
        dens_fine[None],
        jnp.zeros((), jnp.bfloat16),
    )
    child_terms = jnp.dot(
        m2m_ops.reshape(surface, 8 * surface),
        spread.reshape(8 * surface, fine_own),
        preferred_element_type=jnp.float32,
    )
    local_parent = parent - lax.axis_index(AXES) * coarse_own
    members = (local_parent[:, None] == jnp.arange(coarse_own, dtype=jnp.int32)[None, :]).astype(
        jnp.float32
    )
    dens_coarse = jnp.dot(child_terms, members, precision=lax.Precision.HIGHEST).astype(
        jnp.bfloat16
    )

    own = jnp.concatenate([dens_fine, dens_coarse], axis=1)
    picked = (
        wanted.reshape(-1)[:, None] == jnp.arange(fine_own + coarse_own, dtype=jnp.int32)[None, :]
    ).astype(jnp.bfloat16)
    outgoing = lax.dot_general(
        picked, own, (((1,), (1,)), ((), ())), preferred_element_type=jnp.float32
    ).astype(jnp.bfloat16)
    arrived = exchange(outgoing.reshape(peers, fine_cap + coarse_cap, surface))

    remote_fine = (peers - 1) * fine_cap
    remote_coarse = (peers - 1) * coarse_cap
    came_fine = select_columns(
        arrived[:, :fine_cap].reshape(-1, surface), place_fine, remote_fine
    )
    came_coarse = select_columns(
        arrived[:, fine_cap:].reshape(-1, surface), place_coarse, remote_coarse
    )
    table_fine, unit_fine = pack(
        jnp.concatenate([dens_fine.astype(jnp.float32), came_fine], axis=1)
    )
    table_coarse, unit_coarse = pack(
        jnp.concatenate([dens_coarse.astype(jnp.float32), came_coarse], axis=1)
    )
    all_fine = table_fine.shape[1] // LANES
    all_coarse = table_coarse.shape[1] // LANES
    need_fine = (fine_own + used_fine + LANES - 1) // LANES
    need_coarse = (coarse_own + used_coarse + LANES - 1) // LANES
    variants = [(min(3, all_fine), min(2, all_coarse)), (min(4, all_fine), min(2, all_coarse))]
    variants = variants + [(all_fine, all_coarse)]
    pick = jnp.int32(len(variants) - 1)
    for at in reversed(range(len(variants) - 1)):
        fits = (need_fine <= variants[at][0]) & (need_coarse <= variants[at][1])
        pick = jnp.where(fits, at, pick)
    both = translate(
        operators, idx, table_fine, table_coarse, pick.reshape(1), variants, fine_own
    )
    return both[:, :fine_own] * unit_fine, both[:, fine_own:] * (0.5 * unit_coarse)


def solution(mesh):
    return jax.shard_map(
        body,
        mesh=mesh,
        in_specs=(
            P(None, AXES),
            P(AXES),
            P(AXES),
            P(),
            P(),
            P(AXES, None, None),
            P(AXES, None),
            P(AXES, None, None),
            P(AXES, None),
        ),
        out_specs=(P(None, AXES), P(None, AXES)),
        check_vma=False,
    )
```

```python
import functools

import jax
import jax.numpy as jnp
from jax import lax
from jax.experimental import pallas as pl
from jax.experimental.pallas import tpu as pltpu
from jax.sharding import PartitionSpec as P

LANES = 128
CHUNK = 16
BLANK = 1 << 20
AXES = ("leaf", "oct")


def ceil_to(n, m):
    return (n + m - 1) // m * m


def remap(entries, own, cap, shift_ref):
    slot = jnp.maximum(entries - own, 0)
    peer = slot // cap
    at = peer % LANES
    peers = shift_ref.shape[1]
    shift = jnp.zeros_like(entries)
    for k in range(peers // LANES):
        row = jnp.broadcast_to(shift_ref[:, k * LANES : (k + 1) * LANES], entries.shape)
        got = jnp.take_along_axis(row, at, axis=1, mode="promise_in_bounds")
        shift = jnp.where(peer // LANES == k, got, shift)
    column = jnp.where(entries < own, entries, entries - shift)
    return jnp.where(entries < 0, BLANK, column)


def prepare_kernel(
    fine_cap, coarse_cap, m_ref, lf_ref, lc_ref, sf_ref, sc_ref, mr_ref, idx_ref, scr
):
    surface, step_b, offsets = m_ref.shape
    fine_own, coarse_own = lf_ref.shape[0], lc_ref.shape[0]
    width = idx_ref.shape[1]

    @pl.when(pl.program_id(0) == 0)
    def _():
        scr[...] = jnp.zeros_like(scr)
        for first in range(0, offsets, LANES):
            size = min(LANES, offsets - first)
            for ref, own, cap, shift_ref, row in (
                (lf_ref, fine_own, fine_cap, sf_ref, 0),
                (lc_ref, coarse_own, coarse_cap, sc_ref, fine_own),
            ):
                entries = ref[:, first : first + size]
                if size < LANES:
                    blank = jnp.full((own, LANES - size), -1, jnp.int32)
                    entries = jnp.concatenate([entries, blank], axis=1)
                idx_ref[row : row + own, first : first + LANES] = remap(
                    entries, own, cap, shift_ref
                )

    for half in range(step_b // 8):
        for tile, first in enumerate(range(0, offsets, LANES)):
            size = min(LANES, offsets - first)
            block = m_ref[:, half * 8 : half * 8 + 8, first : first + size]
            scr[tile, :, 0:size] = block.astype(jnp.float32).reshape(surface * 8, size)
        for j in range(8):
            for tile in range(width // LANES):
                rows = scr[tile, pl.ds(j, surface, stride=8), :]
                at = j * width + tile * LANES
                mr_ref[half, :, at : at + LANES] = rows.astype(jnp.bfloat16)


def prepare(m2l_ops, list_fine, list_coarse, shift_fine, shift_coarse, fine_cap, coarse_cap):
    surface, _, offsets = m2l_ops.shape
    width = ceil_to(offsets, LANES)
    targets = list_fine.shape[0] + list_coarse.shape[0]
    step_b = 16
    whole = lambda x: pl.BlockSpec(x.shape, lambda i: (0,) * x.ndim)
    return pl.pallas_call(
        functools.partial(prepare_kernel, fine_cap, coarse_cap),
        grid=(pl.cdiv(surface, step_b),),
        in_specs=[
            pl.BlockSpec((surface, step_b, offsets), lambda i: (0, i, 0)),
            whole(list_fine),
            whole(list_coarse),
            whole(shift_fine),
            whole(shift_coarse),
        ],
        out_specs=[
            pl.BlockSpec((step_b // 8, surface, 8 * width), lambda i: (i, 0, 0)),
            pl.BlockSpec((targets, width), lambda i: (0, 0)),
        ],
        out_shape=[
            jax.ShapeDtypeStruct((surface // 8, surface, 8 * width), jnp.bfloat16),
            jax.ShapeDtypeStruct((targets, width), jnp.int32),
        ],
        scratch_shapes=[pltpu.VMEM((width // LANES, surface * 8, LANES), jnp.float32)],
        compiler_params=pltpu.CompilerParams(vmem_limit_bytes=56 << 20),
        cost_estimate=pl.CostEstimate(
            flops=0, bytes_accessed=4 * surface * surface * width, transcendentals=0
        ),
        name="prepare",
    )(m2l_ops, list_fine, list_coarse, shift_fine, shift_coarse)


def translate_kernel(fine_own, variants, pick_ref, idx_ref, tf_ref, tc_ref, m_ref, o_ref, g_ref):
    targets, width = idx_ref.shape
    pairs = m_ref.shape[1] // (2 * width)
    step = pl.program_id(0)

    @pl.when(step == 0)
    def _():
        o_ref[...] = jnp.zeros_like(o_ref)

    def work(fine_tiles, coarse_tiles):
        for first in range(0, width, LANES):
            for low in range(0, targets, CHUNK):
                table, tiles = (tf_ref, fine_tiles) if low < fine_own else (tc_ref, coarse_tiles)
                idx = idx_ref[low : low + CHUNK, first : first + LANES]
                at = idx & (LANES - 1)
                later = [idx >= k * LANES for k in range(1, tiles)]
                blank = idx >= BLANK
                for q in range(pairs):
                    value = None
                    for k in range(tiles):
                        row = table[q : q + 1, k * LANES : (k + 1) * LANES]
                        row = jnp.broadcast_to(row, idx.shape)
                        got = jnp.take_along_axis(row, at, axis=1, mode="promise_in_bounds")
                        value = got if k == 0 else jnp.where(later[k - 1], got, value)
                    value = jnp.where(blank, 0, value)
                    to = 2 * q * width + first
                    g_ref[low : low + CHUNK, to : to + LANES] = (
                        (value << 16).astype(jnp.float32).astype(jnp.bfloat16)
                    )
                    to = to + width
                    g_ref[low : low + CHUNK, to : to + LANES] = value.astype(jnp.float32).astype(
                        jnp.bfloat16
                    )
        o_ref[...] += lax.dot_general(
            m_ref[...],
            g_ref[...],
            (((1,), (1,)), ((), ())),
            preferred_element_type=jnp.float32,
        )

    for at, (fine_tiles, coarse_tiles) in enumerate(variants):
        pl.when(pick_ref[0] == at)(functools.partial(work, fine_tiles, coarse_tiles))


def translate(operators, idx, table_fine, table_coarse, pick, variants, fine_own):
    blocks, surface, depth = operators.shape
    targets, width = idx.shape
    pairs = depth // (2 * width)
    table_fine = table_fine.reshape(blocks, pairs, table_fine.shape[1])
    table_coarse = table_coarse.reshape(blocks, pairs, table_coarse.shape[1])
    whole = lambda x: pl.BlockSpec(x.shape, lambda i, s: (0,) * x.ndim)
    rows = lambda x: pl.BlockSpec((None,) + x.shape[1:], lambda i, s: (i, 0, 0))
    return pl.pallas_call(
        functools.partial(translate_kernel, fine_own, variants),
        grid_spec=pltpu.PrefetchScalarGridSpec(
            num_scalar_prefetch=1,
            grid=(blocks,),
            in_specs=[whole(idx), rows(table_fine), rows(table_coarse), rows(operators)],
            out_specs=pl.BlockSpec((surface, targets), lambda i, s: (0, 0)),
            scratch_shapes=[pltpu.VMEM((targets, depth), jnp.bfloat16)],
        ),
        out_shape=jax.ShapeDtypeStruct((surface, targets), jnp.float32),
        compiler_params=pltpu.CompilerParams(vmem_limit_bytes=56 << 20),
        cost_estimate=pl.CostEstimate(
            flops=2 * blocks * surface * targets * depth,
            bytes_accessed=2 * blocks * surface * depth,
            transcendentals=0,
        ),
        name="translate",
    )(pick, idx, table_fine, table_coarse, operators)


def offsets_of(asks):
    peers, cap = asks.shape
    counts = jnp.sum((asks >= 0).astype(jnp.int32), axis=1)
    order = jnp.arange(peers, dtype=jnp.int32)
    before = jnp.sum(jnp.where(order[None, :] < order[:, None], counts[None, :], 0), axis=1)
    shift = order * cap - before
    place = before[:, None] + jnp.arange(cap, dtype=jnp.int32)[None, :]
    place = jnp.where(asks >= 0, place, -1).reshape(-1)
    padded = jnp.pad(shift, (0, ceil_to(peers, LANES) - peers))[None, :]
    return padded, place, jnp.sum(counts)


def sources_of(asks, place, own, count):
    peers = asks.shape[0]
    octant = (asks + own * jnp.arange(peers, dtype=jnp.int32)[:, None]).reshape(-1)
    columns = jnp.arange(count, dtype=jnp.int32)
    hit = place[None, :] == columns[:, None]
    return jnp.sum(jnp.where(hit, octant[None, :] + 1, 0), axis=1) - 1


def select_columns(rows, sources):
    octants = jnp.arange(rows.shape[0], dtype=jnp.int32)
    hot = (octants[:, None] == sources[None, :]).astype(jnp.bfloat16)
    return lax.dot_general(rows, hot, (((0,), (0,)), ((), ())), preferred_element_type=jnp.float32)


def pack(table):
    surface, count = table.shape
    table = jnp.pad(table, ((0, 0), (0, ceil_to(count, LANES) - count)))
    peak = jnp.maximum(jnp.max(jnp.abs(table)), 1e-30)
    level = jnp.floor(jnp.log2(peak))
    fixed = jnp.round(table * jnp.exp2(13.0 - level)).astype(jnp.int32)
    fixed = fixed.reshape(surface // 2, 2, -1)
    return fixed[:, 1] * 65536 + fixed[:, 0], jnp.exp2(level - 29.0)


def body(
    dens_fine, parent, child_code, m2m_ops, m2l_ops, ask_fine, list_fine, ask_coarse, list_coarse
):
    surface, fine_own = dens_fine.shape
    coarse_own = list_coarse.shape[0]
    asks_fine, asks_coarse = ask_fine[0], ask_coarse[0]
    peers, fine_cap = asks_fine.shape
    coarse_cap = asks_coarse.shape[1]
    all_fine_rows = lax.all_gather(dens_fine.T, AXES, axis=0, tiled=True)

    shift_fine, place_fine, used_fine = offsets_of(asks_fine)
    shift_coarse, place_coarse, used_coarse = offsets_of(asks_coarse)
    operators, idx = prepare(
        m2l_ops, list_fine, list_coarse, shift_fine, shift_coarse, fine_cap, coarse_cap
    )

    positions = jnp.arange(8, dtype=jnp.int32)
    spread = jnp.where(
        (child_code[None, :] == positions[:, None])[:, None, :],
        dens_fine[None],
        jnp.zeros((), jnp.bfloat16),
    )
    child_terms = jnp.dot(
        m2m_ops.reshape(surface, 8 * surface),
        spread.reshape(8 * surface, fine_own),
        preferred_element_type=jnp.float32,
    )
    local_parent = parent - lax.axis_index(AXES) * coarse_own
    members = (local_parent[:, None] == jnp.arange(coarse_own, dtype=jnp.int32)[None, :]).astype(
        jnp.float32
    )
    dens_coarse = jnp.dot(child_terms, members, precision=lax.Precision.HIGHEST).astype(
        jnp.bfloat16
    )

    all_coarse_rows = lax.all_gather(dens_coarse.T, AXES, axis=0, tiled=True)

    remote_fine = (peers - 1) * fine_cap
    remote_coarse = (peers - 1) * coarse_cap
    from_fine = sources_of(asks_fine, place_fine, fine_own, remote_fine)
    from_coarse = sources_of(asks_coarse, place_coarse, coarse_own, remote_coarse)
    came_fine = select_columns(all_fine_rows, from_fine)
    came_coarse = select_columns(all_coarse_rows, from_coarse)
    table_fine, unit_fine = pack(
        jnp.concatenate([dens_fine.astype(jnp.float32), came_fine], axis=1)
    )
    table_coarse, unit_coarse = pack(
        jnp.concatenate([dens_coarse.astype(jnp.float32), came_coarse], axis=1)
    )
    all_fine = table_fine.shape[1] // LANES
    all_coarse = table_coarse.shape[1] // LANES
    need_fine = (fine_own + used_fine + LANES - 1) // LANES
    need_coarse = (coarse_own + used_coarse + LANES - 1) // LANES
    variants = [(min(3, all_fine), min(2, all_coarse)), (min(4, all_fine), min(2, all_coarse))]
    variants = variants + [(all_fine, all_coarse)]
    pick = jnp.int32(len(variants) - 1)
    for at in reversed(range(len(variants) - 1)):
        fits = (need_fine <= variants[at][0]) & (need_coarse <= variants[at][1])
        pick = jnp.where(fits, at, pick)
    both = translate(
        operators, idx, table_fine, table_coarse, pick.reshape(1), variants, fine_own
    )
    return both[:, :fine_own] * unit_fine, both[:, fine_own:] * (0.5 * unit_coarse)


def solution(mesh):
    return jax.shard_map(
        body,
        mesh=mesh,
        in_specs=(
            P(None, AXES),
            P(AXES),
            P(AXES),
            P(),
            P(),
            P(AXES, None, None),
            P(AXES, None),
            P(AXES, None, None),
            P(AXES, None),
        ),
        out_specs=(P(None, AXES), P(None, AXES)),
        check_vma=False,
    )
```

```python
import functools

import jax
import jax.numpy as jnp
from jax import lax
from jax.experimental import pallas as pl
from jax.experimental.pallas import tpu as pltpu
from jax.sharding import PartitionSpec as P

LANES = 128
CHUNK = 16
HALF = LANES // 2
BLANK = 1 << 20
AXES = ("leaf", "oct")
STAGE_A, STAGE_B = 23, 3
VMEM_BYTES = 56 << 20


def ceil_to(n, m):
    return (n + m - 1) // m * m


def lane_iota(shape):
    return lax.broadcasted_iota(jnp.int32, shape, 1)


def whole(x):
    return pl.BlockSpec(x.shape, lambda *i: (0,) * x.ndim)


def shape_of(shape, dtype):
    return jax.ShapeDtypeStruct(shape, dtype)


def asks_kernel(fine_own, f_ref, c_ref, o_ref, scr):
    fine_cap, peers = f_ref.shape
    coarse_cap = c_ref.shape[0]
    scr[...] = jnp.zeros_like(scr)
    scr[0:fine_cap, 0:peers] = f_ref[...]
    coarse = c_ref[...]
    scr[fine_cap : fine_cap + coarse_cap, 0:peers] = jnp.where(coarse < 0, -1, coarse + fine_own)
    o_ref[...] = scr[...].T[0:peers, 0 : fine_cap + coarse_cap]


def join_asks(asks_fine, asks_coarse, fine_own):
    peers = asks_fine.shape[1]
    slots = asks_fine.shape[0] + asks_coarse.shape[0]
    return pl.pallas_call(
        functools.partial(asks_kernel, fine_own),
        out_shape=shape_of((peers, slots), jnp.int32),
        scratch_shapes=[pltpu.VMEM((LANES, LANES), jnp.int32)],
        name="join_asks",
    )(asks_fine, asks_coarse)


def answer_kernel(w_ref, f_ref, c_ref, o_ref, scr, hot):
    peers, slots = w_ref.shape
    own = f_ref.shape[0] + c_ref.shape[0]
    scr[0:peers, 0:slots] = w_ref[...]
    columns = scr[...].T[0:slots, :]
    octant = lane_iota((slots, own))
    for e in range(0, peers, 2):
        picked = [
            jnp.broadcast_to(columns[:, d : d + 1], (slots, own)) == octant for d in (e, e + 1)
        ]
        both = jnp.concatenate([p.astype(jnp.float32) for p in picked], axis=0)
        hot[e * slots : (e + 2) * slots, :] = both.astype(jnp.bfloat16)
    rows = jnp.concatenate([f_ref[...], c_ref[...]], axis=0)
    o_ref[...] = jnp.dot(hot[...], rows, preferred_element_type=jnp.float32).astype(jnp.bfloat16)


def answer(wanted, fine_rows, coarse_rows):
    peers, slots = wanted.shape
    own = fine_rows.shape[0] + coarse_rows.shape[0]
    return pl.pallas_call(
        answer_kernel,
        out_shape=shape_of((peers * slots, fine_rows.shape[1]), jnp.bfloat16),
        scratch_shapes=[
            pltpu.VMEM((LANES, LANES), jnp.int32),
            pltpu.VMEM((peers * slots, own), jnp.bfloat16),
        ],
        name="answer",
    )(wanted, fine_rows, coarse_rows)


def remap(entries, own, cap, shift):
    slot = jnp.maximum(entries - own, 0)
    peer = slot // cap
    moved = jnp.take_along_axis(
        jnp.broadcast_to(shift, entries.shape), peer, axis=1, mode="promise_in_bounds"
    )
    column = jnp.where(entries < own, entries, entries - moved)
    return jnp.where(entries < 0, BLANK, column)


def plan_kernel(
    variants, coarse_at, af_ref, ac_ref, lf_ref, lc_ref, idx_ref, tail_ref, to_ref, pick_ref, cnt
):
    offsets = lf_ref.shape[1]
    body_lanes = idx_ref.shape[1]
    peers = af_ref.shape[1]
    lanes = lane_iota((LANES, LANES))
    earlier = lax.broadcasted_iota(jnp.int32, (LANES, LANES), 0) < lanes
    earlier = earlier.astype(jnp.float32).astype(jnp.bfloat16)
    levels = []
    row = tail_row = 0
    cnt[...] = jnp.zeros_like(cnt)
    for level, (ask_ref, list_ref) in enumerate(((af_ref, lf_ref), (ac_ref, lc_ref))):
        own, cap = list_ref.shape[0], ask_ref.shape[0]
        valid = (ask_ref[...] >= 0).astype(jnp.float32)
        cnt[level, 0:1, 0:peers] = jnp.sum(valid, axis=0, keepdims=True)
        counts = cnt[level]
        before = jnp.dot(
            counts.astype(jnp.bfloat16), earlier, preferred_element_type=jnp.float32
        ).astype(jnp.int32)[0:1]
        total = jnp.sum(counts).astype(jnp.int32)
        counts = counts.astype(jnp.int32)[0:1]
        shift = lane_iota((1, LANES)) * cap - before
        levels.append((own, cap, counts, before, total))
        for first in range(0, body_lanes, LANES):
            idx_ref[row : row + own, first : first + LANES] = remap(
                list_ref[:, first : first + LANES], own, cap, shift
            )
        rest = jnp.concatenate(
            [
                list_ref[:, body_lanes:offsets],
                jnp.full((own, LANES - (offsets - body_lanes)), -1, jnp.int32),
            ],
            axis=1,
        )
        rest = remap(rest, own, cap, shift)
        upper = ceil_to(own // CHUNK, 2) // 2 * CHUNK
        moved = pltpu.roll(rest[upper:], HALF, axis=1)
        if own - upper < upper:
            missing = jnp.full((2 * upper - own, LANES), BLANK, jnp.int32)
            moved = jnp.concatenate([moved, missing], axis=0)
        tail_ref[tail_row : tail_row + upper, :] = jnp.where(
            lane_iota((upper, LANES)) < HALF, rest[0:upper], moved
        )
        row += own
        tail_row += upper

    (fine_own, fine_cap, *fine), (coarse_own, coarse_cap, *coarse) = levels
    slots = fine_cap + coarse_cap
    to_ref[0:fine_own, :] = lax.broadcasted_iota(jnp.int32, (fine_own, LANES), 0)
    to_ref[fine_own:row, :] = (
        lax.broadcasted_iota(jnp.int32, (coarse_own, LANES), 0) + coarse_at
    )
    place = lax.broadcasted_iota(jnp.int32, (slots, LANES), 0)
    for e in range(peers):
        one = lambda x: jnp.broadcast_to(x[:, e : e + 1], (slots, LANES))
        at = place - fine_cap
        to_fine = jnp.where(place < one(fine[0]), fine_own + one(fine[1]) + place, -1)
        to_coarse = jnp.where(
            at < one(coarse[0]), coarse_at + coarse_own + one(coarse[1]) + at, -1
        )
        to_ref[row + e * slots : row + (e + 1) * slots, :] = jnp.where(
            place < fine_cap, to_fine, to_coarse
        )

    pick = jnp.int32(len(variants) - 1)
    for at in reversed(range(len(variants) - 1)):
        fits = (fine_own + fine[2] <= variants[at][0] * LANES) & (
            coarse_own + coarse[2] <= variants[at][1] * LANES
        )
        pick = jnp.where(fits, at, pick)
    pick_ref[0] = pick


def plan(asks_fine, asks_coarse, list_fine, list_coarse, variants, coarse_at):
    own = list_fine.shape[0] + list_coarse.shape[0]
    tails = sum(ceil_to(x.shape[0] // CHUNK, 2) // 2 * CHUNK for x in (list_fine, list_coarse))
    body_lanes = list_fine.shape[1] // LANES * LANES
    slots, peers = asks_fine.shape[0] + asks_coarse.shape[0], asks_fine.shape[1]
    vmem = pl.BlockSpec(memory_space=pltpu.VMEM)
    return pl.pallas_call(
        functools.partial(plan_kernel, variants, coarse_at),
        out_specs=[vmem, vmem, vmem, pl.BlockSpec(memory_space=pltpu.SMEM)],
        out_shape=[
            shape_of((own, body_lanes), jnp.int32),
            shape_of((tails, LANES), jnp.int32),
            shape_of((own + peers * slots, LANES), jnp.int32),
            shape_of((1,), jnp.int32),
        ],
        scratch_shapes=[pltpu.VMEM((2, 8, LANES), jnp.float32)],
        compiler_params=pltpu.CompilerParams(vmem_limit_bytes=VMEM_BYTES),
        name="plan",
    )(asks_fine, asks_coarse, list_fine, list_coarse)


def build_tables(ranges, to_ref, sources, rows_t, table_f, table, unit):
    rows = jnp.concatenate([ref[...] for ref in sources], axis=0)
    rows_t[...] = rows.astype(jnp.float32).T.astype(jnp.bfloat16)
    to = to_ref[...]
    tiles = table_f.shape[0]
    lanes = lane_iota(to.shape)
    for k in range(0, tiles, 2):
        size = min(2, tiles - k)
        hot = [(to == lanes + (k + h) * LANES).astype(jnp.float32) for h in range(size)]
        hot = jnp.concatenate([x.astype(jnp.bfloat16) for x in hot], axis=1)
        columns = jnp.dot(rows_t[...], hot, preferred_element_type=jnp.float32)
        for h in range(size):
            table_f[k + h] = columns[:, h * LANES : (h + 1) * LANES]
    for level, (low, high) in enumerate(ranges):
        values = table_f[low:high]
        peak = jnp.max(jnp.max(jnp.abs(values), axis=0), axis=0, keepdims=True)
        peak = jnp.maximum(jnp.max(peak, axis=1, keepdims=True), 1e-30)
        power = jnp.floor(jnp.log2(jnp.broadcast_to(peak, (8, LANES))))
        unit[level] = jnp.exp2(power - 29.0)
        factor = jnp.exp2(13.0 - power)[0:1]
        for k in range(low, high):
            table_f[k] = jnp.round(table_f[k] * factor)
    pairs = table_f.shape[1] // 2
    for k in range(tiles):
        even = table_f[k, pl.ds(0, pairs, stride=2), :].astype(jnp.int32)
        odd = table_f[k, pl.ds(1, pairs, stride=2), :].astype(jnp.int32)
        both = odd * 65536 + even
        for block in range(pairs // 4):
            table[block, 0:4, k * LANES : (k + 1) * LANES] = both[4 * block : 4 * block + 4]


def stage_block(m_ref, stage):
    surface, _, offsets = m_ref.shape
    for tile, first in enumerate(range(0, offsets, LANES)):
        size = min(LANES, offsets - first)
        for a in range(surface):
            part = m_ref[a, :, first : first + size].astype(jnp.float32)
            if size < LANES:
                gap = jnp.zeros((8, HALF - size), jnp.float32)
                part = jnp.concatenate([part, gap, part, gap], axis=1)
            stage[tile, pl.ds(STAGE_A * a, 8, stride=STAGE_B), :] = part


def lay_half(half, stage, mr_ref):
    surface = mr_ref.shape[0]
    tiles = stage.shape[0]
    for j in range(4):
        for tile in range(tiles):
            rows = stage[tile, pl.ds(STAGE_B * (4 * half + j), surface, stride=STAGE_A), :]
            at = (j * tiles + tile) * LANES
            mr_ref[:, at : at + LANES] = rows.astype(jnp.bfloat16)


def gather_half(half, step, levels, idx_ref, tail_ref, table, g_ref):
    body_lanes = idx_ref.shape[1]
    width = body_lanes + LANES
    lower = lane_iota((CHUNK, LANES)) < HALF

    def put(rows, q, at, value):
        to = 2 * q * width + at
        low = (value << 16).astype(jnp.float32).astype(jnp.bfloat16)
        high = value.astype(jnp.float32).astype(jnp.bfloat16)
        g_ref[rows : rows + CHUNK, to : to + LANES] = low
        g_ref[rows : rows + CHUNK, to + width : to + width + LANES] = high

    for low, high, base, tiles, tail_row in levels:
        rows = [
            [
                jnp.broadcast_to(
                    table[step, pair : pair + 1, (base + k) * LANES : (base + k + 1) * LANES],
                    (CHUNK, LANES),
                )
                for k in range(tiles)
            ]
            for pair in (2 * half, 2 * half + 1)
        ]

        def gathered(idx):
            at = idx & (LANES - 1)
            later = [idx >= k * LANES for k in range(1, tiles)]
            blank = idx >= BLANK
            for q in range(2):
                value = None
                for k in range(tiles):
                    got = jnp.take_along_axis(rows[q][k], at, axis=1, mode="promise_in_bounds")
                    value = got if k == 0 else jnp.where(later[k - 1], got, value)
                yield q, jnp.where(blank, 0, value)

        for first in range(0, body_lanes, LANES):
            for target in range(low, high, CHUNK):
                idx = idx_ref[target : target + CHUNK, first : first + LANES]
                for q, value in gathered(idx):
                    put(target, q, first, value)
        upper = ceil_to((high - low) // CHUNK, 2) // 2 * CHUNK
        for target in range(low, low + upper, CHUNK):
            at = tail_row + target - low
            for q, value in gathered(tail_ref[at : at + CHUNK, :]):
                put(target, q, body_lanes, jnp.where(lower, value, 0))
                if target + upper < high:
                    put(target + upper, q, body_lanes, jnp.where(lower, 0, value))


def translate_kernel(
    variants,
    coarse_tile,
    pick_ref,
    idx_ref,
    tail_ref,
    to_ref,
    f_ref,
    c_ref,
    arrived_ref,
    m_ref,
    of_ref,
    oc_ref,
    rows_t,
    table_f,
    table,
    unit,
    stage,
    acc,
    mr_a,
    mr_b,
    g_a,
    g_b,
):
    fine_own, targets = of_ref.shape[0], idx_ref.shape[0]
    tail_coarse = ceil_to(fine_own // CHUNK, 2) // 2 * CHUNK
    step = pl.program_id(0)

    @pl.when(step == 0)
    def _():
        build_tables(
            ((0, coarse_tile), (coarse_tile, table_f.shape[0])),
            to_ref,
            (f_ref, c_ref, arrived_ref),
            rows_t,
            table_f,
            table,
            unit,
        )
        acc[...] = jnp.zeros_like(acc)
        mr_b[...] = jnp.zeros_like(mr_b)
        g_b[...] = jnp.zeros_like(g_b)

    def product(g_ref, mr_ref):
        acc[...] += lax.dot_general(
            g_ref[...],
            mr_ref[...],
            (((1,), (1,)), ((), ())),
            preferred_element_type=jnp.float32,
        )

    def work(fine_tiles, coarse_tiles):
        levels = (
            (0, fine_own, 0, fine_tiles, 0),
            (fine_own, targets, coarse_tile, coarse_tiles, tail_coarse),
        )
        stage_block(m_ref, stage)
        lay_half(0, stage, mr_a)
        product(g_b, mr_b)
        gather_half(0, step, levels, idx_ref, tail_ref, table, g_a)
        lay_half(1, stage, mr_b)
        product(g_a, mr_a)
        gather_half(1, step, levels, idx_ref, tail_ref, table, g_b)

    for at, tiles in enumerate(variants):
        pl.when(pick_ref[0] == at)(functools.partial(work, *tiles))

    @pl.when(step == pl.num_programs(0) - 1)
    def _():
        product(g_b, mr_b)
        of_ref[...] = acc[0:fine_own, :] * unit[0, 0:1, 0:1]
        oc_ref[...] = acc[fine_own:targets, :] * (0.5 * unit[1, 0:1, 0:1])


def translate(
    pick, idx, tail, to, fine_rows, coarse_rows, arrived, m2l_ops, variants, coarse_tile, tiles
):
    surface, _, offsets = m2l_ops.shape
    width = ceil_to(offsets, LANES)
    targets = idx.shape[0]
    fine_own, coarse_own = fine_rows.shape[0], coarse_rows.shape[0]
    blocks = surface // 8
    return pl.pallas_call(
        functools.partial(translate_kernel, variants, coarse_tile),
        grid=(blocks,),
        in_specs=[
            pl.BlockSpec(memory_space=pltpu.SMEM),
            whole(idx),
            whole(tail),
            whole(to),
            whole(fine_rows),
            whole(coarse_rows),
            whole(arrived),
            pl.BlockSpec((surface, 8, offsets), lambda i: (0, i, 0)),
        ],
        out_specs=[
            pl.BlockSpec((fine_own, surface), lambda i: (0, 0)),
            pl.BlockSpec((coarse_own, surface), lambda i: (0, 0)),
        ],
        out_shape=[
            shape_of((fine_own, surface), jnp.float32),
            shape_of((coarse_own, surface), jnp.float32),
        ],
        scratch_shapes=[
            pltpu.VMEM((surface, to.shape[0]), jnp.bfloat16),
            pltpu.VMEM((tiles, surface, LANES), jnp.float32),
            pltpu.VMEM((blocks, 8, tiles * LANES), jnp.int32),
            pltpu.VMEM((2, 8, LANES), jnp.float32),
            pltpu.VMEM((width // LANES, ceil_to(STAGE_A * surface, 8), LANES), jnp.float32),
            pltpu.VMEM((targets, surface), jnp.float32),
            pltpu.VMEM((surface, 4 * width), jnp.bfloat16),
            pltpu.VMEM((surface, 4 * width), jnp.bfloat16),
            pltpu.VMEM((targets, 4 * width), jnp.bfloat16),
            pltpu.VMEM((targets, 4 * width), jnp.bfloat16),
        ],
        compiler_params=pltpu.CompilerParams(vmem_limit_bytes=VMEM_BYTES),
        cost_estimate=pl.CostEstimate(
            flops=2 * surface * surface * targets * width,
            bytes_accessed=2 * surface * surface * width,
            transcendentals=0,
        ),
        name="translate",
    )(pick, idx, tail, to, fine_rows, coarse_rows, arrived, m2l_ops)


def exchange(x):
    return lax.all_to_all(x, AXES, split_axis=0, concat_axis=0, tiled=True)


def body(
    dens_fine, parent, child_code, m2m_ops, m2l_ops, ask_fine, list_fine, ask_coarse, list_coarse
):
    surface, fine_own = dens_fine.shape
    coarse_own = list_coarse.shape[0]
    asks_fine, asks_coarse = ask_fine[0].T, ask_coarse[0].T
    fine_cap, peers = asks_fine.shape
    coarse_cap = asks_coarse.shape[0]
    wanted = exchange(join_asks(asks_fine, asks_coarse, fine_own))

    fine_tiles = ceil_to(fine_own + (peers - 1) * fine_cap, LANES) // LANES
    coarse_tiles = ceil_to(coarse_own + (peers - 1) * coarse_cap, LANES) // LANES
    variants = [(min(3, fine_tiles), min(2, coarse_tiles)), (min(4, fine_tiles), min(2, coarse_tiles))]
    variants = variants + [(fine_tiles, coarse_tiles)]
    idx, tail, to, pick = plan(
        asks_fine, asks_coarse, list_fine, list_coarse, variants, fine_tiles * LANES
    )

    positions = jnp.arange(8, dtype=jnp.int32)
    spread = jnp.where(
        (child_code[None, :] == positions[:, None])[:, None, :],
        dens_fine[None],
        jnp.zeros((), jnp.bfloat16),
    )
    child_terms = jnp.dot(
        m2m_ops.reshape(surface, 8 * surface),
        spread.reshape(8 * surface, fine_own),
        preferred_element_type=jnp.float32,
    )
    local_parent = parent - lax.axis_index(AXES) * coarse_own
    members = (local_parent[:, None] == jnp.arange(coarse_own, dtype=jnp.int32)[None, :]).astype(
        jnp.float32
    )
    dens_coarse = jnp.dot(child_terms, members, precision=lax.Precision.HIGHEST).astype(
        jnp.bfloat16
    )

    fine_rows, coarse_rows = dens_fine.T, dens_coarse.T
    outgoing = answer(wanted, fine_rows, coarse_rows)
    arrived = exchange(outgoing.reshape(peers, fine_cap + coarse_cap, surface))
    pot_fine, pot_coarse = translate(
        pick,
        idx,
        tail,
        to,
        fine_rows,
        coarse_rows,
        arrived.reshape(-1, surface),
        m2l_ops,
        variants,
        fine_tiles,
        fine_tiles + coarse_tiles,
    )
    return pot_fine.T, pot_coarse.T


def solution(mesh):
    return jax.shard_map(
        body,
        mesh=mesh,
        in_specs=(
            P(None, AXES),
            P(AXES),
            P(AXES),
            P(),
            P(),
            P(AXES, None, None),
            P(AXES, None),
            P(AXES, None, None),
            P(AXES, None),
        ),
        out_specs=(P(None, AXES), P(None, AXES)),
        check_vma=False,
    )
```

```python
import functools

import jax
import jax.numpy as jnp
from jax import lax
from jax.experimental import pallas as pl
from jax.experimental.pallas import tpu as pltpu
from jax.sharding import PartitionSpec as P

LANES = 128
CHUNK = 16
HALF = LANES // 2
BLANK = 1 << 20
LOCAL = LANES
AXES = ("leaf", "oct")
STAGE_A, STAGE_B = 23, 3
VMEM_BYTES = 56 << 20


def ceil_to(n, m):
    return (n + m - 1) // m * m


def lane_iota(shape):
    return lax.broadcasted_iota(jnp.int32, shape, 1)


def whole(x):
    return pl.BlockSpec(x.shape, lambda *i: (0,) * x.ndim)


def shape_of(shape, dtype):
    return jax.ShapeDtypeStruct(shape, dtype)


def asks_kernel(fine_own, f_ref, c_ref, o_ref, scr):
    fine_cap, peers = f_ref.shape
    coarse_cap = c_ref.shape[0]
    scr[...] = jnp.zeros_like(scr)
    scr[0:fine_cap, 0:peers] = f_ref[...]
    coarse = c_ref[...]
    scr[fine_cap : fine_cap + coarse_cap, 0:peers] = jnp.where(coarse < 0, -1, coarse + fine_own)
    o_ref[...] = scr[...].T[0:peers, 0 : fine_cap + coarse_cap]


def join_asks(asks_fine, asks_coarse, fine_own):
    peers = asks_fine.shape[1]
    slots = asks_fine.shape[0] + asks_coarse.shape[0]
    return pl.pallas_call(
        functools.partial(asks_kernel, fine_own),
        out_shape=shape_of((peers, slots), jnp.int32),
        scratch_shapes=[pltpu.VMEM((LANES, LANES), jnp.int32)],
        name="join_asks",
    )(asks_fine, asks_coarse)


def answer_kernel(w_ref, f_ref, c_any, o_ref, scr, hot, c_ref, sem):
    peers, slots = w_ref.shape
    own, surface = f_ref.shape[0] + c_ref.shape[0], f_ref.shape[1]
    fetch = pltpu.make_async_copy(c_any, c_ref, sem)
    fetch.start()
    scr[0:peers, 0:slots] = w_ref[...]
    columns = scr[...].T[0:slots, :]
    octant = lane_iota((slots, own))
    for e in range(0, peers, 2):
        picked = [
            jnp.broadcast_to(columns[:, d : d + 1], (slots, own)) == octant for d in (e, e + 1)
        ]
        both = jnp.concatenate([p.astype(jnp.float32) for p in picked], axis=0)
        hot[e * slots : (e + 2) * slots, :] = both.astype(jnp.bfloat16)
    fetch.wait()
    rows = jnp.concatenate([f_ref[...], c_ref[...]], axis=0)
    found = jnp.dot(hot[...], rows, preferred_element_type=jnp.float32)
    extra = surface - LANES
    rest = jnp.concatenate(
        [found[:, LANES:], jnp.zeros((peers * slots, LANES - extra), jnp.float32)], axis=1
    ).reshape(peers, slots, LANES)
    line = rest[:, 0:8].reshape(peers * 8, LANES)
    for g in range(1, slots // 8):
        part = rest[:, 8 * g : 8 * g + 8].reshape(peers * 8, LANES)
        line = line + pltpu.roll(part, g * extra, axis=1)
    o_ref[...] = jnp.concatenate(
        [found[:, 0:LANES].reshape(peers, slots, LANES), line.reshape(peers, 8, LANES)], axis=1
    ).astype(jnp.bfloat16)


def answer(wanted, fine_rows, coarse_rows):
    peers, slots = wanted.shape
    own = fine_rows.shape[0] + coarse_rows.shape[0]
    return pl.pallas_call(
        answer_kernel,
        in_specs=[whole(wanted), whole(fine_rows), pl.BlockSpec(memory_space=pl.ANY)],
        out_shape=shape_of((peers, slots + 8, LANES), jnp.bfloat16),
        scratch_shapes=[
            pltpu.VMEM((LANES, LANES), jnp.int32),
            pltpu.VMEM((peers * slots, own), jnp.bfloat16),
            pltpu.VMEM(coarse_rows.shape, jnp.bfloat16),
            pltpu.SemaphoreType.DMA,
        ],
        name="answer",
    )(wanted, fine_rows, coarse_rows)


def remap(entries, own, done, cap, shift):
    slot = jnp.maximum(entries - own, 0)
    peer = slot // cap
    moved = jnp.take_along_axis(
        jnp.broadcast_to(shift, entries.shape), peer, axis=1, mode="promise_in_bounds"
    )
    column = jnp.where(entries < own, entries, entries - moved) - done
    return jnp.where(entries < done, BLANK, column)


def plan_kernel(
    variants,
    coarse_at,
    af_ref,
    ac_ref,
    lf_ref,
    lc_ref,
    idx_ref,
    tail_ref,
    to_ref,
    pick_ref,
    own_idx_ref,
    own_tail_ref,
    cnt,
):
    offsets = lf_ref.shape[1]
    body_lanes = idx_ref.shape[1]
    peers = af_ref.shape[1]
    lanes = lane_iota((LANES, LANES))
    earlier = lax.broadcasted_iota(jnp.int32, (LANES, LANES), 0) < lanes
    earlier = earlier.astype(jnp.float32).astype(jnp.bfloat16)
    levels = []
    row = tail_row = 0
    cnt[...] = jnp.zeros_like(cnt)
    for level, (ask_ref, list_ref) in enumerate(((af_ref, lf_ref), (ac_ref, lc_ref))):
        own, cap = list_ref.shape[0], ask_ref.shape[0]
        done = LOCAL if level == 0 else 0
        valid = (ask_ref[...] >= 0).astype(jnp.float32)
        cnt[level, 0:1, 0:peers] = jnp.sum(valid, axis=0, keepdims=True)
        counts = cnt[level]
        before = jnp.dot(
            counts.astype(jnp.bfloat16), earlier, preferred_element_type=jnp.float32
        ).astype(jnp.int32)[0:1]
        total = jnp.sum(counts).astype(jnp.int32)
        counts = counts.astype(jnp.int32)[0:1]
        shift = lane_iota((1, LANES)) * cap - before
        levels.append((own, cap, counts, before, total))
        lists = [list_ref[:, first : first + LANES] for first in range(0, body_lanes, LANES)]
        lists.append(
            jnp.concatenate(
                [
                    list_ref[:, body_lanes:offsets],
                    jnp.full((own, LANES - (offsets - body_lanes)), -1, jnp.int32),
                ],
                axis=1,
            )
        )
        upper = tail_rows(own)

        def keep(columns, to_body, to_tail, at, tail_at):
            for k, x in enumerate(columns[:-1]):
                to_body[at : at + own, k * LANES : (k + 1) * LANES] = x
            rest = columns[-1]
            moved = pltpu.roll(rest[upper:], HALF, axis=1)
            if own - upper < upper:
                missing = jnp.full((2 * upper - own, LANES), BLANK, jnp.int32)
                moved = jnp.concatenate([moved, missing], axis=0)
            to_tail[tail_at : tail_at + upper, :] = jnp.where(
                lane_iota((upper, LANES)) < HALF, rest[0:upper], moved
            )

        keep([remap(x, own, done, cap, shift) for x in lists], idx_ref, tail_ref, row, tail_row)
        if level == 0:
            near = [jnp.where((x < 0) | (x >= LOCAL), BLANK, x) for x in lists]
            keep(near, own_idx_ref, own_tail_ref, 0, 0)
        row += own
        tail_row += upper

    (fine_own, fine_cap, *fine), (coarse_own, coarse_cap, *coarse) = levels
    place = lax.broadcasted_iota(jnp.int32, (8, LANES), 0)
    at = 0
    for level, base in (((fine_cap, *fine), fine_own - LOCAL), ((coarse_cap, *coarse), coarse_at + coarse_own)):
        cap, counts, before, _ = level
        for first in range(0, cap, 8):
            for e in range(peers):
                count = jnp.broadcast_to(counts[:, e : e + 1], (8, LANES))
                start = jnp.broadcast_to(before[:, e : e + 1], (8, LANES)) + base
                k = place + first
                to_ref[at : at + 8, :] = jnp.where(k < count, start + k, -1)
                at += 8
    octant = lax.broadcasted_iota(jnp.int32, (fine_own, LANES), 0)
    to_ref[at : at + fine_own, :] = jnp.maximum(octant - LOCAL, -1)
    octant = lax.broadcasted_iota(jnp.int32, (coarse_own, LANES), 0)
    to_ref[at + fine_own : at + row, :] = octant + coarse_at

    pick = jnp.int32(len(variants) - 1)
    for at in reversed(range(len(variants) - 1)):
        fits = (fine_own - LOCAL + fine[2] <= variants[at][0] * LANES) & (
            coarse_own + coarse[2] <= variants[at][1] * LANES
        )
        pick = jnp.where(fits, at, pick)
    pick_ref[0] = pick


def plan(asks_fine, asks_coarse, list_fine, list_coarse, variants, coarse_at):
    own = list_fine.shape[0] + list_coarse.shape[0]
    tails = sum(tail_rows(x.shape[0]) for x in (list_fine, list_coarse))
    body_lanes = list_fine.shape[1] // LANES * LANES
    slots, peers = asks_fine.shape[0] + asks_coarse.shape[0], asks_fine.shape[1]
    vmem = pl.BlockSpec(memory_space=pltpu.VMEM)
    return pl.pallas_call(
        functools.partial(plan_kernel, variants, coarse_at),
        out_specs=[vmem, vmem, vmem, pl.BlockSpec(memory_space=pltpu.SMEM), vmem, vmem],
        out_shape=[
            shape_of((own, body_lanes), jnp.int32),
            shape_of((tails, LANES), jnp.int32),
            shape_of((own + peers * slots, LANES), jnp.int32),
            shape_of((1,), jnp.int32),
            shape_of((list_fine.shape[0], body_lanes), jnp.int32),
            shape_of((tail_rows(list_fine.shape[0]), LANES), jnp.int32),
        ],
        scratch_shapes=[pltpu.VMEM((2, 8, LANES), jnp.float32)],
        compiler_params=pltpu.CompilerParams(vmem_limit_bytes=VMEM_BYTES),
        name="plan",
    )(asks_fine, asks_coarse, list_fine, list_coarse)


def pack_rows(values, table, tile):
    pairs = values.shape[0] // 2
    even = values[pl.ds(0, pairs, stride=2), :].astype(jnp.int32)
    odd = values[pl.ds(1, pairs, stride=2), :].astype(jnp.int32)
    both = odd * 65536 + even
    for block in range(pairs // 4):
        table[block, 0:4, tile * LANES : (tile + 1) * LANES] = both[4 * block : 4 * block + 4]


def scale_of(values):
    peak = jnp.max(jnp.max(jnp.abs(values), axis=0, keepdims=True), axis=1, keepdims=True)
    power = jnp.floor(jnp.log2(jnp.broadcast_to(jnp.maximum(peak, 1e-30), (8, LANES))))
    return jnp.exp2(13.0 - power)[0:1], jnp.exp2(power - 29.0)


def build_tables(ranges, to_ref, f_ref, c_ref, arrived, rows_t, table_f, table, unit):
    peers, lines, _ = arrived.shape
    surface = rows_t.shape[0]
    extra = surface - LANES
    came = arrived[...].astype(jnp.float32)
    rest = came[:, lines - 8 :].reshape(peers * 8, LANES).T
    at = 0
    for g in range(lines // 8 - 1):
        part = came[:, 8 * g : 8 * g + 8].reshape(peers * 8, LANES).T
        part = jnp.concatenate([part, rest[g * extra : (g + 1) * extra]], axis=0)
        rows_t[:, at : at + peers * 8] = part.astype(jnp.bfloat16)
        at += peers * 8
    own = jnp.concatenate([f_ref[...], c_ref[...]], axis=0).astype(jnp.float32)
    rows_t[:, at : at + own.shape[0]] = own.T.astype(jnp.bfloat16)
    to = to_ref[...]
    tiles = table_f.shape[0]
    lanes = lane_iota(to.shape)
    for k in range(0, tiles, 2):
        size = min(2, tiles - k)
        hot = [(to == lanes + (k + h) * LANES).astype(jnp.float32) for h in range(size)]
        hot = jnp.concatenate([x.astype(jnp.bfloat16) for x in hot], axis=1)
        columns = jnp.dot(rows_t[...], hot, preferred_element_type=jnp.float32)
        for h in range(size):
            table_f[k + h] = columns[:, h * LANES : (h + 1) * LANES]
    for level, (low, high) in enumerate(ranges):
        factor, unit[level] = scale_of(jnp.max(jnp.abs(table_f[low:high]), axis=0))
        for k in range(low, high):
            table_f[k] = jnp.round(table_f[k] * factor)
            pack_rows(table_f.at[k], table, k)


def stage_block(m_ref, stage):
    surface, _, offsets = m_ref.shape
    for tile, first in enumerate(range(0, offsets, LANES)):
        size = min(LANES, offsets - first)
        for a in range(surface):
            part = m_ref[a, :, first : first + size].astype(jnp.float32)
            if size < LANES:
                gap = jnp.zeros((8, HALF - size), jnp.float32)
                part = jnp.concatenate([part, gap, part, gap], axis=1)
            stage[tile, pl.ds(STAGE_A * a, 8, stride=STAGE_B), :] = part


def lay_half(half, stage, *mr_refs):
    surface = mr_refs[0].shape[0]
    tiles = stage.shape[0]
    for j in range(4):
        for tile in range(tiles):
            rows = stage[tile, pl.ds(STAGE_B * (4 * half + j), surface, stride=STAGE_A), :]
            at = (j * tiles + tile) * LANES
            for mr_ref in mr_refs:
                mr_ref[:, at : at + LANES] = rows.astype(jnp.bfloat16)


def gather_half(half, step, levels, idx_ref, tail_ref, table, g_ref):
    body_lanes = idx_ref.shape[1]
    width = body_lanes + LANES
    lower = lane_iota((CHUNK, LANES)) < HALF

    def put(rows, q, at, value):
        to = 2 * q * width + at
        low = (value << 16).astype(jnp.float32).astype(jnp.bfloat16)
        high = value.astype(jnp.float32).astype(jnp.bfloat16)
        g_ref[rows : rows + CHUNK, to : to + LANES] = low
        g_ref[rows : rows + CHUNK, to + width : to + width + LANES] = high

    for low, high, base, tiles, tail_row in levels:
        rows = [
            [
                jnp.broadcast_to(
                    table[step, pair : pair + 1, (base + k) * LANES : (base + k + 1) * LANES],
                    (CHUNK, LANES),
                )
                for k in range(tiles)
            ]
            for pair in (2 * half, 2 * half + 1)
        ]

        def gathered(idx):
            at = idx & (LANES - 1)
            later = [idx >= k * LANES for k in range(1, tiles)]
            blank = idx >= BLANK
            for q in range(2):
                value = None
                for k in range(tiles):
                    got = jnp.take_along_axis(rows[q][k], at, axis=1, mode="promise_in_bounds")
                    value = got if k == 0 else jnp.where(later[k - 1], got, value)
                yield q, jnp.where(blank, 0, value)

        for first in range(0, body_lanes, LANES):
            for target in range(low, high, CHUNK):
                idx = idx_ref[target : target + CHUNK, first : first + LANES]
                for q, value in gathered(idx):
                    put(target, q, first, value)
        upper = tail_rows(high - low)
        for target in range(low, low + upper, CHUNK):
            at = tail_row + target - low
            for q, value in gathered(tail_ref[at : at + CHUNK, :]):
                put(target, q, body_lanes, jnp.where(lower, value, 0))
                if target + upper < high:
                    put(target + upper, q, body_lanes, jnp.where(lower, 0, value))


def multiply(acc, g_ref, mr):
    acc[...] += lax.dot_general(
        g_ref[...], mr, (((1,), (1,)), ((), ())), preferred_element_type=jnp.float32
    )


def tail_rows(own):
    return ceil_to(own // CHUNK, 2) // 2 * CHUNK


def local_kernel(
    f_ref, idx_ref, tail_ref, m_ref, _, mr_ref, o_ref, table_f, table, unit, stage, acc, mr_b, g_a, g_b
):
    own = f_ref.shape[0]
    half = mr_ref.shape[1] // 2
    step = pl.program_id(0)

    @pl.when(step == 0)
    def _():
        table_f[...] = f_ref[0:LOCAL, :].astype(jnp.float32).T
        factor, unit[...] = scale_of(table_f[...])
        table_f[...] = jnp.round(table_f[...] * factor)
        pack_rows(table_f, table, 0)
        acc[...] = jnp.zeros_like(acc)
        mr_b[...] = jnp.zeros_like(mr_b)
        g_b[...] = jnp.zeros_like(g_b)

    levels = ((0, own, 0, 1, 0),)
    stage_block(m_ref, stage)
    lay_half(0, stage, mr_ref.at[:, 0:half])
    multiply(acc, g_b, mr_b[...])
    gather_half(0, step, levels, idx_ref, tail_ref, table, g_a)
    lay_half(1, stage, mr_ref.at[:, half : 2 * half], mr_b)
    multiply(acc, g_a, mr_ref[:, 0:half])
    gather_half(1, step, levels, idx_ref, tail_ref, table, g_b)

    @pl.when(step == pl.num_programs(0) - 1)
    def _():
        multiply(acc, g_b, mr_b[...])
        o_ref[...] = acc[...] * unit[0:1, 0:1]


def local_part(fine_rows, idx, tail, m2l_ops, after):
    surface, _, offsets = m2l_ops.shape
    width = ceil_to(offsets, LANES)
    own = fine_rows.shape[0]
    blocks = surface // 8
    return pl.pallas_call(
        local_kernel,
        grid=(blocks,),
        in_specs=[
            whole(fine_rows),
            whole(idx),
            whole(tail),
            pl.BlockSpec((surface, 8, offsets), lambda i: (0, i, 0)),
            pl.BlockSpec(memory_space=pl.ANY),
        ],
        out_specs=[
            pl.BlockSpec((None, surface, 8 * width), lambda i: (i, 0, 0)),
            pl.BlockSpec((own, surface), lambda i: (0, 0)),
        ],
        out_shape=[
            shape_of((blocks, surface, 8 * width), jnp.bfloat16),
            shape_of((own, surface), jnp.float32),
        ],
        scratch_shapes=[
            pltpu.VMEM((surface, LANES), jnp.float32),
            pltpu.VMEM((blocks, 8, LANES), jnp.int32),
            pltpu.VMEM((8, LANES), jnp.float32),
            pltpu.VMEM((width // LANES, ceil_to(STAGE_A * surface, 8), LANES), jnp.float32),
            pltpu.VMEM((own, surface), jnp.float32),
            pltpu.VMEM((surface, 4 * width), jnp.bfloat16),
            pltpu.VMEM((own, 4 * width), jnp.bfloat16),
            pltpu.VMEM((own, 4 * width), jnp.bfloat16),
        ],
        compiler_params=pltpu.CompilerParams(vmem_limit_bytes=VMEM_BYTES),
        cost_estimate=pl.CostEstimate(
            flops=2 * surface * surface * own * width,
            bytes_accessed=4 * surface * surface * width,
            transcendentals=0,
        ),
        name="local_part",
    )(fine_rows, idx, tail, m2l_ops, after)


def translate_kernel(
    variants,
    coarse_tile,
    pick_ref,
    idx_ref,
    tail_ref,
    to_ref,
    f_ref,
    c_ref,
    arrived_any,
    part_ref,
    ma_ref,
    mb_ref,
    of_ref,
    oc_ref,
    rows_t,
    table_f,
    table,
    unit,
    arrived,
    acc,
    g_a,
    g_b,
    sem,
):
    fine_own, targets = of_ref.shape[0], idx_ref.shape[0]
    step = pl.program_id(0)
    last = pl.num_programs(0) - 1

    @pl.when(step == 0)
    def _():
        fetch = pltpu.make_async_copy(arrived_any, arrived, sem)
        fetch.start()
        acc[...] = jnp.zeros_like(acc)
        g_b[...] = jnp.zeros_like(g_b)
        fetch.wait()
        build_tables(
            ((0, coarse_tile), (coarse_tile, table_f.shape[0])),
            to_ref,
            f_ref,
            c_ref,
            arrived,
            rows_t,
            table_f,
            table,
            unit,
        )

    def work(fine_tiles, coarse_tiles):
        levels = (
            (0, fine_own, 0, fine_tiles, 0),
            (fine_own, targets, coarse_tile, coarse_tiles, tail_rows(fine_own)),
        )
        multiply(acc, g_b, mb_ref[...])
        gather_half(0, step, levels, idx_ref, tail_ref, table, g_a)
        multiply(acc, g_a, ma_ref[...])
        gather_half(1, step, levels, idx_ref, tail_ref, table, g_b)

    for at, tiles in enumerate(variants):
        pl.when((pick_ref[0] == at) & (step < last))(functools.partial(work, *tiles))

    @pl.when(step == last)
    def _():
        multiply(acc, g_b, mb_ref[...])
        of_ref[...] = acc[0:fine_own, :] * unit[0, 0:1, 0:1] + part_ref[...]
        oc_ref[...] = acc[fine_own:targets, :] * (0.5 * unit[1, 0:1, 0:1])


def translate(
    pick, idx, tail, to, fine_rows, coarse_rows, arrived, part, operators, variants, coarse_tile, tiles
):
    blocks, surface, depth = operators.shape
    targets = idx.shape[0]
    fine_own, coarse_own = fine_rows.shape[0], coarse_rows.shape[0]
    return pl.pallas_call(
        functools.partial(translate_kernel, variants, coarse_tile),
        grid=(blocks + 1,),
        in_specs=[
            pl.BlockSpec(memory_space=pltpu.SMEM),
            whole(idx),
            whole(tail),
            whole(to),
            whole(fine_rows),
            whole(coarse_rows),
            pl.BlockSpec(memory_space=pl.ANY),
            whole(part),
            pl.BlockSpec((None, surface, depth // 2), lambda i: (jnp.minimum(i, blocks - 1), 0, 0)),
            pl.BlockSpec((None, surface, depth // 2), lambda i: (jnp.maximum(i - 1, 0), 0, 1)),
        ],
        out_specs=[
            pl.BlockSpec((fine_own, surface), lambda i: (0, 0)),
            pl.BlockSpec((coarse_own, surface), lambda i: (0, 0)),
        ],
        out_shape=[
            shape_of((fine_own, surface), jnp.float32),
            shape_of((coarse_own, surface), jnp.float32),
        ],
        scratch_shapes=[
            pltpu.VMEM((surface, to.shape[0]), jnp.bfloat16),
            pltpu.VMEM((tiles, surface, LANES), jnp.float32),
            pltpu.VMEM((blocks, 8, tiles * LANES), jnp.int32),
            pltpu.VMEM((2, 8, LANES), jnp.float32),
            pltpu.VMEM(arrived.shape, jnp.bfloat16),
            pltpu.VMEM((targets, surface), jnp.float32),
            pltpu.VMEM((targets, depth // 2), jnp.bfloat16),
            pltpu.VMEM((targets, depth // 2), jnp.bfloat16),
            pltpu.SemaphoreType.DMA,
        ],
        compiler_params=pltpu.CompilerParams(vmem_limit_bytes=VMEM_BYTES),
        cost_estimate=pl.CostEstimate(
            flops=blocks * surface * targets * depth * 2,
            bytes_accessed=2 * blocks * surface * depth,
            transcendentals=0,
        ),
        name="translate",
    )(pick, idx, tail, to, fine_rows, coarse_rows, arrived, part, operators, operators)


def exchange(x):
    return lax.all_to_all(x, AXES, split_axis=0, concat_axis=0, tiled=True)


def body(
    dens_fine, parent, child_code, m2m_ops, m2l_ops, ask_fine, list_fine, ask_coarse, list_coarse
):
    surface, fine_own = dens_fine.shape
    coarse_own = list_coarse.shape[0]
    asks_fine, asks_coarse = ask_fine[0].T, ask_coarse[0].T
    fine_cap, peers = asks_fine.shape
    coarse_cap = asks_coarse.shape[0]
    wanted = exchange(join_asks(asks_fine, asks_coarse, fine_own))

    fine_tiles = ceil_to(fine_own - LOCAL + (peers - 1) * fine_cap, LANES) // LANES
    coarse_tiles = ceil_to(coarse_own + (peers - 1) * coarse_cap, LANES) // LANES
    variants = [(min(n, fine_tiles), min(2, coarse_tiles)) for n in (2, 3)]
    variants = variants + [(fine_tiles, coarse_tiles)]
    idx, tail, to, pick, own_idx, own_tail = plan(
        asks_fine, asks_coarse, list_fine, list_coarse, variants, fine_tiles * LANES
    )

    fine_rows = dens_fine.T
    positions = jnp.arange(8, dtype=jnp.int32)
    spread = jnp.where(
        (child_code[:, None] == positions[None, :])[:, :, None],
        fine_rows[:, None, :],
        jnp.zeros((), jnp.bfloat16),
    )
    child_terms = lax.dot_general(
        spread.reshape(fine_own, 8 * surface),
        m2m_ops.reshape(surface, 8 * surface),
        (((1,), (1,)), ((), ())),
        preferred_element_type=jnp.float32,
    )
    local_parent = parent - lax.axis_index(AXES) * coarse_own
    members = (jnp.arange(coarse_own, dtype=jnp.int32)[:, None] == local_parent[None, :]).astype(
        jnp.float32
    )
    coarse_rows = jnp.dot(members, child_terms, precision=lax.Precision.HIGHEST).astype(
        jnp.bfloat16
    )

    arrived = exchange(answer(wanted, fine_rows, coarse_rows))
    operators, part = local_part(fine_rows, own_idx, own_tail, m2l_ops, wanted)
    pot_fine, pot_coarse = translate(
        pick,
        idx,
        tail,
        to,
        fine_rows,
        coarse_rows,
        arrived,
        part,
        operators,
        variants,
        fine_tiles,
        fine_tiles + coarse_tiles,
    )
    return pot_fine.T, pot_coarse.T


def solution(mesh):
    return jax.shard_map(
        body,
        mesh=mesh,
        in_specs=(
            P(None, AXES),
            P(AXES),
            P(AXES),
            P(),
            P(),
            P(AXES, None, None),
            P(AXES, None),
            P(AXES, None, None),
            P(AXES, None),
        ),
        out_specs=(P(None, AXES), P(None, AXES)),
        check_vma=False,
    )
```

```python
import functools

import jax
import jax.numpy as jnp
from jax import lax
from jax.experimental import pallas as pl
from jax.experimental.pallas import tpu as pltpu
from jax.sharding import PartitionSpec as P

LANES = 128
CHUNK = 16
HALF = LANES // 2
BLANK = 1 << 20
LOCAL = 0
AXES = ("leaf", "oct")
STAGE_A, STAGE_B = 23, 3
VMEM_BYTES = 56 << 20


def ceil_to(n, m):
    return (n + m - 1) // m * m


def lane_iota(shape):
    return lax.broadcasted_iota(jnp.int32, shape, 1)


def whole(x):
    return pl.BlockSpec(x.shape, lambda *i: (0,) * x.ndim)


def shape_of(shape, dtype):
    return jax.ShapeDtypeStruct(shape, dtype)


def asks_kernel(fine_own, f_ref, c_ref, o_ref, scr):
    fine_cap, peers = f_ref.shape
    coarse_cap = c_ref.shape[0]
    scr[...] = jnp.zeros_like(scr)
    scr[0:fine_cap, 0:peers] = f_ref[...]
    coarse = c_ref[...]
    scr[fine_cap : fine_cap + coarse_cap, 0:peers] = jnp.where(coarse < 0, -1, coarse + fine_own)
    o_ref[...] = scr[...].T[0:peers, 0 : fine_cap + coarse_cap]


def join_asks(asks_fine, asks_coarse, fine_own):
    peers = asks_fine.shape[1]
    slots = asks_fine.shape[0] + asks_coarse.shape[0]
    return pl.pallas_call(
        functools.partial(asks_kernel, fine_own),
        out_shape=shape_of((peers, slots), jnp.int32),
        scratch_shapes=[pltpu.VMEM((LANES, LANES), jnp.int32)],
        name="join_asks",
    )(asks_fine, asks_coarse)


def answer_kernel(w_ref, f_ref, c_any, o_ref, scr, hot, c_ref, sem):
    peers, slots = w_ref.shape
    own, surface = f_ref.shape[0] + c_ref.shape[0], f_ref.shape[1]
    fetch = pltpu.make_async_copy(c_any, c_ref, sem)
    fetch.start()
    scr[0:peers, 0:slots] = w_ref[...]
    columns = scr[...].T[0:slots, :]
    octant = lane_iota((slots, own))
    for e in range(0, peers, 2):
        picked = [
            jnp.broadcast_to(columns[:, d : d + 1], (slots, own)) == octant for d in (e, e + 1)
        ]
        both = jnp.concatenate([p.astype(jnp.float32) for p in picked], axis=0)
        hot[e * slots : (e + 2) * slots, :] = both.astype(jnp.bfloat16)
    fetch.wait()
    rows = jnp.concatenate([f_ref[...], c_ref[...]], axis=0)
    found = jnp.dot(hot[...], rows, preferred_element_type=jnp.float32)
    extra = surface - LANES
    rest = jnp.concatenate(
        [found[:, LANES:], jnp.zeros((peers * slots, LANES - extra), jnp.float32)], axis=1
    ).reshape(peers, slots, LANES)
    line = rest[:, 0:8].reshape(peers * 8, LANES)
    for g in range(1, slots // 8):
        part = rest[:, 8 * g : 8 * g + 8].reshape(peers * 8, LANES)
        line = line + pltpu.roll(part, g * extra, axis=1)
    o_ref[...] = jnp.concatenate(
        [found[:, 0:LANES].reshape(peers, slots, LANES), line.reshape(peers, 8, LANES)], axis=1
    ).astype(jnp.bfloat16)


def answer(wanted, fine_rows, coarse_rows):
    peers, slots = wanted.shape
    own = fine_rows.shape[0] + coarse_rows.shape[0]
    return pl.pallas_call(
        answer_kernel,
        in_specs=[whole(wanted), whole(fine_rows), pl.BlockSpec(memory_space=pl.ANY)],
        out_shape=shape_of((peers, slots + 8, LANES), jnp.bfloat16),
        scratch_shapes=[
            pltpu.VMEM((LANES, LANES), jnp.int32),
            pltpu.VMEM((peers * slots, own), jnp.bfloat16),
            pltpu.VMEM(coarse_rows.shape, jnp.bfloat16),
            pltpu.SemaphoreType.DMA,
        ],
        name="answer",
    )(wanted, fine_rows, coarse_rows)


def remap(entries, own, done, cap, shift):
    slot = jnp.maximum(entries - own, 0)
    peer = slot // cap
    moved = jnp.take_along_axis(
        jnp.broadcast_to(shift, entries.shape), peer, axis=1, mode="promise_in_bounds"
    )
    column = jnp.where(entries < own, entries, entries - moved) - done
    return jnp.where(entries < done, BLANK, column)


def plan_kernel(
    variants,
    coarse_at,
    af_ref,
    ac_ref,
    lf_ref,
    lc_ref,
    idx_ref,
    tail_ref,
    to_ref,
    pick_ref,
    cnt,
):
    offsets = lf_ref.shape[1]
    body_lanes = idx_ref.shape[1]
    peers = af_ref.shape[1]
    lanes = lane_iota((LANES, LANES))
    earlier = lax.broadcasted_iota(jnp.int32, (LANES, LANES), 0) < lanes
    earlier = earlier.astype(jnp.float32).astype(jnp.bfloat16)
    levels = []
    row = tail_row = 0
    cnt[...] = jnp.zeros_like(cnt)
    for level, (ask_ref, list_ref) in enumerate(((af_ref, lf_ref), (ac_ref, lc_ref))):
        own, cap = list_ref.shape[0], ask_ref.shape[0]
        done = LOCAL if level == 0 else 0
        valid = (ask_ref[...] >= 0).astype(jnp.float32)
        cnt[level, 0:1, 0:peers] = jnp.sum(valid, axis=0, keepdims=True)
        counts = cnt[level]
        before = jnp.dot(
            counts.astype(jnp.bfloat16), earlier, preferred_element_type=jnp.float32
        ).astype(jnp.int32)[0:1]
        total = jnp.sum(counts).astype(jnp.int32)
        counts = counts.astype(jnp.int32)[0:1]
        shift = lane_iota((1, LANES)) * cap - before
        levels.append((own, cap, counts, before, total))
        lists = [list_ref[:, first : first + LANES] for first in range(0, body_lanes, LANES)]
        lists.append(
            jnp.concatenate(
                [
                    list_ref[:, body_lanes:offsets],
                    jnp.full((own, LANES - (offsets - body_lanes)), -1, jnp.int32),
                ],
                axis=1,
            )
        )
        upper = tail_rows(own)

        def keep(columns, to_body, to_tail, at, tail_at):
            for k, x in enumerate(columns[:-1]):
                to_body[at : at + own, k * LANES : (k + 1) * LANES] = x
            rest = columns[-1]
            moved = pltpu.roll(rest[upper:], HALF, axis=1)
            if own - upper < upper:
                missing = jnp.full((2 * upper - own, LANES), BLANK, jnp.int32)
                moved = jnp.concatenate([moved, missing], axis=0)
            to_tail[tail_at : tail_at + upper, :] = jnp.where(
                lane_iota((upper, LANES)) < HALF, rest[0:upper], moved
            )

        keep([remap(x, own, done, cap, shift) for x in lists], idx_ref, tail_ref, row, tail_row)
        row += own
        tail_row += upper

    (fine_own, fine_cap, *fine), (coarse_own, coarse_cap, *coarse) = levels
    place = lax.broadcasted_iota(jnp.int32, (8, LANES), 0)
    at = 0
    for level, base in (((fine_cap, *fine), fine_own - LOCAL), ((coarse_cap, *coarse), coarse_at + coarse_own)):
        cap, counts, before, _ = level
        for first in range(0, cap, 8):
            for e in range(peers):
                count = jnp.broadcast_to(counts[:, e : e + 1], (8, LANES))
                start = jnp.broadcast_to(before[:, e : e + 1], (8, LANES)) + base
                k = place + first
                to_ref[at : at + 8, :] = jnp.where(k < count, start + k, -1)
                at += 8
    octant = lax.broadcasted_iota(jnp.int32, (fine_own, LANES), 0)
    to_ref[at : at + fine_own, :] = jnp.maximum(octant - LOCAL, -1)
    octant = lax.broadcasted_iota(jnp.int32, (coarse_own, LANES), 0)
    to_ref[at + fine_own : at + row, :] = octant + coarse_at

    pick = jnp.int32(len(variants) - 1)
    for at in reversed(range(len(variants) - 1)):
        fits = (fine_own - LOCAL + fine[2] <= variants[at][0] * LANES) & (
            coarse_own + coarse[2] <= variants[at][1] * LANES
        )
        pick = jnp.where(fits, at, pick)
    pick_ref[0] = pick


def plan(asks_fine, asks_coarse, list_fine, list_coarse, variants, coarse_at):
    own = list_fine.shape[0] + list_coarse.shape[0]
    tails = sum(tail_rows(x.shape[0]) for x in (list_fine, list_coarse))
    body_lanes = list_fine.shape[1] // LANES * LANES
    slots, peers = asks_fine.shape[0] + asks_coarse.shape[0], asks_fine.shape[1]
    vmem = pl.BlockSpec(memory_space=pltpu.VMEM)
    return pl.pallas_call(
        functools.partial(plan_kernel, variants, coarse_at),
        out_specs=[vmem, vmem, vmem, pl.BlockSpec(memory_space=pltpu.SMEM)],
        out_shape=[
            shape_of((own, body_lanes), jnp.int32),
            shape_of((tails, LANES), jnp.int32),
            shape_of((own + peers * slots, LANES), jnp.int32),
            shape_of((1,), jnp.int32),
        ],
        scratch_shapes=[pltpu.VMEM((2, 8, LANES), jnp.float32)],
        compiler_params=pltpu.CompilerParams(vmem_limit_bytes=VMEM_BYTES),
        name="plan",
    )(asks_fine, asks_coarse, list_fine, list_coarse)


def pack_rows(values, table, tile):
    pairs = values.shape[0] // 2
    even = values[pl.ds(0, pairs, stride=2), :].astype(jnp.int32)
    odd = values[pl.ds(1, pairs, stride=2), :].astype(jnp.int32)
    both = odd * 65536 + even
    for block in range(pairs // 4):
        table[block, 0:4, tile * LANES : (tile + 1) * LANES] = both[4 * block : 4 * block + 4]


def scale_of(values):
    peak = jnp.max(jnp.max(jnp.abs(values), axis=0, keepdims=True), axis=1, keepdims=True)
    power = jnp.floor(jnp.log2(jnp.broadcast_to(jnp.maximum(peak, 1e-30), (8, LANES))))
    return jnp.exp2(13.0 - power)[0:1], jnp.exp2(power - 29.0)


def build_tables(ranges, to_ref, f_ref, c_ref, arrived, rows_t, table_f, table, unit):
    peers, lines, _ = arrived.shape
    surface = rows_t.shape[0]
    extra = surface - LANES
    came = arrived[...].astype(jnp.float32)
    rest = came[:, lines - 8 :].reshape(peers * 8, LANES).T
    at = 0
    for g in range(lines // 8 - 1):
        part = came[:, 8 * g : 8 * g + 8].reshape(peers * 8, LANES).T
        part = jnp.concatenate([part, rest[g * extra : (g + 1) * extra]], axis=0)
        rows_t[:, at : at + peers * 8] = part.astype(jnp.bfloat16)
        at += peers * 8
    own = jnp.concatenate([f_ref[...], c_ref[...]], axis=0).astype(jnp.float32)
    rows_t[:, at : at + own.shape[0]] = own.T.astype(jnp.bfloat16)
    to = to_ref[...]
    tiles = table_f.shape[0]
    lanes = lane_iota(to.shape)
    for k in range(0, tiles, 2):
        size = min(2, tiles - k)
        hot = [(to == lanes + (k + h) * LANES).astype(jnp.float32) for h in range(size)]
        hot = jnp.concatenate([x.astype(jnp.bfloat16) for x in hot], axis=1)
        columns = jnp.dot(rows_t[...], hot, preferred_element_type=jnp.float32)
        for h in range(size):
            table_f[k + h] = columns[:, h * LANES : (h + 1) * LANES]
    for level, (low, high) in enumerate(ranges):
        factor, unit[level] = scale_of(jnp.max(jnp.abs(table_f[low:high]), axis=0))
        for k in range(low, high):
            table_f[k] = jnp.round(table_f[k] * factor)
            pack_rows(table_f.at[k], table, k)


def stage_block(m_ref, stage):
    surface, _, offsets = m_ref.shape
    for tile, first in enumerate(range(0, offsets, LANES)):
        size = min(LANES, offsets - first)
        for a in range(surface):
            part = m_ref[a, :, first : first + size].astype(jnp.float32)
            stage[tile, pl.ds(STAGE_A * a, 8, stride=STAGE_B), 0:size] = part


def lay_half(half, stage, mr_ref):
    surface = mr_ref.shape[0]
    tiles = stage.shape[0]
    for j in range(4):
        for tile in range(tiles):
            rows = stage[tile, pl.ds(STAGE_B * (4 * half + j), surface, stride=STAGE_A), :]
            at = (j * tiles + tile) * LANES
            mr_ref[:, at : at + LANES] = rows.astype(jnp.bfloat16)


def gather_half(half, step, levels, idx_ref, tail_ref, table, g_ref):
    body_lanes = idx_ref.shape[1]
    width = body_lanes + LANES
    lower = lane_iota((CHUNK, LANES)) < HALF

    def put(rows, q, at, value):
        to = 2 * q * width + at
        low = (value << 16).astype(jnp.float32).astype(jnp.bfloat16)
        high = value.astype(jnp.float32).astype(jnp.bfloat16)
        g_ref[rows : rows + CHUNK, to : to + LANES] = low
        g_ref[rows : rows + CHUNK, to + width : to + width + LANES] = high

    for low, high, base, tiles, tail_row in levels:
        rows = [
            [
                jnp.broadcast_to(
                    table[step, pair : pair + 1, (base + k) * LANES : (base + k + 1) * LANES],
                    (CHUNK, LANES),
                )
                for k in range(tiles)
            ]
            for pair in (2 * half, 2 * half + 1)
        ]

        def gathered(idx):
            at = idx & (LANES - 1)
            later = [idx >= k * LANES for k in range(1, tiles)]
            blank = idx >= BLANK
            for q in range(2):
                value = None
                for k in range(tiles):
                    got = jnp.take_along_axis(rows[q][k], at, axis=1, mode="promise_in_bounds")
                    value = got if k == 0 else jnp.where(later[k - 1], got, value)
                yield q, jnp.where(blank, 0, value)

        for first in range(0, body_lanes, LANES):
            for target in range(low, high, CHUNK):
                idx = idx_ref[target : target + CHUNK, first : first + LANES]
                for q, value in gathered(idx):
                    put(target, q, first, value)
        upper = tail_rows(high - low)
        for target in range(low, low + upper, CHUNK):
            at = tail_row + target - low
            for q, value in gathered(tail_ref[at : at + CHUNK, :]):
                put(target, q, body_lanes, jnp.where(lower, value, 0))
                if target + upper < high:
                    moved = pltpu.roll(value, HALF, axis=1)
                    put(target + upper, q, body_lanes, jnp.where(lower, moved, 0))


def multiply(acc, g_ref, mr):
    acc[...] += lax.dot_general(
        g_ref[...], mr, (((1,), (1,)), ((), ())), preferred_element_type=jnp.float32
    )


def tail_rows(own):
    return ceil_to(own // CHUNK, 2) // 2 * CHUNK


def translate_kernel(
    variants,
    coarse_tile,
    pick_ref,
    idx_ref,
    tail_ref,
    to_ref,
    f_ref,
    c_ref,
    arrived_any,
    m_ref,
    of_ref,
    oc_ref,
    rows_t,
    table_f,
    table,
    unit,
    arrived,
    stage,
    acc,
    mr_a,
    mr_b,
    g_a,
    g_b,
    sem,
):
    fine_own, targets = of_ref.shape[0], idx_ref.shape[0]
    step = pl.program_id(0)

    @pl.when(step == 0)
    def _():
        fetch = pltpu.make_async_copy(arrived_any, arrived, sem)
        fetch.start()
        for ref in (acc, stage, mr_b, g_b):
            ref[...] = jnp.zeros_like(ref)
        fetch.wait()
        build_tables(
            ((0, coarse_tile), (coarse_tile, table_f.shape[0])),
            to_ref,
            f_ref,
            c_ref,
            arrived,
            rows_t,
            table_f,
            table,
            unit,
        )

    def work(fine_tiles, coarse_tiles):
        levels = (
            (0, fine_own, 0, fine_tiles, 0),
            (fine_own, targets, coarse_tile, coarse_tiles, tail_rows(fine_own)),
        )
        stage_block(m_ref, stage)
        lay_half(0, stage, mr_a)
        multiply(acc, g_b, mr_b[...])
        gather_half(0, step, levels, idx_ref, tail_ref, table, g_a)
        lay_half(1, stage, mr_b)
        multiply(acc, g_a, mr_a[...])
        gather_half(1, step, levels, idx_ref, tail_ref, table, g_b)

    for at, tiles in enumerate(variants):
        pl.when(pick_ref[0] == at)(functools.partial(work, *tiles))

    @pl.when(step == pl.num_programs(0) - 1)
    def _():
        multiply(acc, g_b, mr_b[...])
        of_ref[...] = acc[0:fine_own, :] * unit[0, 0:1, 0:1]
        oc_ref[...] = acc[fine_own:targets, :] * (0.5 * unit[1, 0:1, 0:1])


def translate(
    pick, idx, tail, to, fine_rows, coarse_rows, arrived, m2l_ops, variants, coarse_tile, tiles
):
    surface, _, offsets = m2l_ops.shape
    width = ceil_to(offsets, LANES)
    targets = idx.shape[0]
    fine_own, coarse_own = fine_rows.shape[0], coarse_rows.shape[0]
    blocks = surface // 8
    return pl.pallas_call(
        functools.partial(translate_kernel, variants, coarse_tile),
        grid=(blocks,),
        in_specs=[
            pl.BlockSpec(memory_space=pltpu.SMEM),
            whole(idx),
            whole(tail),
            whole(to),
            whole(fine_rows),
            whole(coarse_rows),
            pl.BlockSpec(memory_space=pl.ANY),
            pl.BlockSpec((surface, 8, offsets), lambda i: (0, i, 0)),
        ],
        out_specs=[
            pl.BlockSpec((fine_own, surface), lambda i: (0, 0)),
            pl.BlockSpec((coarse_own, surface), lambda i: (0, 0)),
        ],
        out_shape=[
            shape_of((fine_own, surface), jnp.float32),
            shape_of((coarse_own, surface), jnp.float32),
        ],
        scratch_shapes=[
            pltpu.VMEM((surface, to.shape[0]), jnp.bfloat16),
            pltpu.VMEM((tiles, surface, LANES), jnp.float32),
            pltpu.VMEM((blocks, 8, tiles * LANES), jnp.int32),
            pltpu.VMEM((2, 8, LANES), jnp.float32),
            pltpu.VMEM(arrived.shape, jnp.bfloat16),
            pltpu.VMEM((width // LANES, ceil_to(STAGE_A * surface, 8), LANES), jnp.float32),
            pltpu.VMEM((targets, surface), jnp.float32),
            pltpu.VMEM((surface, 4 * width), jnp.bfloat16),
            pltpu.VMEM((surface, 4 * width), jnp.bfloat16),
            pltpu.VMEM((targets, 4 * width), jnp.bfloat16),
            pltpu.VMEM((targets, 4 * width), jnp.bfloat16),
            pltpu.SemaphoreType.DMA,
        ],
        compiler_params=pltpu.CompilerParams(vmem_limit_bytes=VMEM_BYTES),
        cost_estimate=pl.CostEstimate(
            flops=2 * surface * surface * targets * width,
            bytes_accessed=2 * surface * surface * width,
            transcendentals=0,
        ),
        name="translate",
    )(pick, idx, tail, to, fine_rows, coarse_rows, arrived, m2l_ops)


def exchange(x):
    return lax.all_to_all(x, AXES, split_axis=0, concat_axis=0, tiled=True)


def body(
    dens_fine, parent, child_code, m2m_ops, m2l_ops, ask_fine, list_fine, ask_coarse, list_coarse
):
    surface, fine_own = dens_fine.shape
    coarse_own = list_coarse.shape[0]
    asks_fine, asks_coarse = ask_fine[0].T, ask_coarse[0].T
    fine_cap, peers = asks_fine.shape
    coarse_cap = asks_coarse.shape[0]
    wanted = exchange(join_asks(asks_fine, asks_coarse, fine_own))

    fine_tiles = ceil_to(fine_own - LOCAL + (peers - 1) * fine_cap, LANES) // LANES
    coarse_tiles = ceil_to(coarse_own + (peers - 1) * coarse_cap, LANES) // LANES
    variants = [(min(n, fine_tiles), min(2, coarse_tiles)) for n in (3, 4)]
    variants = variants + [(fine_tiles, coarse_tiles)]
    idx, tail, to, pick = plan(
        asks_fine, asks_coarse, list_fine, list_coarse, variants, fine_tiles * LANES
    )

    fine_rows = dens_fine.T
    positions = jnp.arange(8, dtype=jnp.int32)
    spread = jnp.where(
        (child_code[:, None] == positions[None, :])[:, :, None],
        fine_rows[:, None, :],
        jnp.zeros((), jnp.bfloat16),
    )
    child_terms = lax.dot_general(
        spread.reshape(fine_own, 8 * surface),
        m2m_ops.reshape(surface, 8 * surface),
        (((1,), (1,)), ((), ())),
        preferred_element_type=jnp.float32,
    )
    local_parent = parent - lax.axis_index(AXES) * coarse_own
    members = (jnp.arange(coarse_own, dtype=jnp.int32)[:, None] == local_parent[None, :]).astype(
        jnp.float32
    )
    coarse_rows = jnp.dot(members, child_terms, precision=lax.Precision.HIGHEST).astype(
        jnp.bfloat16
    )

    arrived = exchange(answer(wanted, fine_rows, coarse_rows))
    pot_fine, pot_coarse = translate(
        pick,
        idx,
        tail,
        to,
        fine_rows,
        coarse_rows,
        arrived,
        m2l_ops,
        variants,
        fine_tiles,
        fine_tiles + coarse_tiles,
    )
    return pot_fine.T, pot_coarse.T


def solution(mesh):
    return jax.shard_map(
        body,
        mesh=mesh,
        in_specs=(
            P(None, AXES),
            P(AXES),
            P(AXES),
            P(),
            P(),
            P(AXES, None, None),
            P(AXES, None),
            P(AXES, None, None),
            P(AXES, None),
        ),
        out_specs=(P(None, AXES), P(None, AXES)),
        check_vma=False,
    )
```

```python
import functools

import jax
import jax.numpy as jnp
from jax import lax
from jax.experimental import pallas as pl
from jax.experimental.pallas import tpu as pltpu
from jax.sharding import PartitionSpec as P

LANES = 128
CHUNK = 16
HALF = LANES // 2
BLANK = -1
LOCAL = LANES
AXES = ("leaf", "oct")
STAGE_A, STAGE_B = 23, 3
VMEM_BYTES = 48 << 20


def ceil_to(n, m):
    return (n + m - 1) // m * m


def lane_iota(shape):
    return lax.broadcasted_iota(jnp.int32, shape, 1)


def whole(x):
    return pl.BlockSpec(x.shape, lambda *i: (0,) * x.ndim)


def shape_of(shape, dtype):
    return jax.ShapeDtypeStruct(shape, dtype)


def power_of(values):
    peak = jnp.max(jnp.max(jnp.abs(values), axis=0, keepdims=True), axis=1, keepdims=True)
    return jnp.floor(jnp.log2(jnp.broadcast_to(jnp.maximum(peak, 1e-30), (8, LANES))))


def asks_kernel(f_ref, c_ref, rows_ref, o_ref, scr):
    fine_cap, peers = f_ref.shape
    coarse_cap = c_ref.shape[0]
    slots = fine_cap + coarse_cap
    rows = rows_ref[...].astype(jnp.float32)
    power = power_of(jnp.max(rows.reshape(-1, 8, rows.shape[1]), axis=0))
    low = power_of(jnp.min(rows.reshape(-1, 8, rows.shape[1]), axis=0))
    scr[...] = jnp.zeros_like(scr)
    scr[0:fine_cap, 0:peers] = f_ref[...]
    coarse = c_ref[...]
    scr[fine_cap:slots, 0:peers] = jnp.where(coarse < 0, -1, coarse + rows_ref.shape[0])
    scr[slots : slots + 8, :] = jnp.maximum(power, low).astype(jnp.int32)
    o_ref[...] = scr[...].T[0:peers, 0 : slots + 1]


def join_asks(asks_fine, asks_coarse, fine_rows):
    peers = asks_fine.shape[1]
    slots = asks_fine.shape[0] + asks_coarse.shape[0]
    return pl.pallas_call(
        asks_kernel,
        out_shape=shape_of((peers, slots + 1), jnp.int32),
        scratch_shapes=[pltpu.VMEM((LANES, LANES), jnp.int32)],
        name="join_asks",
    )(asks_fine, asks_coarse, fine_rows)


def fine_power(w_ref):
    peers, columns = w_ref.shape
    power = jnp.max(w_ref[:, columns - 1 : columns], axis=0, keepdims=True)
    return jnp.broadcast_to(power, (8, LANES)).astype(jnp.float32)


def answer_kernel(w_ref, f_ref, c_any, o_ref, scr, hot, c_ref, sem):
    peers, slots = w_ref.shape[0], w_ref.shape[1] - 1
    own, surface = f_ref.shape[0] + c_ref.shape[0], f_ref.shape[1]
    fetch = pltpu.make_async_copy(c_any, c_ref, sem)
    fetch.start()
    scr[0:peers, 0 : slots + 1] = w_ref[...]
    columns = scr[...].T[0:slots, :]
    octant = lane_iota((slots, own))
    for e in range(0, peers, 2):
        picked = [
            jnp.broadcast_to(columns[:, d : d + 1], (slots, own)) == octant for d in (e, e + 1)
        ]
        both = jnp.concatenate([p.astype(jnp.float32) for p in picked], axis=0)
        hot[e * slots : (e + 2) * slots, :] = both.astype(jnp.bfloat16)
    fetch.wait()
    rows = jnp.concatenate([f_ref[...], c_ref[...]], axis=0)
    found = jnp.dot(hot[...], rows, preferred_element_type=jnp.float32)
    extra = surface - LANES
    rest = jnp.concatenate(
        [found[:, LANES:], jnp.zeros((peers * slots, LANES - extra), jnp.float32)], axis=1
    ).reshape(peers, slots, LANES)
    line = rest[:, 0:8].reshape(peers * 8, LANES)
    for g in range(1, slots // 8):
        part = rest[:, 8 * g : 8 * g + 8].reshape(peers * 8, LANES)
        line = line + pltpu.roll(part, g * extra, axis=1)
    o_ref[...] = jnp.concatenate(
        [found[:, 0:LANES].reshape(peers, slots, LANES), line.reshape(peers, 8, LANES)], axis=1
    ).astype(jnp.bfloat16)


def answer(wanted, fine_rows, coarse_rows):
    peers, slots = wanted.shape[0], wanted.shape[1] - 1
    own = fine_rows.shape[0] + coarse_rows.shape[0]
    return pl.pallas_call(
        answer_kernel,
        in_specs=[whole(wanted), whole(fine_rows), pl.BlockSpec(memory_space=pl.ANY)],
        out_shape=shape_of((peers, slots + 8, LANES), jnp.bfloat16),
        scratch_shapes=[
            pltpu.VMEM((LANES, LANES), jnp.int32),
            pltpu.VMEM((peers * slots, own), jnp.bfloat16),
            pltpu.VMEM(coarse_rows.shape, jnp.bfloat16),
            pltpu.SemaphoreType.DMA,
        ],
        compiler_params=pltpu.CompilerParams(vmem_limit_bytes=16 << 20),
        name="answer",
    )(wanted, fine_rows, coarse_rows)


def remap(entries, own, done, cap, shift):
    slot = jnp.maximum(entries - own, 0)
    peer = slot // cap
    moved = jnp.take_along_axis(
        jnp.broadcast_to(shift, entries.shape), peer, axis=1, mode="promise_in_bounds"
    )
    column = jnp.where(entries < own, entries, entries - moved) - done
    return jnp.where(entries < done, BLANK, column)


def plan_kernel(
    variants,
    coarse_at,
    af_ref,
    ac_ref,
    lf_ref,
    lc_ref,
    idx_ref,
    tail_ref,
    to_ref,
    pick_ref,
    own_idx_ref,
    own_tail_ref,
    cnt,
):
    offsets = lf_ref.shape[1]
    body_lanes = idx_ref.shape[1]
    peers = af_ref.shape[1]
    lanes = lane_iota((LANES, LANES))
    earlier = lax.broadcasted_iota(jnp.int32, (LANES, LANES), 0) < lanes
    earlier = earlier.astype(jnp.float32).astype(jnp.bfloat16)
    levels = []
    row = tail_row = 0
    cnt[...] = jnp.zeros_like(cnt)
    for level, (ask_ref, list_ref) in enumerate(((af_ref, lf_ref), (ac_ref, lc_ref))):
        own, cap = list_ref.shape[0], ask_ref.shape[0]
        done = LOCAL if level == 0 else 0
        valid = (ask_ref[...] >= 0).astype(jnp.float32)
        cnt[level, 0:1, 0:peers] = jnp.sum(valid, axis=0, keepdims=True)
        counts = cnt[level]
        before = jnp.dot(
            counts.astype(jnp.bfloat16), earlier, preferred_element_type=jnp.float32
        ).astype(jnp.int32)[0:1]
        total = jnp.sum(counts).astype(jnp.int32)
        counts = counts.astype(jnp.int32)[0:1]
        shift = lane_iota((1, LANES)) * cap - before
        levels.append((own, cap, counts, before, total))
        lists = [list_ref[:, first : first + LANES] for first in range(0, body_lanes, LANES)]
        lists.append(
            jnp.concatenate(
                [
                    list_ref[:, body_lanes:offsets],
                    jnp.full((own, LANES - (offsets - body_lanes)), -1, jnp.int32),
                ],
                axis=1,
            )
        )
        upper = tail_rows(own)

        def keep(columns, to_body, to_tail, at, tail_at):
            for k, x in enumerate(columns[:-1]):
                to_body[at : at + own, k * LANES : (k + 1) * LANES] = x
            rest = columns[-1]
            moved = pltpu.roll(rest[upper:], HALF, axis=1)
            if own - upper < upper:
                missing = jnp.full((2 * upper - own, LANES), BLANK, jnp.int32)
                moved = jnp.concatenate([moved, missing], axis=0)
            to_tail[tail_at : tail_at + upper, :] = jnp.where(
                lane_iota((upper, LANES)) < HALF, rest[0:upper], moved
            )

        keep([remap(x, own, done, cap, shift) for x in lists], idx_ref, tail_ref, row, tail_row)
        if level == 0:
            near = [jnp.where(x < LOCAL, x, BLANK) for x in lists]
            keep(near, own_idx_ref, own_tail_ref, 0, 0)
        row += own
        tail_row += upper

    (fine_own, fine_cap, *fine), (coarse_own, coarse_cap, *coarse) = levels
    place = lax.broadcasted_iota(jnp.int32, (8, LANES), 0)
    at = 0
    for level, base in (((fine_cap, *fine), fine_own - LOCAL), ((coarse_cap, *coarse), coarse_at + coarse_own)):
        cap, counts, before, _ = level
        for first in range(0, cap, 8):
            for e in range(peers):
                count = jnp.broadcast_to(counts[:, e : e + 1], (8, LANES))
                start = jnp.broadcast_to(before[:, e : e + 1], (8, LANES)) + base
                k = place + first
                to_ref[at : at + 8, :] = jnp.where(k < count, start + k, -1)
                at += 8
    octant = lax.broadcasted_iota(jnp.int32, (fine_own, LANES), 0)
    to_ref[at : at + fine_own, :] = jnp.maximum(octant - LOCAL, -1)
    octant = lax.broadcasted_iota(jnp.int32, (coarse_own, LANES), 0)
    to_ref[at + fine_own : at + row, :] = octant + coarse_at

    pick = jnp.int32(len(variants) - 1)
    for at in reversed(range(len(variants) - 1)):
        fits = (fine_own - LOCAL + fine[2] <= variants[at][0] * LANES) & (
            coarse_own + coarse[2] <= variants[at][1] * LANES
        )
        pick = jnp.where(fits, at, pick)
    pick_ref[0] = pick


def plan(asks_fine, asks_coarse, list_fine, list_coarse, variants, coarse_at):
    own = list_fine.shape[0] + list_coarse.shape[0]
    tails = sum(tail_rows(x.shape[0]) for x in (list_fine, list_coarse))
    body_lanes = list_fine.shape[1] // LANES * LANES
    slots, peers = asks_fine.shape[0] + asks_coarse.shape[0], asks_fine.shape[1]
    vmem = pl.BlockSpec(memory_space=pltpu.VMEM)
    return pl.pallas_call(
        functools.partial(plan_kernel, variants, coarse_at),
        out_specs=[vmem, vmem, vmem, pl.BlockSpec(memory_space=pltpu.SMEM), vmem, vmem],
        out_shape=[
            shape_of((own, body_lanes), jnp.int32),
            shape_of((tails, LANES), jnp.int32),
            shape_of((own + peers * slots, LANES), jnp.int32),
            shape_of((1,), jnp.int32),
            shape_of((list_fine.shape[0], body_lanes), jnp.int32),
            shape_of((tail_rows(list_fine.shape[0]), LANES), jnp.int32),
        ],
        scratch_shapes=[pltpu.VMEM((2, 8, LANES), jnp.float32)],
        compiler_params=pltpu.CompilerParams(vmem_limit_bytes=VMEM_BYTES),
        name="plan",
    )(asks_fine, asks_coarse, list_fine, list_coarse)


def pack_rows(values, table, tile):
    pairs = values.shape[0] // 2
    even = values[pl.ds(0, pairs, stride=2), :].astype(jnp.int32)
    odd = values[pl.ds(1, pairs, stride=2), :].astype(jnp.int32)
    both = odd * 65536 + even
    for block in range(pairs // 4):
        table[block, 0:4, tile * LANES : (tile + 1) * LANES] = both[4 * block : 4 * block + 4]


def build_tables(ranges, w_ref, to_ref, f_ref, c_ref, arrived, rows_t, table_f, table, unit):
    peers, lines, _ = arrived.shape
    surface = rows_t.shape[0]
    extra = surface - LANES
    came = arrived[...].astype(jnp.float32)
    rest = came[:, lines - 8 :].reshape(peers * 8, LANES).T
    at = 0
    for g in range(lines // 8 - 1):
        part = came[:, 8 * g : 8 * g + 8].reshape(peers * 8, LANES).T
        part = jnp.concatenate([part, rest[g * extra : (g + 1) * extra]], axis=0)
        rows_t[:, at : at + peers * 8] = part.astype(jnp.bfloat16)
        at += peers * 8
    own = jnp.concatenate([f_ref[...], c_ref[...]], axis=0).astype(jnp.float32)
    rows_t[:, at : at + own.shape[0]] = own.T.astype(jnp.bfloat16)
    to = to_ref[...]
    tiles = table_f.shape[0]
    lanes = lane_iota(to.shape)
    for k in range(0, tiles, 2):
        size = min(2, tiles - k)
        hot = [(to == lanes + (k + h) * LANES).astype(jnp.float32) for h in range(size)]
        hot = jnp.concatenate([x.astype(jnp.bfloat16) for x in hot], axis=1)
        columns = jnp.dot(rows_t[...], hot, preferred_element_type=jnp.float32)
        for h in range(size):
            table_f[k + h] = columns[:, h * LANES : (h + 1) * LANES]
    for level, (low, high) in enumerate(ranges):
        if level == 0:
            power = fine_power(w_ref)
        else:
            power = power_of(jnp.max(jnp.abs(table_f[low:high]), axis=0))
        factor = jnp.exp2(13.0 - power)[0:1]
        unit[level] = jnp.exp2(power - 29.0)
        for k in range(low, high):
            table_f[k] = jnp.round(table_f[k] * factor)
            pack_rows(table_f.at[k], table, k)


def stage_block(m_ref, stage):
    surface, _, offsets = m_ref.shape
    for tile, first in enumerate(range(0, offsets, LANES)):
        size = min(LANES, offsets - first)
        for a in range(surface):
            part = m_ref[a, :, first : first + size].astype(jnp.float32)
            if size < LANES:
                part = jnp.concatenate([part, jnp.zeros((8, LANES - size), jnp.float32)], axis=1)
            stage[tile, pl.ds(STAGE_A * a, 8, stride=STAGE_B), :] = part


def lay_half(half, stage, mr_ref):
    surface = mr_ref.shape[0]
    tiles = stage.shape[0]
    for j in range(4):
        for tile in range(tiles):
            rows = stage[tile, pl.ds(STAGE_B * (4 * half + j), surface, stride=STAGE_A), :]
            at = (j * tiles + tile) * LANES
            mr_ref[:, at : at + LANES] = rows.astype(jnp.bfloat16)


def gather_half(half, step, levels, idx_ref, tail_ref, table, g_ref):
    body_lanes = idx_ref.shape[1]
    width = body_lanes + LANES
    lower = lane_iota((CHUNK, LANES)) < HALF

    def put(rows, q, at, value):
        to = 2 * q * width + at
        low = (value << 16).astype(jnp.float32).astype(jnp.bfloat16)
        high = value.astype(jnp.float32).astype(jnp.bfloat16)
        g_ref[rows : rows + CHUNK, to : to + LANES] = low
        g_ref[rows : rows + CHUNK, to + width : to + width + LANES] = high

    for low, high, base, tiles, tail_row, start in levels:
        rows = [
            [
                jnp.broadcast_to(
                    table[step, pair : pair + 1, (base + k) * LANES : (base + k + 1) * LANES],
                    (CHUNK, LANES),
                )
                for k in range(tiles)
            ]
            for pair in (2 * half, 2 * half + 1)
        ]

        def gathered(idx, start_row):
            at = idx & (LANES - 1)
            inside = [idx >= k * LANES for k in range(tiles)]
            for q in range(2):
                if start is None:
                    value = jnp.zeros((CHUNK, LANES), jnp.int32)
                else:
                    value = start[2 * half + q, start_row : start_row + CHUNK, :]
                for k in range(tiles):
                    got = jnp.take_along_axis(rows[q][k], at, axis=1, mode="promise_in_bounds")
                    value = jnp.where(inside[k], got, value)
                yield q, value

        own = high - low
        for first in range(0, body_lanes, LANES):
            for target in range(low, high, CHUNK):
                idx = idx_ref[target : target + CHUNK, first : first + LANES]
                for q, value in gathered(idx, first // LANES * own + target - low):
                    put(target, q, first, value)
        upper = tail_rows(own)
        for target in range(low, low + upper, CHUNK):
            at = target - low
            idx = tail_ref[tail_row + at : tail_row + at + CHUNK, :]
            for q, value in gathered(idx, body_lanes // LANES * own + at):
                put(target, q, body_lanes, jnp.where(lower, value, 0))
                if target + upper < high:
                    moved = pltpu.roll(value, HALF, axis=1)
                    put(target + upper, q, body_lanes, jnp.where(lower, moved, 0))


def near_kernel(w_ref, f_ref, idx_ref, tail_ref, o_ref, table_f, table):
    step = pl.program_id(0)
    own, body_lanes = idx_ref.shape

    @pl.when(step == 0)
    def _():
        factor = jnp.exp2(13.0 - fine_power(w_ref))[0:1]
        table_f[...] = jnp.round(f_ref[0:LOCAL, :].astype(jnp.float32).T * factor)
        pack_rows(table_f, table, 0)

    rows = [jnp.broadcast_to(table[step, q : q + 1, :], (CHUNK, LANES)) for q in range(4)]

    def take(idx, to):
        at = idx & (LANES - 1)
        inside = idx >= 0
        for q in range(4):
            got = jnp.take_along_axis(rows[q], at, axis=1, mode="promise_in_bounds")
            o_ref[q, to : to + CHUNK, :] = jnp.where(inside, got, 0)

    for first in range(0, body_lanes, LANES):
        for target in range(0, own, CHUNK):
            take(
                idx_ref[target : target + CHUNK, first : first + LANES],
                first // LANES * own + target,
            )
    for at in range(0, tail_ref.shape[0], CHUNK):
        take(tail_ref[at : at + CHUNK, :], body_lanes // LANES * own + at)


def near_words(wanted, fine_rows, idx, tail):
    surface = fine_rows.shape[1]
    blocks = surface // 8
    rows = idx.shape[0] * (idx.shape[1] // LANES) + tail.shape[0]
    return pl.pallas_call(
        near_kernel,
        grid=(blocks,),
        in_specs=[whole(wanted), whole(fine_rows), whole(idx), whole(tail)],
        out_specs=pl.BlockSpec((None, 4, rows, LANES), lambda i: (i, 0, 0, 0)),
        out_shape=shape_of((blocks, 4, rows, LANES), jnp.int32),
        scratch_shapes=[
            pltpu.VMEM((surface, LANES), jnp.float32),
            pltpu.VMEM((blocks, 8, LANES), jnp.int32),
        ],
        compiler_params=pltpu.CompilerParams(vmem_limit_bytes=VMEM_BYTES),
        cost_estimate=pl.CostEstimate(
            flops=0, bytes_accessed=16 * blocks * rows * LANES, transcendentals=0
        ),
        name="near_words",
    )(wanted, fine_rows, idx, tail)


def multiply(acc, g_ref, mr):
    acc[...] += lax.dot_general(
        g_ref[...], mr, (((1,), (1,)), ((), ())), preferred_element_type=jnp.float32
    )


def tail_rows(own):
    return ceil_to(own // CHUNK, 2) // 2 * CHUNK


def translate_kernel(
    variants,
    coarse_tile,
    pick_ref,
    idx_ref,
    tail_ref,
    to_ref,
    f_ref,
    c_ref,
    arrived_any,
    w_ref,
    near_ref,
    m_ref,
    of_ref,
    oc_ref,
    rows_t,
    table_f,
    table,
    unit,
    arrived,
    stage,
    acc,
    mr_a,
    mr_b,
    g_a,
    g_b,
    sem,
):
    fine_own, targets = of_ref.shape[0], idx_ref.shape[0]
    step = pl.program_id(0)

    @pl.when(step == 0)
    def _():
        fetch = pltpu.make_async_copy(arrived_any, arrived, sem)
        fetch.start()
        for ref in (acc, mr_b, g_b):
            ref[...] = jnp.zeros_like(ref)
        fetch.wait()
        build_tables(
            ((0, coarse_tile), (coarse_tile, table_f.shape[0])),
            w_ref,
            to_ref,
            f_ref,
            c_ref,
            arrived,
            rows_t,
            table_f,
            table,
            unit,
        )

    def work(fine_tiles, coarse_tiles):
        levels = (
            (0, fine_own, 0, fine_tiles, 0, near_ref),
            (fine_own, targets, coarse_tile, coarse_tiles, tail_rows(fine_own), None),
        )
        stage_block(m_ref, stage)
        lay_half(0, stage, mr_a)
        multiply(acc, g_b, mr_b[...])
        gather_half(0, step, levels, idx_ref, tail_ref, table, g_a)
        lay_half(1, stage, mr_b)
        multiply(acc, g_a, mr_a[...])
        gather_half(1, step, levels, idx_ref, tail_ref, table, g_b)

    for at, tiles in enumerate(variants):
        pl.when(pick_ref[0] == at)(functools.partial(work, *tiles))

    @pl.when(step == pl.num_programs(0) - 1)
    def _():
        multiply(acc, g_b, mr_b[...])
        of_ref[...] = acc[0:fine_own, :] * unit[0, 0:1, 0:1]
        oc_ref[...] = acc[fine_own:targets, :] * (0.5 * unit[1, 0:1, 0:1])


def translate(
    pick,
    idx,
    tail,
    to,
    fine_rows,
    coarse_rows,
    arrived,
    wanted,
    near,
    m2l_ops,
    variants,
    coarse_tile,
    tiles,
):
    surface, _, offsets = m2l_ops.shape
    width = ceil_to(offsets, LANES)
    targets = idx.shape[0]
    fine_own, coarse_own = fine_rows.shape[0], coarse_rows.shape[0]
    blocks = surface // 8
    return pl.pallas_call(
        functools.partial(translate_kernel, variants, coarse_tile),
        grid=(blocks,),
        in_specs=[
            pl.BlockSpec(memory_space=pltpu.SMEM),
            whole(idx),
            whole(tail),
            whole(to),
            whole(fine_rows),
            whole(coarse_rows),
            pl.BlockSpec(memory_space=pl.ANY),
            whole(wanted),
            pl.BlockSpec((None,) + near.shape[1:], lambda i: (i, 0, 0, 0)),
            pl.BlockSpec((surface, 8, offsets), lambda i: (0, i, 0)),
        ],
        out_specs=[
            pl.BlockSpec((fine_own, surface), lambda i: (0, 0)),
            pl.BlockSpec((coarse_own, surface), lambda i: (0, 0)),
        ],
        out_shape=[
            shape_of((fine_own, surface), jnp.float32),
            shape_of((coarse_own, surface), jnp.float32),
        ],
        scratch_shapes=[
            pltpu.VMEM((surface, to.shape[0]), jnp.bfloat16),
            pltpu.VMEM((tiles, surface, LANES), jnp.float32),
            pltpu.VMEM((blocks, 8, tiles * LANES), jnp.int32),
            pltpu.VMEM((2, 8, LANES), jnp.float32),
            pltpu.VMEM(arrived.shape, jnp.bfloat16),
            pltpu.VMEM((width // LANES, ceil_to(STAGE_A * surface, 8), LANES), jnp.float32),
            pltpu.VMEM((targets, surface), jnp.float32),
            pltpu.VMEM((surface, 4 * width), jnp.bfloat16),
            pltpu.VMEM((surface, 4 * width), jnp.bfloat16),
            pltpu.VMEM((targets, 4 * width), jnp.bfloat16),
            pltpu.VMEM((targets, 4 * width), jnp.bfloat16),
            pltpu.SemaphoreType.DMA,
        ],
        compiler_params=pltpu.CompilerParams(vmem_limit_bytes=VMEM_BYTES),
        cost_estimate=pl.CostEstimate(
            flops=2 * surface * surface * targets * width,
            bytes_accessed=2 * surface * surface * width,
            transcendentals=0,
        ),
        name="translate",
    )(pick, idx, tail, to, fine_rows, coarse_rows, arrived, wanted, near, m2l_ops)


def exchange(x):
    return lax.all_to_all(x, AXES, split_axis=0, concat_axis=0, tiled=True)


def body(
    dens_fine, parent, child_code, m2m_ops, m2l_ops, ask_fine, list_fine, ask_coarse, list_coarse
):
    surface, fine_own = dens_fine.shape
    coarse_own = list_coarse.shape[0]
    asks_fine, asks_coarse = ask_fine[0].T, ask_coarse[0].T
    fine_cap, peers = asks_fine.shape
    coarse_cap = asks_coarse.shape[0]
    fine_rows = dens_fine.T
    wanted = exchange(join_asks(asks_fine, asks_coarse, fine_rows))

    fine_tiles = ceil_to(fine_own - LOCAL + (peers - 1) * fine_cap, LANES) // LANES
    coarse_tiles = ceil_to(coarse_own + (peers - 1) * coarse_cap, LANES) // LANES
    variants = [(min(n, fine_tiles), min(2, coarse_tiles)) for n in (2, 3)]
    variants = variants + [(fine_tiles, coarse_tiles)]
    idx, tail, to, pick, own_idx, own_tail = plan(
        asks_fine, asks_coarse, list_fine, list_coarse, variants, fine_tiles * LANES
    )

    positions = jnp.arange(8, dtype=jnp.int32)
    spread = jnp.where(
        (child_code[:, None] == positions[None, :])[:, :, None],
        fine_rows[:, None, :],
        jnp.zeros((), jnp.bfloat16),
    )
    child_terms = lax.dot_general(
        spread.reshape(fine_own, 8 * surface),
        m2m_ops.reshape(surface, 8 * surface),
        (((1,), (1,)), ((), ())),
        preferred_element_type=jnp.float32,
    )
    local_parent = parent - lax.axis_index(AXES) * coarse_own
    members = (jnp.arange(coarse_own, dtype=jnp.int32)[:, None] == local_parent[None, :]).astype(
        jnp.float32
    )
    coarse_rows = jnp.dot(members, child_terms, precision=lax.Precision.HIGHEST).astype(
        jnp.bfloat16
    )

    arrived = exchange(answer(wanted, fine_rows, coarse_rows))
    near = near_words(wanted, fine_rows, own_idx, own_tail)
    pot_fine, pot_coarse = translate(
        pick,
        idx,
        tail,
        to,
        fine_rows,
        coarse_rows,
        arrived,
        wanted,
        near,
        m2l_ops,
        variants,
        fine_tiles,
        fine_tiles + coarse_tiles,
    )
    return pot_fine.T, pot_coarse.T


def solution(mesh):
    return jax.shard_map(
        body,
        mesh=mesh,
        in_specs=(
            P(None, AXES),
            P(AXES),
            P(AXES),
            P(),
            P(),
            P(AXES, None, None),
            P(AXES, None),
            P(AXES, None, None),
            P(AXES, None),
        ),
        out_specs=(P(None, AXES), P(None, AXES)),
        check_vma=False,
    )
```

```python
import functools

import jax
import jax.numpy as jnp
from jax import lax
from jax.experimental import pallas as pl
from jax.experimental.pallas import tpu as pltpu
from jax.sharding import PartitionSpec as P

LANES = 128
CHUNK = 16
BLANK = -1
LOCAL = 0
AXES = ("leaf", "oct")
STAGE_A, STAGE_B = 23, 3
VMEM_BYTES = 56 << 20


def ceil_to(n, m):
    return (n + m - 1) // m * m


def lane_iota(shape):
    return lax.broadcasted_iota(jnp.int32, shape, 1)


def whole(x):
    return pl.BlockSpec(x.shape, lambda *i: (0,) * x.ndim)


def shape_of(shape, dtype):
    return jax.ShapeDtypeStruct(shape, dtype)


def asks_kernel(fine_own, f_ref, c_ref, o_ref, scr):
    fine_cap, peers = f_ref.shape
    coarse_cap = c_ref.shape[0]
    scr[...] = jnp.zeros_like(scr)
    scr[0:fine_cap, 0:peers] = f_ref[...]
    coarse = c_ref[...]
    scr[fine_cap : fine_cap + coarse_cap, 0:peers] = jnp.where(coarse < 0, -1, coarse + fine_own)
    o_ref[...] = scr[...].T[0:peers, 0 : fine_cap + coarse_cap]


def join_asks(asks_fine, asks_coarse, fine_own):
    peers = asks_fine.shape[1]
    slots = asks_fine.shape[0] + asks_coarse.shape[0]
    return pl.pallas_call(
        functools.partial(asks_kernel, fine_own),
        out_shape=shape_of((peers, slots), jnp.int32),
        scratch_shapes=[pltpu.VMEM((LANES, LANES), jnp.int32)],
        name="join_asks",
    )(asks_fine, asks_coarse)


def answer_kernel(w_ref, f_ref, c_any, o_ref, scr, hot, c_ref, sem):
    peers, slots = w_ref.shape
    own, surface = f_ref.shape[0] + c_ref.shape[0], f_ref.shape[1]
    fetch = pltpu.make_async_copy(c_any, c_ref, sem)
    fetch.start()
    scr[0:peers, 0:slots] = w_ref[...]
    columns = scr[...].T[0:slots, :]
    octant = lane_iota((slots, own))
    for e in range(0, peers, 2):
        picked = [
            jnp.broadcast_to(columns[:, d : d + 1], (slots, own)) == octant for d in (e, e + 1)
        ]
        both = jnp.concatenate([p.astype(jnp.float32) for p in picked], axis=0)
        hot[e * slots : (e + 2) * slots, :] = both.astype(jnp.bfloat16)
    fetch.wait()
    rows = jnp.concatenate([f_ref[...], c_ref[...]], axis=0)
    found = jnp.dot(hot[...], rows, preferred_element_type=jnp.float32)
    extra = surface - LANES
    rest = jnp.concatenate(
        [found[:, LANES:], jnp.zeros((peers * slots, LANES - extra), jnp.float32)], axis=1
    ).reshape(peers, slots, LANES)
    line = rest[:, 0:8].reshape(peers * 8, LANES)
    for g in range(1, slots // 8):
        part = rest[:, 8 * g : 8 * g + 8].reshape(peers * 8, LANES)
        line = line + pltpu.roll(part, g * extra, axis=1)
    o_ref[...] = jnp.concatenate(
        [found[:, 0:LANES].reshape(peers, slots, LANES), line.reshape(peers, 8, LANES)], axis=1
    ).astype(jnp.bfloat16)


def answer(wanted, fine_rows, coarse_rows):
    peers, slots = wanted.shape
    own = fine_rows.shape[0] + coarse_rows.shape[0]
    return pl.pallas_call(
        answer_kernel,
        in_specs=[whole(wanted), whole(fine_rows), pl.BlockSpec(memory_space=pl.ANY)],
        out_shape=shape_of((peers, slots + 8, LANES), jnp.bfloat16),
        scratch_shapes=[
            pltpu.VMEM((LANES, LANES), jnp.int32),
            pltpu.VMEM((peers * slots, own), jnp.bfloat16),
            pltpu.VMEM(coarse_rows.shape, jnp.bfloat16),
            pltpu.SemaphoreType.DMA,
        ],
        compiler_params=pltpu.CompilerParams(vmem_limit_bytes=16 << 20),
        name="answer",
    )(wanted, fine_rows, coarse_rows)


def remap(entries, own, done, cap, shift):
    slot = jnp.maximum(entries - own, 0)
    peer = slot // cap
    moved = jnp.take_along_axis(
        jnp.broadcast_to(shift, entries.shape), peer, axis=1, mode="promise_in_bounds"
    )
    column = jnp.where(entries < own, entries, entries - moved) - done
    return jnp.where(entries < done, BLANK, column)


def plan_kernel(
    variants,
    coarse_at,
    af_ref,
    ac_ref,
    lf_ref,
    lc_ref,
    idx_ref,
    to_ref,
    pick_ref,
    cnt,
):
    offsets = lf_ref.shape[1]
    body_lanes = offsets // LANES * LANES
    peers = af_ref.shape[1]
    lanes = lane_iota((LANES, LANES))
    earlier = lax.broadcasted_iota(jnp.int32, (LANES, LANES), 0) < lanes
    earlier = earlier.astype(jnp.float32).astype(jnp.bfloat16)
    levels = []
    row = 0
    cnt[...] = jnp.zeros_like(cnt)
    for level, (ask_ref, list_ref) in enumerate(((af_ref, lf_ref), (ac_ref, lc_ref))):
        own, cap = list_ref.shape[0], ask_ref.shape[0]
        done = LOCAL if level == 0 else 0
        valid = (ask_ref[...] >= 0).astype(jnp.float32)
        cnt[level, 0:1, 0:peers] = jnp.sum(valid, axis=0, keepdims=True)
        counts = cnt[level]
        before = jnp.dot(
            counts.astype(jnp.bfloat16), earlier, preferred_element_type=jnp.float32
        ).astype(jnp.int32)[0:1]
        total = jnp.sum(counts).astype(jnp.int32)
        counts = counts.astype(jnp.int32)[0:1]
        shift = lane_iota((1, LANES)) * cap - before
        levels.append((own, cap, counts, before, total))
        lists = [list_ref[:, first : first + LANES] for first in range(0, body_lanes, LANES)]
        lists.append(
            jnp.concatenate(
                [
                    list_ref[:, body_lanes:offsets],
                    jnp.full((own, LANES - (offsets - body_lanes)), -1, jnp.int32),
                ],
                axis=1,
            )
        )
        for k, x in enumerate(lists):
            idx_ref[row : row + own, k * LANES : (k + 1) * LANES] = remap(
                x, own, done, cap, shift
            )
        row += own

    (fine_own, fine_cap, *fine), (coarse_own, coarse_cap, *coarse) = levels
    place = lax.broadcasted_iota(jnp.int32, (8, LANES), 0)
    at = 0
    for level, base in (((fine_cap, *fine), fine_own - LOCAL), ((coarse_cap, *coarse), coarse_at + coarse_own)):
        cap, counts, before, _ = level
        for first in range(0, cap, 8):
            for e in range(peers):
                count = jnp.broadcast_to(counts[:, e : e + 1], (8, LANES))
                start = jnp.broadcast_to(before[:, e : e + 1], (8, LANES)) + base
                k = place + first
                to_ref[at : at + 8, :] = jnp.where(k < count, start + k, -1)
                at += 8
    octant = lax.broadcasted_iota(jnp.int32, (fine_own, LANES), 0)
    to_ref[at : at + fine_own, :] = jnp.maximum(octant - LOCAL, -1)
    octant = lax.broadcasted_iota(jnp.int32, (coarse_own, LANES), 0)
    to_ref[at + fine_own : at + row, :] = octant + coarse_at

    pick = jnp.int32(len(variants) - 1)
    for at in reversed(range(len(variants) - 1)):
        fits = (fine_own - LOCAL + fine[2] <= variants[at][0] * LANES) & (
            coarse_own + coarse[2] <= variants[at][1] * LANES
        )
        pick = jnp.where(fits, at, pick)
    pick_ref[0] = pick


def plan(asks_fine, asks_coarse, list_fine, list_coarse, variants, coarse_at):
    own = list_fine.shape[0] + list_coarse.shape[0]
    width = ceil_to(list_fine.shape[1], LANES)
    slots, peers = asks_fine.shape[0] + asks_coarse.shape[0], asks_fine.shape[1]
    vmem = pl.BlockSpec(memory_space=pltpu.VMEM)
    return pl.pallas_call(
        functools.partial(plan_kernel, variants, coarse_at),
        out_specs=[vmem, vmem, pl.BlockSpec(memory_space=pltpu.SMEM)],
        out_shape=[
            shape_of((own, width), jnp.int32),
            shape_of((own + peers * slots, LANES), jnp.int32),
            shape_of((1,), jnp.int32),
        ],
        scratch_shapes=[pltpu.VMEM((2, 8, LANES), jnp.float32)],
        compiler_params=pltpu.CompilerParams(vmem_limit_bytes=VMEM_BYTES),
        name="plan",
    )(asks_fine, asks_coarse, list_fine, list_coarse)


def pack_rows(values, table, tile):
    pairs = values.shape[0] // 2
    even = values[pl.ds(0, pairs, stride=2), :].astype(jnp.int32)
    odd = values[pl.ds(1, pairs, stride=2), :].astype(jnp.int32)
    both = odd * 65536 + even
    for block in range(pairs // 4):
        table[block, 0:4, tile * LANES : (tile + 1) * LANES] = both[4 * block : 4 * block + 4]


def scale_of(values):
    peak = jnp.max(jnp.max(jnp.abs(values), axis=0, keepdims=True), axis=1, keepdims=True)
    power = jnp.floor(jnp.log2(jnp.broadcast_to(jnp.maximum(peak, 1e-30), (8, LANES))))
    return jnp.exp2(13.0 - power)[0:1], jnp.exp2(power - 29.0)


def build_tables(ranges, to_ref, f_ref, c_ref, arrived, rows_t, table_f, table, unit):
    peers, lines, _ = arrived.shape
    surface = rows_t.shape[0]
    extra = surface - LANES
    came = arrived[...].astype(jnp.float32)
    rest = came[:, lines - 8 :].reshape(peers * 8, LANES).T
    at = 0
    for g in range(lines // 8 - 1):
        part = came[:, 8 * g : 8 * g + 8].reshape(peers * 8, LANES).T
        part = jnp.concatenate([part, rest[g * extra : (g + 1) * extra]], axis=0)
        rows_t[:, at : at + peers * 8] = part.astype(jnp.bfloat16)
        at += peers * 8
    own = jnp.concatenate([f_ref[...], c_ref[...]], axis=0).astype(jnp.float32)
    rows_t[:, at : at + own.shape[0]] = own.T.astype(jnp.bfloat16)
    to = to_ref[...]
    tiles = table_f.shape[0]
    lanes = lane_iota(to.shape)
    for k in range(0, tiles, 2):
        size = min(2, tiles - k)
        hot = [(to == lanes + (k + h) * LANES).astype(jnp.float32) for h in range(size)]
        hot = jnp.concatenate([x.astype(jnp.bfloat16) for x in hot], axis=1)
        columns = jnp.dot(rows_t[...], hot, preferred_element_type=jnp.float32)
        for h in range(size):
            table_f[k + h] = columns[:, h * LANES : (h + 1) * LANES]
    for level, (low, high) in enumerate(ranges):
        factor, unit[level] = scale_of(jnp.max(jnp.abs(table_f[low:high]), axis=0))
        for k in range(low, high):
            table_f[k] = jnp.round(table_f[k] * factor)
            pack_rows(table_f.at[k], table, k)


def stage_block(offsets, m_ref, stage):
    surface, _, width = m_ref.shape
    for tile, first in enumerate(range(0, width, LANES)):
        inside = lane_iota((8, LANES)) < offsets - first
        for a in range(surface):
            part = m_ref[a, :, first : first + LANES].astype(jnp.float32)
            if first + LANES > offsets:
                part = jnp.where(inside, part, 0.0)
            stage[tile, pl.ds(STAGE_A * a, 8, stride=STAGE_B), :] = part


def lay_half(half, stage, mr_ref):
    surface = mr_ref.shape[0]
    tiles = stage.shape[0]
    for j in range(4):
        for tile in range(tiles):
            rows = stage[tile, pl.ds(STAGE_B * (4 * half + j), surface, stride=STAGE_A), :]
            at = (j * tiles + tile) * LANES
            mr_ref[:, at : at + LANES] = rows.astype(jnp.bfloat16)


def gather_half(half, step, levels, idx_ref, table, g_ref):
    width = idx_ref.shape[1]
    for low, high, base, tiles in levels:
        rows = [
            [
                jnp.broadcast_to(
                    table[step, pair : pair + 1, (base + k) * LANES : (base + k + 1) * LANES],
                    (CHUNK, LANES),
                )
                for k in range(tiles)
            ]
            for pair in (2 * half, 2 * half + 1)
        ]
        for first in range(0, width, LANES):
            for target in range(low, high, CHUNK):
                idx = idx_ref[target : target + CHUNK, first : first + LANES]
                at = idx & (LANES - 1)
                inside = [idx >= k * LANES for k in range(tiles)]
                for q in range(2):
                    value = jnp.zeros((CHUNK, LANES), jnp.int32)
                    for k in range(tiles):
                        got = jnp.take_along_axis(rows[q][k], at, axis=1, mode="promise_in_bounds")
                        value = jnp.where(inside[k], got, value)
                    low_half = (value << 16).astype(jnp.float32).astype(jnp.bfloat16)
                    high_half = value.astype(jnp.float32).astype(jnp.bfloat16)
                    to = 2 * q * width + first
                    g_ref[target : target + CHUNK, to : to + LANES] = low_half
                    g_ref[target : target + CHUNK, to + width : to + width + LANES] = high_half


def multiply(acc, g_ref, mr):
    acc[...] += lax.dot_general(
        g_ref[...], mr, (((1,), (1,)), ((), ())), preferred_element_type=jnp.float32
    )


def translate_kernel(
    variants,
    coarse_tile,
    offsets,
    pick_ref,
    idx_ref,
    to_ref,
    f_ref,
    c_ref,
    arrived_any,
    m_ref,
    of_ref,
    oc_ref,
    rows_t,
    table_f,
    table,
    unit,
    arrived,
    stage,
    acc,
    mr_a,
    mr_b,
    g_a,
    g_b,
    sem,
):
    fine_own, targets = of_ref.shape[0], idx_ref.shape[0]
    step = pl.program_id(0)

    @pl.when(step == 0)
    def _():
        fetch = pltpu.make_async_copy(arrived_any, arrived, sem)
        fetch.start()
        for ref in (acc, mr_b, g_b):
            ref[...] = jnp.zeros_like(ref)
        fetch.wait()
        build_tables(
            ((0, coarse_tile), (coarse_tile, table_f.shape[0])),
            to_ref,
            f_ref,
            c_ref,
            arrived,
            rows_t,
            table_f,
            table,
            unit,
        )

    def work(fine_tiles, coarse_tiles):
        levels = (
            (0, fine_own, 0, fine_tiles),
            (fine_own, targets, coarse_tile, coarse_tiles),
        )
        stage_block(offsets, m_ref, stage)
        lay_half(0, stage, mr_a)
        multiply(acc, g_b, mr_b[...])
        gather_half(0, step, levels, idx_ref, table, g_a)
        lay_half(1, stage, mr_b)
        multiply(acc, g_a, mr_a[...])
        gather_half(1, step, levels, idx_ref, table, g_b)

    for at, tiles in enumerate(variants):
        pl.when(pick_ref[0] == at)(functools.partial(work, *tiles))

    @pl.when(step == pl.num_programs(0) - 1)
    def _():
        multiply(acc, g_b, mr_b[...])
        of_ref[...] = acc[0:fine_own, :] * unit[0, 0:1, 0:1]
        oc_ref[...] = acc[fine_own:targets, :] * (0.5 * unit[1, 0:1, 0:1])


def translate(
    pick, idx, to, fine_rows, coarse_rows, arrived, m2l_ops, variants, coarse_tile, tiles
):
    surface, _, offsets = m2l_ops.shape
    width = ceil_to(offsets, LANES)
    targets = idx.shape[0]
    fine_own, coarse_own = fine_rows.shape[0], coarse_rows.shape[0]
    blocks = surface // 8
    return pl.pallas_call(
        functools.partial(translate_kernel, variants, coarse_tile, offsets),
        grid=(blocks,),
        in_specs=[
            pl.BlockSpec(memory_space=pltpu.SMEM),
            whole(idx),
            whole(to),
            whole(fine_rows),
            whole(coarse_rows),
            pl.BlockSpec(memory_space=pl.ANY),
            pl.BlockSpec((surface, 8, width), lambda i: (0, i, 0)),
        ],
        out_specs=[
            pl.BlockSpec((fine_own, surface), lambda i: (0, 0)),
            pl.BlockSpec((coarse_own, surface), lambda i: (0, 0)),
        ],
        out_shape=[
            shape_of((fine_own, surface), jnp.float32),
            shape_of((coarse_own, surface), jnp.float32),
        ],
        scratch_shapes=[
            pltpu.VMEM((surface, to.shape[0]), jnp.bfloat16),
            pltpu.VMEM((tiles, surface, LANES), jnp.float32),
            pltpu.VMEM((blocks, 8, tiles * LANES), jnp.int32),
            pltpu.VMEM((2, 8, LANES), jnp.float32),
            pltpu.VMEM(arrived.shape, jnp.bfloat16),
            pltpu.VMEM((width // LANES, ceil_to(STAGE_A * surface, 8), LANES), jnp.float32),
            pltpu.VMEM((targets, surface), jnp.float32),
            pltpu.VMEM((surface, 4 * width), jnp.bfloat16),
            pltpu.VMEM((surface, 4 * width), jnp.bfloat16),
            pltpu.VMEM((targets, 4 * width), jnp.bfloat16),
            pltpu.VMEM((targets, 4 * width), jnp.bfloat16),
            pltpu.SemaphoreType.DMA,
        ],
        compiler_params=pltpu.CompilerParams(vmem_limit_bytes=VMEM_BYTES),
        cost_estimate=pl.CostEstimate(
            flops=2 * surface * surface * targets * width,
            bytes_accessed=2 * surface * surface * width,
            transcendentals=0,
        ),
        name="translate",
    )(pick, idx, to, fine_rows, coarse_rows, arrived, m2l_ops)


def exchange(x):
    return lax.all_to_all(x, AXES, split_axis=0, concat_axis=0, tiled=True)


def body(
    dens_fine, parent, child_code, m2m_ops, m2l_ops, ask_fine, list_fine, ask_coarse, list_coarse
):
    surface, fine_own = dens_fine.shape
    coarse_own = list_coarse.shape[0]
    asks_fine, asks_coarse = ask_fine[0].T, ask_coarse[0].T
    fine_cap, peers = asks_fine.shape
    coarse_cap = asks_coarse.shape[0]
    wanted = exchange(join_asks(asks_fine, asks_coarse, fine_own))

    fine_tiles = ceil_to(fine_own - LOCAL + (peers - 1) * fine_cap, LANES) // LANES
    coarse_tiles = ceil_to(coarse_own + (peers - 1) * coarse_cap, LANES) // LANES
    variants = [(min(n, fine_tiles), min(2, coarse_tiles)) for n in (3, 4)]
    variants = variants + [(fine_tiles, coarse_tiles)]
    idx, to, pick = plan(
        asks_fine, asks_coarse, list_fine, list_coarse, variants, fine_tiles * LANES
    )

    fine_rows = dens_fine.T
    positions = jnp.arange(8, dtype=jnp.int32)
    spread = jnp.where(
        (child_code[:, None] == positions[None, :])[:, :, None],
        fine_rows[:, None, :],
        jnp.zeros((), jnp.bfloat16),
    )
    child_terms = lax.dot_general(
        spread.reshape(fine_own, 8 * surface),
        m2m_ops.reshape(surface, 8 * surface),
        (((1,), (1,)), ((), ())),
        preferred_element_type=jnp.float32,
    )
    local_parent = parent - lax.axis_index(AXES) * coarse_own
    members = (jnp.arange(coarse_own, dtype=jnp.int32)[:, None] == local_parent[None, :]).astype(
        jnp.float32
    )
    coarse_rows = jnp.dot(members, child_terms, precision=lax.Precision.HIGHEST).astype(
        jnp.bfloat16
    )

    arrived = exchange(answer(wanted, fine_rows, coarse_rows))
    pot_fine, pot_coarse = translate(
        pick,
        idx,
        to,
        fine_rows,
        coarse_rows,
        arrived,
        m2l_ops,
        variants,
        fine_tiles,
        fine_tiles + coarse_tiles,
    )
    return pot_fine.T, pot_coarse.T


def solution(mesh):
    return jax.shard_map(
        body,
        mesh=mesh,
        in_specs=(
            P(None, AXES),
            P(AXES),
            P(AXES),
            P(),
            P(),
            P(AXES, None, None),
            P(AXES, None),
            P(AXES, None, None),
            P(AXES, None),
        ),
        out_specs=(P(None, AXES), P(None, AXES)),
        check_vma=False,
    )
```

```python
import functools

import jax
import jax.numpy as jnp
from jax import lax
from jax.experimental import pallas as pl
from jax.experimental.pallas import tpu as pltpu
from jax.sharding import PartitionSpec as P

LANES = 128
CHUNK = 16
BLANK = -1
LOCAL = 0
AXES = ("leaf", "oct")
STAGE_A, STAGE_B = 23, 3
VMEM_BYTES = 56 << 20


def ceil_to(n, m):
    return (n + m - 1) // m * m


def lane_iota(shape):
    return lax.broadcasted_iota(jnp.int32, shape, 1)


def whole(x):
    return pl.BlockSpec(x.shape, lambda *i: (0,) * x.ndim)


def shape_of(shape, dtype):
    return jax.ShapeDtypeStruct(shape, dtype)


def asks_kernel(fine_own, f_ref, c_ref, o_ref, scr):
    fine_cap, peers = f_ref.shape
    coarse_cap = c_ref.shape[0]
    scr[...] = jnp.zeros_like(scr)
    scr[0:fine_cap, 0:peers] = f_ref[...]
    coarse = c_ref[...]
    scr[fine_cap : fine_cap + coarse_cap, 0:peers] = jnp.where(coarse < 0, -1, coarse + fine_own)
    o_ref[...] = scr[...].T[0:peers, 0 : fine_cap + coarse_cap]


def join_asks(asks_fine, asks_coarse, fine_own):
    peers = asks_fine.shape[1]
    slots = asks_fine.shape[0] + asks_coarse.shape[0]
    return pl.pallas_call(
        functools.partial(asks_kernel, fine_own),
        out_shape=shape_of((peers, slots), jnp.int32),
        scratch_shapes=[pltpu.VMEM((LANES, LANES), jnp.int32)],
        name="join_asks",
    )(asks_fine, asks_coarse)


def answer_kernel(w_ref, f_ref, c_any, o_ref, scr, hot, c_ref, sem):
    peers, slots = w_ref.shape
    own, surface = f_ref.shape[0] + c_ref.shape[0], f_ref.shape[1]
    fetch = pltpu.make_async_copy(c_any, c_ref, sem)
    fetch.start()
    scr[0:peers, 0:slots] = w_ref[...]
    columns = scr[...].T[0:slots, :]
    octant = lane_iota((slots, own))
    for e in range(0, peers, 2):
        picked = [
            jnp.broadcast_to(columns[:, d : d + 1], (slots, own)) == octant for d in (e, e + 1)
        ]
        both = jnp.concatenate([p.astype(jnp.float32) for p in picked], axis=0)
        hot[e * slots : (e + 2) * slots, :] = both.astype(jnp.bfloat16)
    fetch.wait()
    rows = jnp.concatenate([f_ref[...], c_ref[...]], axis=0)
    found = jnp.dot(hot[...], rows, preferred_element_type=jnp.float32)
    extra = surface - LANES
    rest = jnp.concatenate(
        [found[:, LANES:], jnp.zeros((peers * slots, LANES - extra), jnp.float32)], axis=1
    ).reshape(peers, slots, LANES)
    line = rest[:, 0:8].reshape(peers * 8, LANES)
    for g in range(1, slots // 8):
        part = rest[:, 8 * g : 8 * g + 8].reshape(peers * 8, LANES)
        line = line + pltpu.roll(part, g * extra, axis=1)
    o_ref[...] = jnp.concatenate(
        [found[:, 0:LANES].reshape(peers, slots, LANES), line.reshape(peers, 8, LANES)], axis=1
    ).astype(jnp.bfloat16)


def answer(wanted, fine_rows, coarse_rows):
    peers, slots = wanted.shape
    own = fine_rows.shape[0] + coarse_rows.shape[0]
    return pl.pallas_call(
        answer_kernel,
        in_specs=[whole(wanted), whole(fine_rows), pl.BlockSpec(memory_space=pl.ANY)],
        out_shape=shape_of((peers, slots + 8, LANES), jnp.bfloat16),
        scratch_shapes=[
            pltpu.VMEM((LANES, LANES), jnp.int32),
            pltpu.VMEM((peers * slots, own), jnp.bfloat16),
            pltpu.VMEM(coarse_rows.shape, jnp.bfloat16),
            pltpu.SemaphoreType.DMA,
        ],
        compiler_params=pltpu.CompilerParams(vmem_limit_bytes=16 << 20),
        name="answer",
    )(wanted, fine_rows, coarse_rows)


def remap(entries, own, done, cap, shift):
    slot = jnp.maximum(entries - own, 0)
    peer = slot // cap
    moved = jnp.take_along_axis(
        jnp.broadcast_to(shift, entries.shape), peer, axis=1, mode="promise_in_bounds"
    )
    column = jnp.where(entries < own, entries, entries - moved) - done
    return jnp.where(entries < done, BLANK, column)


def plan_kernel(
    variants,
    coarse_at,
    af_ref,
    ac_ref,
    lf_ref,
    lc_ref,
    idx_ref,
    to_ref,
    pick_ref,
    cnt,
):
    offsets = lf_ref.shape[1]
    body_lanes = offsets // LANES * LANES
    peers = af_ref.shape[1]
    lanes = lane_iota((LANES, LANES))
    earlier = lax.broadcasted_iota(jnp.int32, (LANES, LANES), 0) < lanes
    earlier = earlier.astype(jnp.float32).astype(jnp.bfloat16)
    levels = []
    row = 0
    cnt[...] = jnp.zeros_like(cnt)
    for level, (ask_ref, list_ref) in enumerate(((af_ref, lf_ref), (ac_ref, lc_ref))):
        own, cap = list_ref.shape[0], ask_ref.shape[0]
        done = LOCAL if level == 0 else 0
        valid = (ask_ref[...] >= 0).astype(jnp.float32)
        cnt[level, 0:1, 0:peers] = jnp.sum(valid, axis=0, keepdims=True)
        counts = cnt[level]
        before = jnp.dot(
            counts.astype(jnp.bfloat16), earlier, preferred_element_type=jnp.float32
        ).astype(jnp.int32)[0:1]
        total = jnp.sum(counts).astype(jnp.int32)
        counts = counts.astype(jnp.int32)[0:1]
        shift = lane_iota((1, LANES)) * cap - before
        levels.append((own, cap, counts, before, total))
        lists = [list_ref[:, first : first + LANES] for first in range(0, body_lanes, LANES)]
        lists.append(
            jnp.concatenate(
                [
                    list_ref[:, body_lanes:offsets],
                    jnp.full((own, LANES - (offsets - body_lanes)), -1, jnp.int32),
                ],
                axis=1,
            )
        )
        for k, x in enumerate(lists):
            idx_ref[row : row + own, k * LANES : (k + 1) * LANES] = remap(
                x, own, done, cap, shift
            )
        row += own

    (fine_own, fine_cap, *fine), (coarse_own, coarse_cap, *coarse) = levels
    place = lax.broadcasted_iota(jnp.int32, (8, LANES), 0)
    at = 0
    for level, base in (((fine_cap, *fine), fine_own - LOCAL), ((coarse_cap, *coarse), coarse_at + coarse_own)):
        cap, counts, before, _ = level
        for first in range(0, cap, 8):
            for e in range(peers):
                count = jnp.broadcast_to(counts[:, e : e + 1], (8, LANES))
                start = jnp.broadcast_to(before[:, e : e + 1], (8, LANES)) + base
                k = place + first
                to_ref[at : at + 8, :] = jnp.where(k < count, start + k, -1)
                at += 8
    octant = lax.broadcasted_iota(jnp.int32, (fine_own, LANES), 0)
    to_ref[at : at + fine_own, :] = jnp.maximum(octant - LOCAL, -1)
    octant = lax.broadcasted_iota(jnp.int32, (coarse_own, LANES), 0)
    to_ref[at + fine_own : at + row, :] = octant + coarse_at

    pick = jnp.int32(len(variants) - 1)
    for at in reversed(range(len(variants) - 1)):
        fits = (fine_own - LOCAL + fine[2] <= variants[at][0] * LANES) & (
            coarse_own + coarse[2] <= variants[at][1] * LANES
        )
        pick = jnp.where(fits, at, pick)
    pick_ref[0] = pick


def plan(asks_fine, asks_coarse, list_fine, list_coarse, variants, coarse_at):
    own = list_fine.shape[0] + list_coarse.shape[0]
    width = ceil_to(list_fine.shape[1], LANES)
    slots, peers = asks_fine.shape[0] + asks_coarse.shape[0], asks_fine.shape[1]
    vmem = pl.BlockSpec(memory_space=pltpu.VMEM)
    return pl.pallas_call(
        functools.partial(plan_kernel, variants, coarse_at),
        out_specs=[vmem, vmem, pl.BlockSpec(memory_space=pltpu.SMEM)],
        out_shape=[
            shape_of((own, width), jnp.int32),
            shape_of((own + peers * slots, LANES), jnp.int32),
            shape_of((1,), jnp.int32),
        ],
        scratch_shapes=[pltpu.VMEM((2, 8, LANES), jnp.float32)],
        compiler_params=pltpu.CompilerParams(vmem_limit_bytes=VMEM_BYTES),
        name="plan",
    )(asks_fine, asks_coarse, list_fine, list_coarse)


def pack_rows(values, table, tile):
    pairs = values.shape[0] // 2
    even = values[pl.ds(0, pairs, stride=2), :].astype(jnp.int32)
    odd = values[pl.ds(1, pairs, stride=2), :].astype(jnp.int32)
    both = odd * 65536 + even
    for block in range(pairs // 4):
        table[block, 0:4, tile * LANES : (tile + 1) * LANES] = both[4 * block : 4 * block + 4]


def scale_of(values):
    peak = jnp.max(jnp.max(jnp.abs(values), axis=0, keepdims=True), axis=1, keepdims=True)
    power = jnp.floor(jnp.log2(jnp.broadcast_to(jnp.maximum(peak, 1e-30), (8, LANES))))
    return jnp.exp2(13.0 - power)[0:1], jnp.exp2(power - 29.0)


def build_tables(ranges, to_ref, f_ref, c_ref, arrived, rows_t, table_f, table, unit):
    peers, lines, _ = arrived.shape
    surface = rows_t.shape[0]
    extra = surface - LANES
    came = arrived[...].astype(jnp.float32)
    rest = came[:, lines - 8 :].reshape(peers * 8, LANES).T
    at = 0
    for g in range(lines // 8 - 1):
        part = came[:, 8 * g : 8 * g + 8].reshape(peers * 8, LANES).T
        part = jnp.concatenate([part, rest[g * extra : (g + 1) * extra]], axis=0)
        rows_t[:, at : at + peers * 8] = part.astype(jnp.bfloat16)
        at += peers * 8
    own = jnp.concatenate([f_ref[...], c_ref[...]], axis=0).astype(jnp.float32)
    rows_t[:, at : at + own.shape[0]] = own.T.astype(jnp.bfloat16)
    to = to_ref[...]
    tiles = table_f.shape[0]
    lanes = lane_iota(to.shape)
    for k in range(0, tiles, 2):
        size = min(2, tiles - k)
        hot = [(to == lanes + (k + h) * LANES).astype(jnp.float32) for h in range(size)]
        hot = jnp.concatenate([x.astype(jnp.bfloat16) for x in hot], axis=1)
        columns = jnp.dot(rows_t[...], hot, preferred_element_type=jnp.float32)
        for h in range(size):
            table_f[k + h] = columns[:, h * LANES : (h + 1) * LANES]
    for level, (low, high) in enumerate(ranges):
        factor, unit[level] = scale_of(jnp.max(jnp.abs(table_f[low:high]), axis=0))
        for k in range(low, high):
            table_f[k] = jnp.round(table_f[k] * factor)
            pack_rows(table_f.at[k], table, k)


def stage_block(offsets, m_ref, stage):
    surface, _, width = m_ref.shape
    for tile, first in enumerate(range(0, width, LANES)):
        inside = lane_iota((8, LANES)) < offsets - first
        for a in range(surface):
            part = m_ref[a, :, first : first + LANES].astype(jnp.float32)
            if first + LANES > offsets:
                part = jnp.where(inside, part, 0.0)
            stage[tile, pl.ds(STAGE_A * a, 8, stride=STAGE_B), :] = part


def lay_block(stage, mr_ref):
    surface = mr_ref.shape[0]
    tiles = stage.shape[0]
    for j in range(8):
        for tile in range(tiles):
            rows = stage[tile, pl.ds(STAGE_B * j, surface, stride=STAGE_A), :]
            at = (j * tiles + tile) * LANES
            mr_ref[:, at : at + LANES] = rows.astype(jnp.bfloat16)


def gather_block(step, levels, idx_ref, table, g_ref):
    width = idx_ref.shape[1]
    for low, high, base, tiles in levels:
        rows = [
            [
                jnp.broadcast_to(
                    table[step, q : q + 1, (base + k) * LANES : (base + k + 1) * LANES],
                    (8, LANES),
                )
                for k in range(tiles)
            ]
            for q in range(4)
        ]

        def words(target, first):
            idx = idx_ref[target : target + 8, first : first + LANES]
            at = idx & (LANES - 1)
            later = [idx >= k * LANES for k in range(1, tiles)]
            blank = idx < 0
            values = []
            for q in range(4):
                value = None
                for k in range(tiles):
                    got = jnp.take_along_axis(rows[q][k], at, axis=1, mode="promise_in_bounds")
                    value = got if k == 0 else jnp.where(later[k - 1], got, value)
                values.append(jnp.where(blank, 0, value))
            return values

        for first in range(0, width, LANES):
            for target in range(low, high, CHUNK):
                upper, lower = words(target, first), words(target + 8, first)
                for q in range(4):
                    value = jnp.concatenate([upper[q], lower[q]], axis=0)
                    low_half = (value << 16).astype(jnp.float32).astype(jnp.bfloat16)
                    high_half = value.astype(jnp.float32).astype(jnp.bfloat16)
                    to = 2 * q * width + first
                    g_ref[target : target + CHUNK, to : to + LANES] = low_half
                    g_ref[target : target + CHUNK, to + width : to + width + LANES] = high_half


def multiply(acc, g_ref, mr):
    acc[...] += lax.dot_general(
        g_ref[...], mr, (((1,), (1,)), ((), ())), preferred_element_type=jnp.float32
    )


def translate_kernel(
    variants,
    coarse_tile,
    offsets,
    pick_ref,
    idx_ref,
    to_ref,
    f_ref,
    c_ref,
    arrived_any,
    m_ref,
    of_ref,
    oc_ref,
    rows_t,
    table_f,
    table,
    unit,
    arrived,
    stage,
    acc,
    mr,
    g,
    sem,
):
    fine_own, targets = of_ref.shape[0], idx_ref.shape[0]
    step = pl.program_id(0)

    @pl.when(step == 0)
    def _():
        fetch = pltpu.make_async_copy(arrived_any, arrived, sem)
        fetch.start()
        for ref in (acc, mr, g):
            ref[...] = jnp.zeros_like(ref)
        fetch.wait()
        build_tables(
            ((0, coarse_tile), (coarse_tile, table_f.shape[0])),
            to_ref,
            f_ref,
            c_ref,
            arrived,
            rows_t,
            table_f,
            table,
            unit,
        )

    def work(fine_tiles, coarse_tiles):
        levels = (
            (0, fine_own, 0, fine_tiles),
            (fine_own, targets, coarse_tile, coarse_tiles),
        )
        multiply(acc, g, mr[...])
        stage_block(offsets, m_ref, stage)
        lay_block(stage, mr)
        gather_block(step, levels, idx_ref, table, g)

    for at, tiles in enumerate(variants):
        pl.when(pick_ref[0] == at)(functools.partial(work, *tiles))

    @pl.when(step == pl.num_programs(0) - 1)
    def _():
        multiply(acc, g, mr[...])
        of_ref[...] = acc[0:fine_own, :] * unit[0, 0:1, 0:1]
        oc_ref[...] = acc[fine_own:targets, :] * (0.5 * unit[1, 0:1, 0:1])


def translate(
    pick, idx, to, fine_rows, coarse_rows, arrived, m2l_ops, variants, coarse_tile, tiles
):
    surface, _, offsets = m2l_ops.shape
    width = ceil_to(offsets, LANES)
    targets = idx.shape[0]
    fine_own, coarse_own = fine_rows.shape[0], coarse_rows.shape[0]
    blocks = surface // 8
    return pl.pallas_call(
        functools.partial(translate_kernel, variants, coarse_tile, offsets),
        grid=(blocks,),
        in_specs=[
            pl.BlockSpec(memory_space=pltpu.SMEM),
            whole(idx),
            whole(to),
            whole(fine_rows),
            whole(coarse_rows),
            pl.BlockSpec(memory_space=pl.ANY),
            pl.BlockSpec((surface, 8, width), lambda i: (0, i, 0)),
        ],
        out_specs=[
            pl.BlockSpec((fine_own, surface), lambda i: (0, 0)),
            pl.BlockSpec((coarse_own, surface), lambda i: (0, 0)),
        ],
        out_shape=[
            shape_of((fine_own, surface), jnp.float32),
            shape_of((coarse_own, surface), jnp.float32),
        ],
        scratch_shapes=[
            pltpu.VMEM((surface, to.shape[0]), jnp.bfloat16),
            pltpu.VMEM((tiles, surface, LANES), jnp.float32),
            pltpu.VMEM((blocks, 8, tiles * LANES), jnp.int32),
            pltpu.VMEM((2, 8, LANES), jnp.float32),
            pltpu.VMEM(arrived.shape, jnp.bfloat16),
            pltpu.VMEM((width // LANES, ceil_to(STAGE_A * surface, 8), LANES), jnp.float32),
            pltpu.VMEM((targets, surface), jnp.float32),
            pltpu.VMEM((surface, 8 * width), jnp.bfloat16),
            pltpu.VMEM((targets, 8 * width), jnp.bfloat16),
            pltpu.SemaphoreType.DMA,
        ],
        compiler_params=pltpu.CompilerParams(vmem_limit_bytes=VMEM_BYTES),
        cost_estimate=pl.CostEstimate(
            flops=2 * surface * surface * targets * width,
            bytes_accessed=2 * surface * surface * width,
            transcendentals=0,
        ),
        name="translate",
    )(pick, idx, to, fine_rows, coarse_rows, arrived, m2l_ops)


def exchange(x):
    return lax.all_to_all(x, AXES, split_axis=0, concat_axis=0, tiled=True)


def body(
    dens_fine, parent, child_code, m2m_ops, m2l_ops, ask_fine, list_fine, ask_coarse, list_coarse
):
    surface, fine_own = dens_fine.shape
    coarse_own = list_coarse.shape[0]
    asks_fine, asks_coarse = ask_fine[0].T, ask_coarse[0].T
    fine_cap, peers = asks_fine.shape
    coarse_cap = asks_coarse.shape[0]
    wanted = exchange(join_asks(asks_fine, asks_coarse, fine_own))

    fine_tiles = ceil_to(fine_own - LOCAL + (peers - 1) * fine_cap, LANES) // LANES
    coarse_tiles = ceil_to(coarse_own + (peers - 1) * coarse_cap, LANES) // LANES
    variants = [(min(n, fine_tiles), min(2, coarse_tiles)) for n in (3, 4)]
    variants = variants + [(fine_tiles, coarse_tiles)]
    idx, to, pick = plan(
        asks_fine, asks_coarse, list_fine, list_coarse, variants, fine_tiles * LANES
    )

    fine_rows = dens_fine.T
    positions = jnp.arange(8, dtype=jnp.int32)
    spread = jnp.where(
        (child_code[:, None] == positions[None, :])[:, :, None],
        fine_rows[:, None, :],
        jnp.zeros((), jnp.bfloat16),
    )
    child_terms = lax.dot_general(
        spread.reshape(fine_own, 8 * surface),
        m2m_ops.reshape(surface, 8 * surface),
        (((1,), (1,)), ((), ())),
        preferred_element_type=jnp.float32,
    )
    local_parent = parent - lax.axis_index(AXES) * coarse_own
    members = (jnp.arange(coarse_own, dtype=jnp.int32)[:, None] == local_parent[None, :]).astype(
        jnp.float32
    )
    coarse_rows = jnp.dot(members, child_terms, precision=lax.Precision.HIGHEST).astype(
        jnp.bfloat16
    )

    arrived = exchange(answer(wanted, fine_rows, coarse_rows))
    pot_fine, pot_coarse = translate(
        pick,
        idx,
        to,
        fine_rows,
        coarse_rows,
        arrived,
        m2l_ops,
        variants,
        fine_tiles,
        fine_tiles + coarse_tiles,
    )
    return pot_fine.T, pot_coarse.T


def solution(mesh):
    return jax.shard_map(
        body,
        mesh=mesh,
        in_specs=(
            P(None, AXES),
            P(AXES),
            P(AXES),
            P(),
            P(),
            P(AXES, None, None),
            P(AXES, None),
            P(AXES, None, None),
            P(AXES, None),
        ),
        out_specs=(P(None, AXES), P(None, AXES)),
        check_vma=False,
    )
```

```python
import functools

import jax
import jax.numpy as jnp
from jax import lax
from jax.experimental import pallas as pl
from jax.experimental.pallas import tpu as pltpu
from jax.sharding import PartitionSpec as P

LANES = 128
CHUNK = 16
PAIRS = 8
BLANK = -1
LOCAL = 0
AXES = ("leaf", "oct")
STAGE_A, STAGE_B = 23, 3
VMEM_BYTES = 56 << 20


def ceil_to(n, m):
    return (n + m - 1) // m * m


def lane_iota(shape):
    return lax.broadcasted_iota(jnp.int32, shape, 1)


def whole(x):
    return pl.BlockSpec(x.shape, lambda *i: (0,) * x.ndim)


def shape_of(shape, dtype):
    return jax.ShapeDtypeStruct(shape, dtype)


def asks_kernel(fine_own, f_ref, c_ref, o_ref, scr):
    fine_cap, peers = f_ref.shape
    coarse_cap = c_ref.shape[0]
    scr[...] = jnp.zeros_like(scr)
    scr[0:fine_cap, 0:peers] = f_ref[...]
    coarse = c_ref[...]
    scr[fine_cap : fine_cap + coarse_cap, 0:peers] = jnp.where(coarse < 0, -1, coarse + fine_own)
    o_ref[...] = scr[...].T[0:peers, 0 : fine_cap + coarse_cap]


def join_asks(asks_fine, asks_coarse, fine_own):
    peers = asks_fine.shape[1]
    slots = asks_fine.shape[0] + asks_coarse.shape[0]
    return pl.pallas_call(
        functools.partial(asks_kernel, fine_own),
        out_shape=shape_of((peers, slots), jnp.int32),
        scratch_shapes=[pltpu.VMEM((LANES, LANES), jnp.int32)],
        name="join_asks",
    )(asks_fine, asks_coarse)


def answer_kernel(w_ref, own_ref, o_ref, scr, hot):
    peers, slots = w_ref.shape
    own, surface = own_ref.shape
    scr[0:peers, 0:slots] = w_ref[...]
    columns = scr[...].T[0:slots, :]
    octant = lane_iota((slots, own))
    for e in range(0, peers, 2):
        picked = [
            jnp.broadcast_to(columns[:, d : d + 1], (slots, own)) == octant for d in (e, e + 1)
        ]
        both = jnp.concatenate([p.astype(jnp.float32) for p in picked], axis=0)
        hot[e * slots : (e + 2) * slots, :] = both.astype(jnp.bfloat16)
    found = jnp.dot(hot[...], own_ref[...], preferred_element_type=jnp.float32)
    extra = surface - LANES
    rest = jnp.concatenate(
        [found[:, LANES:], jnp.zeros((peers * slots, LANES - extra), jnp.float32)], axis=1
    ).reshape(peers, slots, LANES)
    line = rest[:, 0:8].reshape(peers * 8, LANES)
    for g in range(1, slots // 8):
        part = rest[:, 8 * g : 8 * g + 8].reshape(peers * 8, LANES)
        line = line + pltpu.roll(part, g * extra, axis=1)
    o_ref[...] = jnp.concatenate(
        [found[:, 0:LANES].reshape(peers, slots, LANES), line.reshape(peers, 8, LANES)], axis=1
    ).astype(jnp.bfloat16)


def answer(wanted, own_rows):
    peers, slots = wanted.shape
    return pl.pallas_call(
        answer_kernel,
        out_shape=shape_of((peers, slots + 8, LANES), jnp.bfloat16),
        scratch_shapes=[
            pltpu.VMEM((LANES, LANES), jnp.int32),
            pltpu.VMEM((peers * slots, own_rows.shape[0]), jnp.bfloat16),
        ],
        compiler_params=pltpu.CompilerParams(vmem_limit_bytes=16 << 20),
        name="answer",
    )(wanted, own_rows)


def remap(entries, own, done, cap, shift):
    slot = jnp.maximum(entries - own, 0)
    peer = slot // cap
    moved = jnp.take_along_axis(
        jnp.broadcast_to(shift, entries.shape), peer, axis=1, mode="promise_in_bounds"
    )
    column = jnp.where(entries < own, entries, entries - moved) - done
    return jnp.where(entries < done, BLANK, column)


def plan_kernel(
    variants,
    coarse_at,
    af_ref,
    ac_ref,
    lf_ref,
    lc_ref,
    idx_ref,
    to_ref,
    pick_ref,
    cnt,
):
    offsets = lf_ref.shape[1]
    body_lanes = offsets // LANES * LANES
    peers = af_ref.shape[1]
    lanes = lane_iota((LANES, LANES))
    earlier = lax.broadcasted_iota(jnp.int32, (LANES, LANES), 0) < lanes
    earlier = earlier.astype(jnp.float32).astype(jnp.bfloat16)
    levels = []
    row = 0
    cnt[...] = jnp.zeros_like(cnt)
    for level, (ask_ref, list_ref) in enumerate(((af_ref, lf_ref), (ac_ref, lc_ref))):
        own, cap = list_ref.shape[0], ask_ref.shape[0]
        done = LOCAL if level == 0 else 0
        valid = (ask_ref[...] >= 0).astype(jnp.float32)
        cnt[level, 0:1, 0:peers] = jnp.sum(valid, axis=0, keepdims=True)
        counts = cnt[level]
        before = jnp.dot(
            counts.astype(jnp.bfloat16), earlier, preferred_element_type=jnp.float32
        ).astype(jnp.int32)[0:1]
        total = jnp.sum(counts).astype(jnp.int32)
        counts = counts.astype(jnp.int32)[0:1]
        shift = lane_iota((1, LANES)) * cap - before
        levels.append((own, cap, counts, before, total))
        lists = [list_ref[:, first : first + LANES] for first in range(0, body_lanes, LANES)]
        lists.append(
            jnp.concatenate(
                [
                    list_ref[:, body_lanes:offsets],
                    jnp.full((own, LANES - (offsets - body_lanes)), -1, jnp.int32),
                ],
                axis=1,
            )
        )
        for k, x in enumerate(lists):
            idx_ref[row : row + own, k * LANES : (k + 1) * LANES] = remap(
                x, own, done, cap, shift
            )
        row += own

    (fine_own, fine_cap, *fine), (coarse_own, coarse_cap, *coarse) = levels
    place = lax.broadcasted_iota(jnp.int32, (8, LANES), 0)
    at = 0
    for level, base in (((fine_cap, *fine), fine_own - LOCAL), ((coarse_cap, *coarse), coarse_at + coarse_own)):
        cap, counts, before, _ = level
        for first in range(0, cap, 8):
            for e in range(peers):
                count = jnp.broadcast_to(counts[:, e : e + 1], (8, LANES))
                start = jnp.broadcast_to(before[:, e : e + 1], (8, LANES)) + base
                k = place + first
                to_ref[at : at + 8, :] = jnp.where(k < count, start + k, -1)
                at += 8
    octant = lax.broadcasted_iota(jnp.int32, (fine_own, LANES), 0)
    to_ref[at : at + fine_own, :] = jnp.maximum(octant - LOCAL, -1)
    octant = lax.broadcasted_iota(jnp.int32, (coarse_own, LANES), 0)
    to_ref[at + fine_own : at + row, :] = octant + coarse_at

    pick = jnp.int32(len(variants) - 1)
    for at in reversed(range(len(variants) - 1)):
        fits = (fine_own - LOCAL + fine[2] <= variants[at][0] * LANES) & (
            coarse_own + coarse[2] <= variants[at][1] * LANES
        )
        pick = jnp.where(fits, at, pick)
    pick_ref[0] = pick


def plan(asks_fine, asks_coarse, list_fine, list_coarse, variants, coarse_at):
    own = list_fine.shape[0] + list_coarse.shape[0]
    width = ceil_to(list_fine.shape[1], LANES)
    slots, peers = asks_fine.shape[0] + asks_coarse.shape[0], asks_fine.shape[1]
    vmem = pl.BlockSpec(memory_space=pltpu.VMEM)
    return pl.pallas_call(
        functools.partial(plan_kernel, variants, coarse_at),
        out_specs=[vmem, vmem, pl.BlockSpec(memory_space=pltpu.SMEM)],
        out_shape=[
            shape_of((own, width), jnp.int32),
            shape_of((own + peers * slots, LANES), jnp.int32),
            shape_of((1,), jnp.int32),
        ],
        scratch_shapes=[pltpu.VMEM((2, 8, LANES), jnp.float32)],
        compiler_params=pltpu.CompilerParams(vmem_limit_bytes=VMEM_BYTES),
        name="plan",
    )(asks_fine, asks_coarse, list_fine, list_coarse)


def pack_rows(values, table, tile):
    pairs = values.shape[0] // 2
    even = values[pl.ds(0, pairs, stride=2), :].astype(jnp.int32)
    odd = values[pl.ds(1, pairs, stride=2), :].astype(jnp.int32)
    both = odd * 65536 + even
    for block in range(table.shape[0]):
        part = both[8 * block : 8 * block + 8]
        if part.shape[0] < 8:
            part = jnp.concatenate([part, jnp.zeros((8 - part.shape[0], LANES), jnp.int32)], axis=0)
        table[block, :, tile * LANES : (tile + 1) * LANES] = part


def scale_of(values):
    peak = jnp.max(jnp.max(jnp.abs(values), axis=0, keepdims=True), axis=1, keepdims=True)
    power = jnp.floor(jnp.log2(jnp.broadcast_to(jnp.maximum(peak, 1e-30), (8, LANES))))
    return jnp.exp2(13.0 - power)[0:1], jnp.exp2(power - 29.0)


def build_tables(ranges, to_ref, own_ref, arrived, rows_t, table_f, table, unit):
    peers, lines, _ = arrived.shape
    surface = rows_t.shape[0]
    extra = surface - LANES
    came = arrived[...].astype(jnp.float32)
    rest = came[:, lines - 8 :].reshape(peers * 8, LANES).T
    at = 0
    for g in range(lines // 8 - 1):
        part = came[:, 8 * g : 8 * g + 8].reshape(peers * 8, LANES).T
        part = jnp.concatenate([part, rest[g * extra : (g + 1) * extra]], axis=0)
        rows_t[:, at : at + peers * 8] = part.astype(jnp.bfloat16)
        at += peers * 8
    own = own_ref[...].astype(jnp.float32)
    rows_t[:, at : at + own.shape[0]] = own.T.astype(jnp.bfloat16)
    to = to_ref[...]
    tiles = table_f.shape[0]
    lanes = lane_iota(to.shape)
    for k in range(0, tiles, 2):
        size = min(2, tiles - k)
        hot = [(to == lanes + (k + h) * LANES).astype(jnp.float32) for h in range(size)]
        hot = jnp.concatenate([x.astype(jnp.bfloat16) for x in hot], axis=1)
        columns = jnp.dot(rows_t[...], hot, preferred_element_type=jnp.float32)
        for h in range(size):
            table_f[k + h] = columns[:, h * LANES : (h + 1) * LANES]
    for level, (low, high) in enumerate(ranges):
        factor, unit[level] = scale_of(jnp.max(jnp.abs(table_f[low:high]), axis=0))
        for k in range(low, high):
            table_f[k] = jnp.round(table_f[k] * factor)
            pack_rows(table_f.at[k], table, k)


def lay_block(surface, offsets, left, m_ref, stage, mr_ref):
    _, step_b, width = m_ref.shape
    tiles = width // LANES
    for group in range(0, step_b, 8):
        row = lax.broadcasted_iota(jnp.int32, (8, LANES), 0) + group
        for tile in range(tiles):
            inside = lane_iota((8, LANES)) < offsets - tile * LANES
            if group:
                inside = inside & (row < left)
            for a in range(surface):
                part = m_ref[a, group : group + 8, tile * LANES : (tile + 1) * LANES]
                part = part.astype(jnp.float32)
                if group or (tile + 1) * LANES > offsets:
                    part = jnp.where(inside, part, 0.0)
                stage[group // 8, tile, pl.ds(STAGE_A * a, 8, stride=STAGE_B), :] = part
        for j in range(8):
            for tile in range(tiles):
                rows = stage[group // 8, tile, pl.ds(STAGE_B * j, surface, stride=STAGE_A), :]
                at = ((group + j) * tiles + tile) * LANES
                mr_ref[:, at : at + LANES] = rows.astype(jnp.bfloat16)


def gather_block(step, levels, idx_ref, table, g_ref):
    width = idx_ref.shape[1]
    for low, high, base, tiles in levels:
        rows = [
            [
                jnp.broadcast_to(
                    table[step, q : q + 1, (base + k) * LANES : (base + k + 1) * LANES],
                    (8, LANES),
                )
                for k in range(tiles)
            ]
            for q in range(PAIRS)
        ]

        def words(target, first):
            idx = idx_ref[target : target + 8, first : first + LANES]
            at = idx & (LANES - 1)
            later = [idx >= k * LANES for k in range(1, tiles)]
            blank = idx < 0
            values = []
            for q in range(PAIRS):
                value = None
                for k in range(tiles):
                    got = jnp.take_along_axis(rows[q][k], at, axis=1, mode="promise_in_bounds")
                    value = got if k == 0 else jnp.where(later[k - 1], got, value)
                values.append(jnp.where(blank, 0, value))
            return values

        for first in range(0, width, LANES):
            for target in range(low, high, CHUNK):
                upper, lower = words(target, first), words(target + 8, first)
                for q in range(PAIRS):
                    value = jnp.concatenate([upper[q], lower[q]], axis=0)
                    low_half = (value << 16).astype(jnp.float32).astype(jnp.bfloat16)
                    high_half = value.astype(jnp.float32).astype(jnp.bfloat16)
                    to = 2 * q * width + first
                    g_ref[target : target + CHUNK, to : to + LANES] = low_half
                    g_ref[target : target + CHUNK, to + width : to + width + LANES] = high_half


def multiply(acc, g_ref, mr):
    acc[...] += lax.dot_general(
        g_ref[...], mr, (((1,), (1,)), ((), ())), preferred_element_type=jnp.float32
    )


def translate_kernel(
    variants,
    coarse_tile,
    offsets,
    pick_ref,
    idx_ref,
    to_ref,
    own_ref,
    arrived_any,
    m_ref,
    of_ref,
    oc_ref,
    rows_t,
    table_f,
    table,
    unit,
    arrived,
    stage,
    acc,
    mr,
    g,
    sem,
):
    fine_own, targets = of_ref.shape[0], idx_ref.shape[0]
    step = pl.program_id(0)

    @pl.when(step == 0)
    def _():
        fetch = pltpu.make_async_copy(arrived_any, arrived, sem)
        fetch.start()
        for ref in (acc, mr, g):
            ref[...] = jnp.zeros_like(ref)
        fetch.wait()
        build_tables(
            ((0, coarse_tile), (coarse_tile, table_f.shape[0])),
            to_ref,
            own_ref,
            arrived,
            rows_t,
            table_f,
            table,
            unit,
        )

    def work(fine_tiles, coarse_tiles):
        levels = (
            (0, fine_own, 0, fine_tiles),
            (fine_own, targets, coarse_tile, coarse_tiles),
        )
        multiply(acc, g, mr[...])
        surface = of_ref.shape[1]
        lay_block(surface, offsets, surface - step * 2 * PAIRS, m_ref, stage, mr)
        gather_block(step, levels, idx_ref, table, g)

    for at, tiles in enumerate(variants):
        pl.when(pick_ref[0] == at)(functools.partial(work, *tiles))

    @pl.when(step == pl.num_programs(0) - 1)
    def _():
        multiply(acc, g, mr[...])
        of_ref[...] = acc[0:fine_own, :] * unit[0, 0:1, 0:1]
        oc_ref[...] = acc[fine_own:targets, :] * (0.5 * unit[1, 0:1, 0:1])


def translate(
    pick, idx, to, own_rows, arrived, m2l_ops, variants, coarse_tile, tiles, fine_own
):
    surface, _, offsets = m2l_ops.shape
    width = ceil_to(offsets, LANES)
    targets = idx.shape[0]
    coarse_own = targets - fine_own
    blocks = pl.cdiv(surface, 2 * PAIRS)
    return pl.pallas_call(
        functools.partial(translate_kernel, variants, coarse_tile, offsets),
        grid=(blocks,),
        in_specs=[
            pl.BlockSpec(memory_space=pltpu.SMEM),
            whole(idx),
            whole(to),
            whole(own_rows),
            pl.BlockSpec(memory_space=pl.ANY),
            pl.BlockSpec((surface, 2 * PAIRS, width), lambda i: (0, i, 0)),
        ],
        out_specs=[
            pl.BlockSpec((fine_own, surface), lambda i: (0, 0)),
            pl.BlockSpec((coarse_own, surface), lambda i: (0, 0)),
        ],
        out_shape=[
            shape_of((fine_own, surface), jnp.float32),
            shape_of((coarse_own, surface), jnp.float32),
        ],
        scratch_shapes=[
            pltpu.VMEM((surface, to.shape[0]), jnp.bfloat16),
            pltpu.VMEM((tiles, surface, LANES), jnp.float32),
            pltpu.VMEM((blocks, 8, tiles * LANES), jnp.int32),
            pltpu.VMEM((2, 8, LANES), jnp.float32),
            pltpu.VMEM(arrived.shape, jnp.bfloat16),
            pltpu.VMEM(
                (PAIRS // 4, width // LANES, ceil_to(STAGE_A * surface, 8), LANES), jnp.float32
            ),
            pltpu.VMEM((targets, surface), jnp.float32),
            pltpu.VMEM((surface, 2 * PAIRS * width), jnp.bfloat16),
            pltpu.VMEM((targets, 2 * PAIRS * width), jnp.bfloat16),
            pltpu.SemaphoreType.DMA,
        ],
        compiler_params=pltpu.CompilerParams(vmem_limit_bytes=48 << 20),
        cost_estimate=pl.CostEstimate(
            flops=2 * surface * surface * targets * width,
            bytes_accessed=2 * surface * surface * width,
            transcendentals=0,
        ),
        name="translate",
    )(pick, idx, to, own_rows, arrived, m2l_ops)


def exchange(x):
    return lax.all_to_all(x, AXES, split_axis=0, concat_axis=0, tiled=True)


def body(
    dens_fine, parent, child_code, m2m_ops, m2l_ops, ask_fine, list_fine, ask_coarse, list_coarse
):
    surface, fine_own = dens_fine.shape
    coarse_own = list_coarse.shape[0]
    asks_fine, asks_coarse = ask_fine[0].T, ask_coarse[0].T
    fine_cap, peers = asks_fine.shape
    coarse_cap = asks_coarse.shape[0]
    wanted = exchange(join_asks(asks_fine, asks_coarse, fine_own))

    fine_tiles = ceil_to(fine_own - LOCAL + (peers - 1) * fine_cap, LANES) // LANES
    coarse_tiles = ceil_to(coarse_own + (peers - 1) * coarse_cap, LANES) // LANES
    variants = [(min(n, fine_tiles), min(2, coarse_tiles)) for n in (3, 4)]
    variants = variants + [(fine_tiles, coarse_tiles)]
    idx, to, pick = plan(
        asks_fine, asks_coarse, list_fine, list_coarse, variants, fine_tiles * LANES
    )

    fine_rows = dens_fine.T
    positions = jnp.arange(8, dtype=jnp.int32)
    spread = jnp.where(
        (child_code[:, None] == positions[None, :])[:, :, None],
        fine_rows[:, None, :],
        jnp.zeros((), jnp.bfloat16),
    )
    child_terms = lax.dot_general(
        spread.reshape(fine_own, 8 * surface),
        m2m_ops.reshape(surface, 8 * surface),
        (((1,), (1,)), ((), ())),
        preferred_element_type=jnp.float32,
    )
    local_parent = parent - lax.axis_index(AXES) * coarse_own
    members = (jnp.arange(coarse_own, dtype=jnp.int32)[:, None] == local_parent[None, :]).astype(
        jnp.float32
    )
    coarse_rows = jnp.dot(members, child_terms, precision=lax.Precision.HIGHEST).astype(
        jnp.bfloat16
    )

    own_rows = jnp.concatenate([fine_rows, coarse_rows], axis=0)
    arrived = exchange(answer(wanted, own_rows))
    pot_fine, pot_coarse = translate(
        pick,
        idx,
        to,
        own_rows,
        arrived,
        m2l_ops,
        variants,
        fine_tiles,
        fine_tiles + coarse_tiles,
        fine_own,
    )
    return pot_fine.T, pot_coarse.T


def solution(mesh):
    return jax.shard_map(
        body,
        mesh=mesh,
        in_specs=(
            P(None, AXES),
            P(AXES),
            P(AXES),
            P(),
            P(),
            P(AXES, None, None),
            P(AXES, None),
            P(AXES, None, None),
            P(AXES, None),
        ),
        out_specs=(P(None, AXES), P(None, AXES)),
        check_vma=False,
    )
```

```python
import functools

import jax
import jax.numpy as jnp
from jax import lax
from jax.experimental import pallas as pl
from jax.experimental.pallas import tpu as pltpu
from jax.sharding import PartitionSpec as P

LANES = 128
CHUNK = 16
PAIRS = 8
BLANK = -1
LOCAL = 0
AXES = ("leaf", "oct")
STAGE_A, STAGE_B = 23, 3
VMEM_BYTES = 48 << 20


def ceil_to(n, m):
    return (n + m - 1) // m * m


def lane_iota(shape):
    return lax.broadcasted_iota(jnp.int32, shape, 1)


def whole(x):
    return pl.BlockSpec(x.shape, lambda *i: (0,) * x.ndim)


def shape_of(shape, dtype):
    return jax.ShapeDtypeStruct(shape, dtype)


def asks_kernel(fine_own, f_ref, c_ref, o_ref, scr):
    fine_cap, peers = f_ref.shape
    coarse_cap = c_ref.shape[0]
    scr[...] = jnp.zeros_like(scr)
    scr[0:fine_cap, 0:peers] = f_ref[...]
    coarse = c_ref[...]
    scr[fine_cap : fine_cap + coarse_cap, 0:peers] = jnp.where(coarse < 0, -1, coarse + fine_own)
    o_ref[...] = scr[...].T[0:peers, 0 : fine_cap + coarse_cap]


def join_asks(asks_fine, asks_coarse, fine_own):
    peers = asks_fine.shape[1]
    slots = asks_fine.shape[0] + asks_coarse.shape[0]
    return pl.pallas_call(
        functools.partial(asks_kernel, fine_own),
        out_shape=shape_of((peers, slots), jnp.int32),
        scratch_shapes=[pltpu.VMEM((LANES, LANES), jnp.int32)],
        name="join_asks",
    )(asks_fine, asks_coarse)


def answer_kernel(w_ref, own_ref, o_ref, scr, hot):
    peers, slots = w_ref.shape
    own, surface = own_ref.shape
    scr[0:peers, 0:slots] = w_ref[...]
    columns = scr[...].T[0:slots, :]
    octant = lane_iota((slots, own))
    for e in range(0, peers, 2):
        picked = [
            jnp.broadcast_to(columns[:, d : d + 1], (slots, own)) == octant for d in (e, e + 1)
        ]
        both = jnp.concatenate([p.astype(jnp.float32) for p in picked], axis=0)
        hot[e * slots : (e + 2) * slots, :] = both.astype(jnp.bfloat16)
    found = jnp.dot(hot[...], own_ref[...], preferred_element_type=jnp.float32)
    extra = surface - LANES
    rest = jnp.concatenate(
        [found[:, LANES:], jnp.zeros((peers * slots, LANES - extra), jnp.float32)], axis=1
    ).reshape(peers, slots, LANES)
    line = rest[:, 0:8].reshape(peers * 8, LANES)
    for g in range(1, slots // 8):
        part = rest[:, 8 * g : 8 * g + 8].reshape(peers * 8, LANES)
        line = line + pltpu.roll(part, g * extra, axis=1)
    o_ref[...] = jnp.concatenate(
        [found[:, 0:LANES].reshape(peers, slots, LANES), line.reshape(peers, 8, LANES)], axis=1
    ).astype(jnp.bfloat16)


def answer(wanted, own_rows):
    peers, slots = wanted.shape
    return pl.pallas_call(
        answer_kernel,
        out_shape=shape_of((peers, slots + 8, LANES), jnp.bfloat16),
        scratch_shapes=[
            pltpu.VMEM((LANES, LANES), jnp.int32),
            pltpu.VMEM((peers * slots, own_rows.shape[0]), jnp.bfloat16),
        ],
        compiler_params=pltpu.CompilerParams(vmem_limit_bytes=16 << 20),
        name="answer",
    )(wanted, own_rows)


def remap(entries, own, done, cap, shift):
    slot = jnp.maximum(entries - own, 0)
    peer = slot // cap
    moved = jnp.take_along_axis(
        jnp.broadcast_to(shift, entries.shape), peer, axis=1, mode="promise_in_bounds"
    )
    column = jnp.where(entries < own, entries, entries - moved) - done
    return jnp.where(entries < done, BLANK, column)


def plan_kernel(
    variants,
    coarse_at,
    af_ref,
    ac_ref,
    lf_ref,
    lc_ref,
    idx_ref,
    to_ref,
    pick_ref,
    cnt,
):
    offsets = lf_ref.shape[1]
    body_lanes = offsets // LANES * LANES
    peers = af_ref.shape[1]
    lanes = lane_iota((LANES, LANES))
    earlier = lax.broadcasted_iota(jnp.int32, (LANES, LANES), 0) < lanes
    earlier = earlier.astype(jnp.float32).astype(jnp.bfloat16)
    levels = []
    row = 0
    cnt[...] = jnp.zeros_like(cnt)
    for level, (ask_ref, list_ref) in enumerate(((af_ref, lf_ref), (ac_ref, lc_ref))):
        own, cap = list_ref.shape[0], ask_ref.shape[0]
        done = LOCAL if level == 0 else 0
        valid = (ask_ref[...] >= 0).astype(jnp.float32)
        cnt[level, 0:1, 0:peers] = jnp.sum(valid, axis=0, keepdims=True)
        counts = cnt[level]
        before = jnp.dot(
            counts.astype(jnp.bfloat16), earlier, preferred_element_type=jnp.float32
        ).astype(jnp.int32)[0:1]
        total = jnp.sum(counts).astype(jnp.int32)
        counts = counts.astype(jnp.int32)[0:1]
        shift = lane_iota((1, LANES)) * cap - before
        levels.append((own, cap, counts, before, total))
        lists = [list_ref[:, first : first + LANES] for first in range(0, body_lanes, LANES)]
        lists.append(
            jnp.concatenate(
                [
                    list_ref[:, body_lanes:offsets],
                    jnp.full((own, LANES - (offsets - body_lanes)), -1, jnp.int32),
                ],
                axis=1,
            )
        )
        for k, x in enumerate(lists):
            idx_ref[row : row + own, k * LANES : (k + 1) * LANES] = remap(
                x, own, done, cap, shift
            )
        row += own

    (fine_own, fine_cap, *fine), (coarse_own, coarse_cap, *coarse) = levels
    place = lax.broadcasted_iota(jnp.int32, (8, LANES), 0)
    at = 0
    for level, base in (((fine_cap, *fine), fine_own - LOCAL), ((coarse_cap, *coarse), coarse_at + coarse_own)):
        cap, counts, before, _ = level
        for first in range(0, cap, 8):
            for e in range(peers):
                count = jnp.broadcast_to(counts[:, e : e + 1], (8, LANES))
                start = jnp.broadcast_to(before[:, e : e + 1], (8, LANES)) + base
                k = place + first
                to_ref[at : at + 8, :] = jnp.where(k < count, start + k, -1)
                at += 8
    octant = lax.broadcasted_iota(jnp.int32, (fine_own, LANES), 0)
    to_ref[at : at + fine_own, :] = jnp.maximum(octant - LOCAL, -1)
    octant = lax.broadcasted_iota(jnp.int32, (coarse_own, LANES), 0)
    to_ref[at + fine_own : at + row, :] = octant + coarse_at

    pick = jnp.int32(len(variants) - 1)
    for at in reversed(range(len(variants) - 1)):
        fits = (fine_own - LOCAL + fine[2] <= variants[at][0] * LANES) & (
            coarse_own + coarse[2] <= variants[at][1] * LANES
        )
        pick = jnp.where(fits, at, pick)
    pick_ref[0] = pick


def plan(asks_fine, asks_coarse, list_fine, list_coarse, variants, coarse_at):
    own = list_fine.shape[0] + list_coarse.shape[0]
    width = ceil_to(list_fine.shape[1], LANES)
    slots, peers = asks_fine.shape[0] + asks_coarse.shape[0], asks_fine.shape[1]
    vmem = pl.BlockSpec(memory_space=pltpu.VMEM)
    return pl.pallas_call(
        functools.partial(plan_kernel, variants, coarse_at),
        out_specs=[vmem, vmem, pl.BlockSpec(memory_space=pltpu.SMEM)],
        out_shape=[
            shape_of((own, width), jnp.int32),
            shape_of((own + peers * slots, LANES), jnp.int32),
            shape_of((1,), jnp.int32),
        ],
        scratch_shapes=[pltpu.VMEM((2, 8, LANES), jnp.float32)],
        compiler_params=pltpu.CompilerParams(vmem_limit_bytes=VMEM_BYTES),
        name="plan",
    )(asks_fine, asks_coarse, list_fine, list_coarse)


def pack_rows(values, table, tile):
    pairs = values.shape[0] // 2
    even = values[pl.ds(0, pairs, stride=2), :].astype(jnp.int32)
    odd = values[pl.ds(1, pairs, stride=2), :].astype(jnp.int32)
    both = odd * 65536 + even
    for block in range(table.shape[0]):
        part = both[8 * block : 8 * block + 8]
        if part.shape[0] < 8:
            part = jnp.concatenate([part, jnp.zeros((8 - part.shape[0], LANES), jnp.int32)], axis=0)
        table[block, :, tile * LANES : (tile + 1) * LANES] = part


def scale_of(values):
    peak = jnp.max(jnp.max(jnp.abs(values), axis=0, keepdims=True), axis=1, keepdims=True)
    power = jnp.floor(jnp.log2(jnp.broadcast_to(jnp.maximum(peak, 1e-30), (8, LANES))))
    return jnp.exp2(13.0 - power)[0:1], jnp.exp2(power - 29.0)


def build_tables(ranges, to_ref, own_ref, arrived, rows_t, table_f, table, unit):
    peers, lines, _ = arrived.shape
    surface = rows_t.shape[0]
    extra = surface - LANES
    came = arrived[...].astype(jnp.float32)
    rest = came[:, lines - 8 :].reshape(peers * 8, LANES).T
    at = 0
    for g in range(lines // 8 - 1):
        part = came[:, 8 * g : 8 * g + 8].reshape(peers * 8, LANES).T
        part = jnp.concatenate([part, rest[g * extra : (g + 1) * extra]], axis=0)
        rows_t[:, at : at + peers * 8] = part.astype(jnp.bfloat16)
        at += peers * 8
    own = own_ref[...].astype(jnp.float32)
    rows_t[:, at : at + own.shape[0]] = own.T.astype(jnp.bfloat16)
    to = to_ref[...]
    tiles = table_f.shape[0]
    lanes = lane_iota(to.shape)
    for k in range(0, tiles, 2):
        size = min(2, tiles - k)
        hot = [(to == lanes + (k + h) * LANES).astype(jnp.float32) for h in range(size)]
        hot = jnp.concatenate([x.astype(jnp.bfloat16) for x in hot], axis=1)
        columns = jnp.dot(rows_t[...], hot, preferred_element_type=jnp.float32)
        for h in range(size):
            table_f[k + h] = columns[:, h * LANES : (h + 1) * LANES]
    for level, (low, high) in enumerate(ranges):
        factor, unit[level] = scale_of(jnp.max(jnp.abs(table_f[low:high]), axis=0))
        for k in range(low, high):
            table_f[k] = jnp.round(table_f[k] * factor)
            pack_rows(table_f.at[k], table, k)


def lay_pieces(surface, offsets, left, m_ref, stage, mr_ref, slot):
    _, step_b, width = m_ref.shape
    tiles = width // LANES

    def spread(group, tile, first):
        inside = lane_iota((8, LANES)) < offsets - tile * LANES
        if group:
            row = lax.broadcasted_iota(jnp.int32, (8, LANES), 0) + group
            inside = inside & (row < left)
        for a in range(first, first + 19):
            part = m_ref[a, group : group + 8, tile * LANES : (tile + 1) * LANES]
            part = part.astype(jnp.float32)
            if group or (tile + 1) * LANES > offsets:
                part = jnp.where(inside, part, 0.0)
            stage[group // 8, tile, pl.ds(STAGE_A * a, 8, stride=STAGE_B), :] = part

    def lay(group, tile, j):
        rows = stage[group // 8, tile, pl.ds(STAGE_B * j, surface, stride=STAGE_A), :]
        at = ((group + j) * tiles + tile) * LANES
        mr_ref[slot, :, at : at + LANES] = rows.astype(jnp.bfloat16)

    for group in range(0, step_b, 8):
        for tile in range(tiles):
            for first in range(0, surface, 19):
                yield functools.partial(spread, group, tile, first)
            for j in range(8):
                yield functools.partial(lay, group, tile, j)


def product(acc, g_ref, mr_ref, slot, first, last):
    acc[...] += lax.dot_general(
        g_ref[slot, :, first:last],
        mr_ref[slot, :, first:last],
        (((1,), (1,)), ((), ())),
        preferred_element_type=jnp.float32,
    )


def gather_pieces(step, levels, idx_ref, table, g_ref, slot):
    width = idx_ref.shape[1]
    for low, high, base, tiles in levels:
        rows = [
            [
                jnp.broadcast_to(
                    table[step, q : q + 1, (base + k) * LANES : (base + k + 1) * LANES],
                    (8, LANES),
                )
                for k in range(tiles)
            ]
            for q in range(PAIRS)
        ]

        def words(rows, tiles, target, first):
            idx = idx_ref[target : target + 8, first : first + LANES]
            at = idx & (LANES - 1)
            later = [idx >= k * LANES for k in range(1, tiles)]
            blank = idx < 0
            values = []
            for q in range(PAIRS):
                value = None
                for k in range(tiles):
                    got = jnp.take_along_axis(rows[q][k], at, axis=1, mode="promise_in_bounds")
                    value = got if k == 0 else jnp.where(later[k - 1], got, value)
                values.append(jnp.where(blank, 0, value))
            return values

        def unit(rows, tiles, target, first):
            upper = words(rows, tiles, target, first)
            lower = words(rows, tiles, target + 8, first)
            for q in range(PAIRS):
                value = jnp.concatenate([upper[q], lower[q]], axis=0)
                low_half = (value << 16).astype(jnp.float32).astype(jnp.bfloat16)
                high_half = value.astype(jnp.float32).astype(jnp.bfloat16)
                to = 2 * q * width + first
                g_ref[slot, target : target + CHUNK, to : to + LANES] = low_half
                to = to + width
                g_ref[slot, target : target + CHUNK, to : to + LANES] = high_half

        for first in range(0, width, LANES):
            for target in range(low, high, CHUNK):
                yield functools.partial(unit, rows, tiles, target, first)


def interleave(main, others):
    done = [0] * len(others)
    for n, piece in enumerate(main):
        piece()
        for i, pieces in enumerate(others):
            until = (n + 1) * len(pieces) // len(main)
            for other in pieces[done[i] : until]:
                other()
            done[i] = until


def translate_kernel(
    variants,
    coarse_tile,
    offsets,
    pick_ref,
    idx_ref,
    to_ref,
    own_ref,
    arrived_any,
    m_ref,
    of_ref,
    oc_ref,
    rows_t,
    table_f,
    table,
    unit,
    arrived,
    stage,
    acc,
    mr,
    g,
    sem,
):
    fine_own, targets = of_ref.shape[0], idx_ref.shape[0]
    step = pl.program_id(0)
    now = lax.rem(step, 2)

    @pl.when(step == 0)
    def _():
        fetch = pltpu.make_async_copy(arrived_any, arrived, sem)
        fetch.start()
        fetch.wait()
        build_tables(
            ((0, coarse_tile), (coarse_tile, table_f.shape[0])),
            to_ref,
            own_ref,
            arrived,
            rows_t,
            table_f,
            table,
            unit,
        )

    def work(fine_tiles, coarse_tiles):
        levels = (
            (0, fine_own, 0, fine_tiles),
            (fine_own, targets, coarse_tile, coarse_tiles),
        )
        surface = of_ref.shape[1]
        depth = g.shape[2]
        parts = [
            functools.partial(product, acc, g, mr, 1 - now, first, first + depth // 4)
            for first in range(0, depth, depth // 4)
        ]
        left = surface - step * 2 * PAIRS
        interleave(
            list(gather_pieces(step, levels, idx_ref, table, g, now)),
            [list(lay_pieces(surface, offsets, left, m_ref, stage, mr, now)), parts],
        )

    for at, tiles in enumerate(variants):
        pl.when(pick_ref[0] == at)(functools.partial(work, *tiles))

    @pl.when(step == 0)
    def _():
        acc[...] = jnp.zeros_like(acc)

    @pl.when(step == pl.num_programs(0) - 1)
    def _():
        product(acc, g, mr, now, 0, g.shape[2])
        of_ref[...] = acc[0:fine_own, :] * unit[0, 0:1, 0:1]
        oc_ref[...] = acc[fine_own:targets, :] * (0.5 * unit[1, 0:1, 0:1])


def translate(
    pick, idx, to, own_rows, arrived, m2l_ops, variants, coarse_tile, tiles, fine_own
):
    surface, _, offsets = m2l_ops.shape
    width = ceil_to(offsets, LANES)
    targets = idx.shape[0]
    coarse_own = targets - fine_own
    blocks = pl.cdiv(surface, 2 * PAIRS)
    return pl.pallas_call(
        functools.partial(translate_kernel, variants, coarse_tile, offsets),
        grid=(blocks,),
        in_specs=[
            pl.BlockSpec(memory_space=pltpu.SMEM),
            whole(idx),
            whole(to),
            whole(own_rows),
            pl.BlockSpec(memory_space=pl.ANY),
            pl.BlockSpec((surface, 2 * PAIRS, width), lambda i: (0, i, 0)),
        ],
        out_specs=[
            pl.BlockSpec((fine_own, surface), lambda i: (0, 0)),
            pl.BlockSpec((coarse_own, surface), lambda i: (0, 0)),
        ],
        out_shape=[
            shape_of((fine_own, surface), jnp.float32),
            shape_of((coarse_own, surface), jnp.float32),
        ],
        scratch_shapes=[
            pltpu.VMEM((surface, to.shape[0]), jnp.bfloat16),
            pltpu.VMEM((tiles, surface, LANES), jnp.float32),
            pltpu.VMEM((blocks, 8, tiles * LANES), jnp.int32),
            pltpu.VMEM((2, 8, LANES), jnp.float32),
            pltpu.VMEM(arrived.shape, jnp.bfloat16),
            pltpu.VMEM(
                (PAIRS // 4, width // LANES, ceil_to(STAGE_A * surface, 8), LANES), jnp.float32
            ),
            pltpu.VMEM((targets, surface), jnp.float32),
            pltpu.VMEM((2, surface, 2 * PAIRS * width), jnp.bfloat16),
            pltpu.VMEM((2, targets, 2 * PAIRS * width), jnp.bfloat16),
            pltpu.SemaphoreType.DMA,
        ],
        compiler_params=pltpu.CompilerParams(vmem_limit_bytes=48 << 20),
        cost_estimate=pl.CostEstimate(
            flops=2 * surface * surface * targets * width,
            bytes_accessed=2 * surface * surface * width,
            transcendentals=0,
        ),
        name="translate",
    )(pick, idx, to, own_rows, arrived, m2l_ops)


def exchange(x):
    return lax.all_to_all(x, AXES, split_axis=0, concat_axis=0, tiled=True)


def body(
    dens_fine, parent, child_code, m2m_ops, m2l_ops, ask_fine, list_fine, ask_coarse, list_coarse
):
    surface, fine_own = dens_fine.shape
    coarse_own = list_coarse.shape[0]
    asks_fine, asks_coarse = ask_fine[0].T, ask_coarse[0].T
    fine_cap, peers = asks_fine.shape
    coarse_cap = asks_coarse.shape[0]
    wanted = exchange(join_asks(asks_fine, asks_coarse, fine_own))

    fine_tiles = ceil_to(fine_own - LOCAL + (peers - 1) * fine_cap, LANES) // LANES
    coarse_tiles = ceil_to(coarse_own + (peers - 1) * coarse_cap, LANES) // LANES
    variants = [(min(n, fine_tiles), min(2, coarse_tiles)) for n in (3, 4)]
    variants = variants + [(fine_tiles, coarse_tiles)]
    idx, to, pick = plan(
        asks_fine, asks_coarse, list_fine, list_coarse, variants, fine_tiles * LANES
    )

    fine_rows = dens_fine.T
    positions = jnp.arange(8, dtype=jnp.int32)
    spread = jnp.where(
        (child_code[:, None] == positions[None, :])[:, :, None],
        fine_rows[:, None, :],
        jnp.zeros((), jnp.bfloat16),
    )
    child_terms = lax.dot_general(
        spread.reshape(fine_own, 8 * surface),
        m2m_ops.reshape(surface, 8 * surface),
        (((1,), (1,)), ((), ())),
        preferred_element_type=jnp.float32,
    )
    local_parent = parent - lax.axis_index(AXES) * coarse_own
    members = (jnp.arange(coarse_own, dtype=jnp.int32)[:, None] == local_parent[None, :]).astype(
        jnp.float32
    )
    coarse_rows = jnp.dot(members, child_terms, precision=lax.Precision.HIGHEST).astype(
        jnp.bfloat16
    )

    own_rows = jnp.concatenate([fine_rows, coarse_rows], axis=0)
    arrived = exchange(answer(wanted, own_rows))
    pot_fine, pot_coarse = translate(
        pick,
        idx,
        to,
        own_rows,
        arrived,
        m2l_ops,
        variants,
        fine_tiles,
        fine_tiles + coarse_tiles,
        fine_own,
    )
    return pot_fine.T, pot_coarse.T


def solution(mesh):
    return jax.shard_map(
        body,
        mesh=mesh,
        in_specs=(
            P(None, AXES),
            P(AXES),
            P(AXES),
            P(),
            P(),
            P(AXES, None, None),
            P(AXES, None),
            P(AXES, None, None),
            P(AXES, None),
        ),
        out_specs=(P(None, AXES), P(None, AXES)),
        check_vma=False,
    )
```

```python
import functools

import jax
import jax.numpy as jnp
from jax import lax
from jax.experimental import pallas as pl
from jax.experimental.pallas import tpu as pltpu
from jax.sharding import PartitionSpec as P

LANES = 128
CHUNK = 16
PAIRS = 8
BLANK = -1
LOCAL = 0
AXES = ("leaf", "oct")
STAGE_A, STAGE_B = 23, 3
VMEM_BYTES = 48 << 20


def ceil_to(n, m):
    return (n + m - 1) // m * m


def lane_iota(shape):
    return lax.broadcasted_iota(jnp.int32, shape, 1)


def whole(x):
    return pl.BlockSpec(x.shape, lambda *i: (0,) * x.ndim)


def shape_of(shape, dtype):
    return jax.ShapeDtypeStruct(shape, dtype)


def asks_kernel(fine_own, f_ref, c_ref, o_ref, scr):
    fine_cap, peers = f_ref.shape
    coarse_cap = c_ref.shape[0]
    scr[...] = jnp.zeros_like(scr)
    scr[0:fine_cap, 0:peers] = f_ref[...]
    coarse = c_ref[...]
    scr[fine_cap : fine_cap + coarse_cap, 0:peers] = jnp.where(coarse < 0, -1, coarse + fine_own)
    o_ref[...] = scr[...].T[0:peers, 0 : fine_cap + coarse_cap]


def join_asks(asks_fine, asks_coarse, fine_own):
    peers = asks_fine.shape[1]
    slots = asks_fine.shape[0] + asks_coarse.shape[0]
    return pl.pallas_call(
        functools.partial(asks_kernel, fine_own),
        out_shape=shape_of((peers, slots), jnp.int32),
        scratch_shapes=[pltpu.VMEM((LANES, LANES), jnp.int32)],
        name="join_asks",
    )(asks_fine, asks_coarse)


def answer_kernel(w_ref, own_ref, o_ref, scr, hot):
    peers, slots = w_ref.shape
    own, surface = own_ref.shape
    scr[0:peers, 0:slots] = w_ref[...]
    columns = scr[...].T[0:slots, :]
    octant = lane_iota((slots, own))
    for e in range(0, peers, 2):
        picked = [
            jnp.broadcast_to(columns[:, d : d + 1], (slots, own)) == octant for d in (e, e + 1)
        ]
        both = jnp.concatenate([p.astype(jnp.float32) for p in picked], axis=0)
        hot[e * slots : (e + 2) * slots, :] = both.astype(jnp.bfloat16)
    found = jnp.dot(hot[...], own_ref[...], preferred_element_type=jnp.float32)
    extra = surface - LANES
    rest = jnp.concatenate(
        [found[:, LANES:], jnp.zeros((peers * slots, LANES - extra), jnp.float32)], axis=1
    ).reshape(peers, slots, LANES)
    line = rest[:, 0:8].reshape(peers * 8, LANES)
    for g in range(1, slots // 8):
        part = rest[:, 8 * g : 8 * g + 8].reshape(peers * 8, LANES)
        line = line + pltpu.roll(part, g * extra, axis=1)
    o_ref[...] = jnp.concatenate(
        [found[:, 0:LANES].reshape(peers, slots, LANES), line.reshape(peers, 8, LANES)], axis=1
    ).astype(jnp.bfloat16)


def answer(wanted, own_rows):
    peers, slots = wanted.shape
    return pl.pallas_call(
        answer_kernel,
        out_shape=shape_of((peers, slots + 8, LANES), jnp.bfloat16),
        scratch_shapes=[
            pltpu.VMEM((LANES, LANES), jnp.int32),
            pltpu.VMEM((peers * slots, own_rows.shape[0]), jnp.bfloat16),
        ],
        compiler_params=pltpu.CompilerParams(vmem_limit_bytes=16 << 20),
        name="answer",
    )(wanted, own_rows)


def remap(entries, own, done, cap, shift):
    slot = jnp.maximum(entries - own, 0)
    peer = slot // cap
    moved = jnp.take_along_axis(
        jnp.broadcast_to(shift, entries.shape), peer, axis=1, mode="promise_in_bounds"
    )
    column = jnp.where(entries < own, entries, entries - moved) - done
    return jnp.where(entries < done, BLANK, column)


def plan_kernel(
    variants,
    coarse_at,
    af_ref,
    ac_ref,
    lf_ref,
    lc_ref,
    idx_ref,
    to_ref,
    pick_ref,
    cnt,
):
    offsets = lf_ref.shape[1]
    body_lanes = offsets // LANES * LANES
    peers = af_ref.shape[1]
    lanes = lane_iota((LANES, LANES))
    earlier = lax.broadcasted_iota(jnp.int32, (LANES, LANES), 0) < lanes
    earlier = earlier.astype(jnp.float32).astype(jnp.bfloat16)
    levels = []
    row = 0
    cnt[...] = jnp.zeros_like(cnt)
    for level, (ask_ref, list_ref) in enumerate(((af_ref, lf_ref), (ac_ref, lc_ref))):
        own, cap = list_ref.shape[0], ask_ref.shape[0]
        done = LOCAL if level == 0 else 0
        valid = (ask_ref[...] >= 0).astype(jnp.float32)
        cnt[level, 0:1, 0:peers] = jnp.sum(valid, axis=0, keepdims=True)
        counts = cnt[level]
        before = jnp.dot(
            counts.astype(jnp.bfloat16), earlier, preferred_element_type=jnp.float32
        ).astype(jnp.int32)[0:1]
        total = jnp.sum(counts).astype(jnp.int32)
        counts = counts.astype(jnp.int32)[0:1]
        shift = lane_iota((1, LANES)) * cap - before
        levels.append((own, cap, counts, before, total))
        lists = [list_ref[:, first : first + LANES] for first in range(0, body_lanes, LANES)]
        lists.append(
            jnp.concatenate(
                [
                    list_ref[:, body_lanes:offsets],
                    jnp.full((own, LANES - (offsets - body_lanes)), -1, jnp.int32),
                ],
                axis=1,
            )
        )
        for k, x in enumerate(lists):
            idx_ref[row : row + own, k * LANES : (k + 1) * LANES] = remap(
                x, own, done, cap, shift
            )
        row += own

    (fine_own, fine_cap, *fine), (coarse_own, coarse_cap, *coarse) = levels
    place = lax.broadcasted_iota(jnp.int32, (8, LANES), 0)
    at = 0
    for level, base in (((fine_cap, *fine), fine_own - LOCAL), ((coarse_cap, *coarse), coarse_at + coarse_own)):
        cap, counts, before, _ = level
        for first in range(0, cap, 8):
            for e in range(peers):
                count = jnp.broadcast_to(counts[:, e : e + 1], (8, LANES))
                start = jnp.broadcast_to(before[:, e : e + 1], (8, LANES)) + base
                k = place + first
                to_ref[at : at + 8, :] = jnp.where(k < count, start + k, -1)
                at += 8
    octant = lax.broadcasted_iota(jnp.int32, (fine_own, LANES), 0)
    to_ref[at : at + fine_own, :] = jnp.maximum(octant - LOCAL, -1)
    octant = lax.broadcasted_iota(jnp.int32, (coarse_own, LANES), 0)
    to_ref[at + fine_own : at + row, :] = octant + coarse_at

    pick = jnp.int32(len(variants) - 1)
    for at in reversed(range(len(variants) - 1)):
        fits = (fine_own - LOCAL + fine[2] <= variants[at][0] * LANES) & (
            coarse_own + coarse[2] <= variants[at][1] * LANES
        )
        pick = jnp.where(fits, at, pick)
    pick_ref[0] = pick


def plan(asks_fine, asks_coarse, list_fine, list_coarse, variants, coarse_at):
    own = list_fine.shape[0] + list_coarse.shape[0]
    width = ceil_to(list_fine.shape[1], LANES)
    slots, peers = asks_fine.shape[0] + asks_coarse.shape[0], asks_fine.shape[1]
    vmem = pl.BlockSpec(memory_space=pltpu.VMEM)
    return pl.pallas_call(
        functools.partial(plan_kernel, variants, coarse_at),
        out_specs=[vmem, vmem, pl.BlockSpec(memory_space=pltpu.SMEM)],
        out_shape=[
            shape_of((own, width), jnp.int32),
            shape_of((own + peers * slots, LANES), jnp.int32),
            shape_of((1,), jnp.int32),
        ],
        scratch_shapes=[pltpu.VMEM((2, 8, LANES), jnp.float32)],
        compiler_params=pltpu.CompilerParams(vmem_limit_bytes=VMEM_BYTES),
        name="plan",
    )(asks_fine, asks_coarse, list_fine, list_coarse)


def pack_rows(values, table, tile):
    pairs = values.shape[0] // 2
    even = values[pl.ds(0, pairs, stride=2), :].astype(jnp.int32)
    odd = values[pl.ds(1, pairs, stride=2), :].astype(jnp.int32)
    both = odd * 65536 + even
    for block in range(table.shape[0]):
        part = both[8 * block : 8 * block + 8]
        if part.shape[0] < 8:
            part = jnp.concatenate([part, jnp.zeros((8 - part.shape[0], LANES), jnp.int32)], axis=0)
        table[block, :, tile * LANES : (tile + 1) * LANES] = part


def scale_of(values):
    peak = jnp.max(jnp.max(jnp.abs(values), axis=0, keepdims=True), axis=1, keepdims=True)
    power = jnp.floor(jnp.log2(jnp.broadcast_to(jnp.maximum(peak, 1e-30), (8, LANES))))
    return jnp.exp2(13.0 - power)[0:1], jnp.exp2(power - 29.0)


def build_tables(ranges, to_ref, own_ref, arrived, rows_t, table_f, table, unit):
    peers, lines, _ = arrived.shape
    surface = rows_t.shape[0]
    extra = surface - LANES
    came = arrived[...].astype(jnp.float32)
    rest = came[:, lines - 8 :].reshape(peers * 8, LANES).T
    at = 0
    for g in range(lines // 8 - 1):
        part = came[:, 8 * g : 8 * g + 8].reshape(peers * 8, LANES).T
        part = jnp.concatenate([part, rest[g * extra : (g + 1) * extra]], axis=0)
        rows_t[:, at : at + peers * 8] = part.astype(jnp.bfloat16)
        at += peers * 8
    own = own_ref[...].astype(jnp.float32)
    rows_t[:, at : at + own.shape[0]] = own.T.astype(jnp.bfloat16)
    to = to_ref[...]
    tiles = table_f.shape[0]
    lanes = lane_iota(to.shape)
    for k in range(0, tiles, 2):
        size = min(2, tiles - k)
        hot = [(to == lanes + (k + h) * LANES).astype(jnp.float32) for h in range(size)]
        hot = jnp.concatenate([x.astype(jnp.bfloat16) for x in hot], axis=1)
        columns = jnp.dot(rows_t[...], hot, preferred_element_type=jnp.float32)
        for h in range(size):
            table_f[k + h] = columns[:, h * LANES : (h + 1) * LANES]
    for level, (low, high) in enumerate(ranges):
        factor, unit[level] = scale_of(jnp.max(jnp.abs(table_f[low:high]), axis=0))
        for k in range(low, high):
            table_f[k] = jnp.round(table_f[k] * factor)
            pack_rows(table_f.at[k], table, k)


def lay_pieces(surface, offsets, left, m_ref, stage, mr_ref):
    _, step_b, width = m_ref.shape
    tiles = width // LANES

    def spread(group, tile, first):
        inside = lane_iota((8, LANES)) < offsets - tile * LANES
        if group:
            row = lax.broadcasted_iota(jnp.int32, (8, LANES), 0) + group
            inside = inside & (row < left)
        for a in range(first, first + 19):
            part = m_ref[a, group : group + 8, tile * LANES : (tile + 1) * LANES]
            part = part.astype(jnp.float32)
            if group or (tile + 1) * LANES > offsets:
                part = jnp.where(inside, part, 0.0)
            stage[group // 8, tile, pl.ds(STAGE_A * a, 8, stride=STAGE_B), :] = part

    def lay(group, tile, j):
        rows = stage[group // 8, tile, pl.ds(STAGE_B * j, surface, stride=STAGE_A), :]
        at = ((group + j) * tiles + tile) * LANES
        mr_ref[:, at : at + LANES] = rows.astype(jnp.bfloat16)

    for group in range(0, step_b, 8):
        for tile in range(tiles):
            for first in range(0, surface, 19):
                yield functools.partial(spread, group, tile, first)
            for j in range(8):
                yield functools.partial(lay, group, tile, j)


def product(acc, g_ref, mr_ref):
    acc[...] += lax.dot_general(
        g_ref[...],
        mr_ref[...],
        (((1,), (1,)), ((), ())),
        preferred_element_type=jnp.float32,
    )


def gather_pieces(step, levels, idx_ref, table, g_ref):
    width = idx_ref.shape[1]
    for low, high, base, tiles in levels:
        rows = [
            [
                jnp.broadcast_to(
                    table[step, q : q + 1, (base + k) * LANES : (base + k + 1) * LANES],
                    (8, LANES),
                )
                for k in range(tiles)
            ]
            for q in range(PAIRS)
        ]

        def words(rows, tiles, target, first):
            idx = idx_ref[target : target + 8, first : first + LANES]
            at = idx & (LANES - 1)
            later = [idx >= k * LANES for k in range(1, tiles)]
            blank = idx < 0
            values = []
            for q in range(PAIRS):
                value = None
                for k in range(tiles):
                    got = jnp.take_along_axis(rows[q][k], at, axis=1, mode="promise_in_bounds")
                    value = got if k == 0 else jnp.where(later[k - 1], got, value)
                values.append(jnp.where(blank, 0, value))
            return values

        def unit(rows, tiles, target, first):
            upper = words(rows, tiles, target, first)
            lower = words(rows, tiles, target + 8, first)
            for q in range(PAIRS):
                value = jnp.concatenate([upper[q], lower[q]], axis=0)
                low_half = (value << 16).astype(jnp.float32).astype(jnp.bfloat16)
                high_half = value.astype(jnp.float32).astype(jnp.bfloat16)
                to = 2 * q * width + first
                g_ref[target : target + CHUNK, to : to + LANES] = low_half
                to = to + width
                g_ref[target : target + CHUNK, to : to + LANES] = high_half

        for first in range(0, width, LANES):
            for target in range(low, high, CHUNK):
                yield functools.partial(unit, rows, tiles, target, first)


def interleave(main, others):
    done = 0
    for n, piece in enumerate(main):
        piece()
        until = (n + 1) * len(others) // len(main)
        for other in others[done:until]:
            other()
        done = until


def translate_kernel(
    variants,
    coarse_tile,
    offsets,
    pick_ref,
    idx_ref,
    to_ref,
    own_ref,
    arrived_any,
    m_ref,
    of_ref,
    oc_ref,
    rows_t,
    table_f,
    table,
    unit,
    arrived,
    stage,
    acc,
    mr,
    g,
    sem,
):
    fine_own, targets = of_ref.shape[0], idx_ref.shape[0]
    step = pl.program_id(0)

    @pl.when(step == 0)
    def _():
        fetch = pltpu.make_async_copy(arrived_any, arrived, sem)
        fetch.start()
        fetch.wait()
        build_tables(
            ((0, coarse_tile), (coarse_tile, table_f.shape[0])),
            to_ref,
            own_ref,
            arrived,
            rows_t,
            table_f,
            table,
            unit,
        )

    def work(fine_tiles, coarse_tiles):
        levels = (
            (0, fine_own, 0, fine_tiles),
            (fine_own, targets, coarse_tile, coarse_tiles),
        )
        surface = of_ref.shape[1]
        left = surface - step * 2 * PAIRS
        product(acc, g, mr)
        interleave(
            list(gather_pieces(step, levels, idx_ref, table, g)),
            list(lay_pieces(surface, offsets, left, m_ref, stage, mr)),
        )

    for at, tiles in enumerate(variants):
        pl.when(pick_ref[0] == at)(functools.partial(work, *tiles))

    @pl.when(step == 0)
    def _():
        acc[...] = jnp.zeros_like(acc)

    @pl.when(step == pl.num_programs(0) - 1)
    def _():
        product(acc, g, mr)
        of_ref[...] = acc[0:fine_own, :] * unit[0, 0:1, 0:1]
        oc_ref[...] = acc[fine_own:targets, :] * (0.5 * unit[1, 0:1, 0:1])


def translate(
    pick, idx, to, own_rows, arrived, m2l_ops, variants, coarse_tile, tiles, fine_own
):
    surface, _, offsets = m2l_ops.shape
    width = ceil_to(offsets, LANES)
    targets = idx.shape[0]
    coarse_own = targets - fine_own
    blocks = pl.cdiv(surface, 2 * PAIRS)
    return pl.pallas_call(
        functools.partial(translate_kernel, variants, coarse_tile, offsets),
        grid=(blocks,),
        in_specs=[
            pl.BlockSpec(memory_space=pltpu.SMEM),
            whole(idx),
            whole(to),
            whole(own_rows),
            pl.BlockSpec(memory_space=pl.ANY),
            pl.BlockSpec((surface, 2 * PAIRS, width), lambda i: (0, i, 0)),
        ],
        out_specs=[
            pl.BlockSpec((fine_own, surface), lambda i: (0, 0)),
            pl.BlockSpec((coarse_own, surface), lambda i: (0, 0)),
        ],
        out_shape=[
            shape_of((fine_own, surface), jnp.float32),
            shape_of((coarse_own, surface), jnp.float32),
        ],
        scratch_shapes=[
            pltpu.VMEM((surface, to.shape[0]), jnp.bfloat16),
            pltpu.VMEM((tiles, surface, LANES), jnp.float32),
            pltpu.VMEM((blocks, 8, tiles * LANES), jnp.int32),
            pltpu.VMEM((2, 8, LANES), jnp.float32),
            pltpu.VMEM(arrived.shape, jnp.bfloat16),
            pltpu.VMEM(
                (PAIRS // 4, width // LANES, ceil_to(STAGE_A * surface, 8), LANES), jnp.float32
            ),
            pltpu.VMEM((targets, surface), jnp.float32),
            pltpu.VMEM((surface, 2 * PAIRS * width), jnp.bfloat16),
            pltpu.VMEM((targets, 2 * PAIRS * width), jnp.bfloat16),
            pltpu.SemaphoreType.DMA,
        ],
        compiler_params=pltpu.CompilerParams(vmem_limit_bytes=48 << 20),
        cost_estimate=pl.CostEstimate(
            flops=2 * surface * surface * targets * width,
            bytes_accessed=2 * surface * surface * width,
            transcendentals=0,
        ),
        name="translate",
    )(pick, idx, to, own_rows, arrived, m2l_ops)


def exchange(x):
    return lax.all_to_all(x, AXES, split_axis=0, concat_axis=0, tiled=True)


def body(
    dens_fine, parent, child_code, m2m_ops, m2l_ops, ask_fine, list_fine, ask_coarse, list_coarse
):
    surface, fine_own = dens_fine.shape
    coarse_own = list_coarse.shape[0]
    asks_fine, asks_coarse = ask_fine[0].T, ask_coarse[0].T
    fine_cap, peers = asks_fine.shape
    coarse_cap = asks_coarse.shape[0]
    wanted = exchange(join_asks(asks_fine, asks_coarse, fine_own))

    fine_tiles = ceil_to(fine_own - LOCAL + (peers - 1) * fine_cap, LANES) // LANES
    coarse_tiles = ceil_to(coarse_own + (peers - 1) * coarse_cap, LANES) // LANES
    variants = [(min(n, fine_tiles), min(2, coarse_tiles)) for n in (3, 4)]
    variants = variants + [(fine_tiles, coarse_tiles)]
    idx, to, pick = plan(
        asks_fine, asks_coarse, list_fine, list_coarse, variants, fine_tiles * LANES
    )

    fine_rows = dens_fine.T
    positions = jnp.arange(8, dtype=jnp.int32)
    spread = jnp.where(
        (child_code[:, None] == positions[None, :])[:, :, None],
        fine_rows[:, None, :],
        jnp.zeros((), jnp.bfloat16),
    )
    child_terms = lax.dot_general(
        spread.reshape(fine_own, 8 * surface),
        m2m_ops.reshape(surface, 8 * surface),
        (((1,), (1,)), ((), ())),
        preferred_element_type=jnp.float32,
    )
    local_parent = parent - lax.axis_index(AXES) * coarse_own
    members = (jnp.arange(coarse_own, dtype=jnp.int32)[:, None] == local_parent[None, :]).astype(
        jnp.float32
    )
    coarse_rows = jnp.dot(members, child_terms, precision=lax.Precision.HIGHEST).astype(
        jnp.bfloat16
    )

    own_rows = jnp.concatenate([fine_rows, coarse_rows], axis=0)
    arrived = exchange(answer(wanted, own_rows))
    pot_fine, pot_coarse = translate(
        pick,
        idx,
        to,
        own_rows,
        arrived,
        m2l_ops,
        variants,
        fine_tiles,
        fine_tiles + coarse_tiles,
        fine_own,
    )
    return pot_fine.T, pot_coarse.T


def solution(mesh):
    return jax.shard_map(
        body,
        mesh=mesh,
        in_specs=(
            P(None, AXES),
            P(AXES),
            P(AXES),
            P(),
            P(),
            P(AXES, None, None),
            P(AXES, None),
            P(AXES, None, None),
            P(AXES, None),
        ),
        out_specs=(P(None, AXES), P(None, AXES)),
        check_vma=False,
    )
```

```python
import functools

import jax
import jax.numpy as jnp
from jax import lax
from jax.experimental import pallas as pl
from jax.experimental.pallas import tpu as pltpu
from jax.sharding import PartitionSpec as P

LANES = 128
CHUNK = 16
PAIRS = 8
BLANK = -1
LOCAL = 0
AXES = ("leaf", "oct")
STAGE_A, STAGE_B = 23, 3
VMEM_BYTES = 48 << 20


def ceil_to(n, m):
    return (n + m - 1) // m * m


def lane_iota(shape):
    return lax.broadcasted_iota(jnp.int32, shape, 1)


def whole(x):
    return pl.BlockSpec(x.shape, lambda *i: (0,) * x.ndim)


def shape_of(shape, dtype):
    return jax.ShapeDtypeStruct(shape, dtype)


def asks_kernel(fine_own, f_ref, c_ref, o_ref, scr):
    fine_cap, peers = f_ref.shape
    coarse_cap = c_ref.shape[0]
    scr[...] = jnp.zeros_like(scr)
    scr[0:fine_cap, 0:peers] = f_ref[...]
    coarse = c_ref[...]
    scr[fine_cap : fine_cap + coarse_cap, 0:peers] = jnp.where(coarse < 0, -1, coarse + fine_own)
    o_ref[...] = scr[...].T[0:peers, 0 : fine_cap + coarse_cap]


def join_asks(asks_fine, asks_coarse, fine_own):
    peers = asks_fine.shape[1]
    slots = asks_fine.shape[0] + asks_coarse.shape[0]
    return pl.pallas_call(
        functools.partial(asks_kernel, fine_own),
        out_shape=shape_of((peers, slots), jnp.int32),
        scratch_shapes=[pltpu.VMEM((LANES, LANES), jnp.int32)],
        name="join_asks",
    )(asks_fine, asks_coarse)


def answer_kernel(w_ref, own_ref, o_ref, scr, hot):
    peers, slots = w_ref.shape
    own, surface = own_ref.shape
    scr[0:peers, 0:slots] = w_ref[...]
    columns = scr[...].T[0:slots, :]
    octant = lane_iota((slots, own))
    for e in range(0, peers, 2):
        picked = [
            jnp.broadcast_to(columns[:, d : d + 1], (slots, own)) == octant for d in (e, e + 1)
        ]
        both = jnp.concatenate([p.astype(jnp.float32) for p in picked], axis=0)
        hot[e * slots : (e + 2) * slots, :] = both.astype(jnp.bfloat16)
    found = jnp.dot(hot[...], own_ref[...], preferred_element_type=jnp.float32)
    extra = surface - LANES
    rest = jnp.concatenate(
        [found[:, LANES:], jnp.zeros((peers * slots, LANES - extra), jnp.float32)], axis=1
    ).reshape(peers, slots, LANES)
    line = rest[:, 0:8].reshape(peers * 8, LANES)
    for g in range(1, slots // 8):
        part = rest[:, 8 * g : 8 * g + 8].reshape(peers * 8, LANES)
        line = line + pltpu.roll(part, g * extra, axis=1)
    o_ref[...] = jnp.concatenate(
        [found[:, 0:LANES].reshape(peers, slots, LANES), line.reshape(peers, 8, LANES)], axis=1
    ).astype(jnp.bfloat16)


def answer(wanted, own_rows):
    peers, slots = wanted.shape
    return pl.pallas_call(
        answer_kernel,
        out_shape=shape_of((peers, slots + 8, LANES), jnp.bfloat16),
        scratch_shapes=[
            pltpu.VMEM((LANES, LANES), jnp.int32),
            pltpu.VMEM((peers * slots, own_rows.shape[0]), jnp.bfloat16),
        ],
        compiler_params=pltpu.CompilerParams(vmem_limit_bytes=16 << 20),
        name="answer",
    )(wanted, own_rows)


def remap(entries, own, done, cap, shift):
    slot = jnp.maximum(entries - own, 0)
    peer = slot // cap
    moved = jnp.take_along_axis(
        jnp.broadcast_to(shift, entries.shape), peer, axis=1, mode="promise_in_bounds"
    )
    column = jnp.where(entries < own, entries, entries - moved) - done
    return jnp.where(entries < done, BLANK, column)


def plan_kernel(
    variants,
    coarse_at,
    af_ref,
    ac_ref,
    lf_ref,
    lc_ref,
    idx_ref,
    to_ref,
    pick_ref,
    cnt,
):
    offsets = lf_ref.shape[1]
    body_lanes = offsets // LANES * LANES
    peers = af_ref.shape[1]
    lanes = lane_iota((LANES, LANES))
    earlier = lax.broadcasted_iota(jnp.int32, (LANES, LANES), 0) < lanes
    earlier = earlier.astype(jnp.float32).astype(jnp.bfloat16)
    levels = []
    row = 0
    cnt[...] = jnp.zeros_like(cnt)
    for level, (ask_ref, list_ref) in enumerate(((af_ref, lf_ref), (ac_ref, lc_ref))):
        own, cap = list_ref.shape[0], ask_ref.shape[0]
        done = LOCAL if level == 0 else 0
        valid = (ask_ref[...] >= 0).astype(jnp.float32)
        cnt[level, 0:1, 0:peers] = jnp.sum(valid, axis=0, keepdims=True)
        counts = cnt[level]
        before = jnp.dot(
            counts.astype(jnp.bfloat16), earlier, preferred_element_type=jnp.float32
        ).astype(jnp.int32)[0:1]
        total = jnp.sum(counts).astype(jnp.int32)
        counts = counts.astype(jnp.int32)[0:1]
        shift = lane_iota((1, LANES)) * cap - before
        levels.append((own, cap, counts, before, total))
        lists = [list_ref[:, first : first + LANES] for first in range(0, body_lanes, LANES)]
        lists.append(
            jnp.concatenate(
                [
                    list_ref[:, body_lanes:offsets],
                    jnp.full((own, LANES - (offsets - body_lanes)), -1, jnp.int32),
                ],
                axis=1,
            )
        )
        for k, x in enumerate(lists):
            idx_ref[row : row + own, k * LANES : (k + 1) * LANES] = remap(
                x, own, done, cap, shift
            )
        row += own

    (fine_own, fine_cap, *fine), (coarse_own, coarse_cap, *coarse) = levels
    place = lax.broadcasted_iota(jnp.int32, (8, LANES), 0)
    at = 0
    for level, base in (((fine_cap, *fine), fine_own - LOCAL), ((coarse_cap, *coarse), coarse_at + coarse_own)):
        cap, counts, before, _ = level
        for first in range(0, cap, 8):
            for e in range(peers):
                count = jnp.broadcast_to(counts[:, e : e + 1], (8, LANES))
                start = jnp.broadcast_to(before[:, e : e + 1], (8, LANES)) + base
                k = place + first
                to_ref[at : at + 8, :] = jnp.where(k < count, start + k, -1)
                at += 8
    octant = lax.broadcasted_iota(jnp.int32, (fine_own, LANES), 0)
    to_ref[at : at + fine_own, :] = jnp.maximum(octant - LOCAL, -1)
    octant = lax.broadcasted_iota(jnp.int32, (coarse_own, LANES), 0)
    to_ref[at + fine_own : at + row, :] = octant + coarse_at

    pick = jnp.int32(len(variants) - 1)
    for at in reversed(range(len(variants) - 1)):
        fits = (fine_own - LOCAL + fine[2] <= variants[at][0] * LANES) & (
            coarse_own + coarse[2] <= variants[at][1] * LANES
        )
        pick = jnp.where(fits, at, pick)
    pick_ref[0] = pick


def plan(asks_fine, asks_coarse, list_fine, list_coarse, variants, coarse_at):
    own = list_fine.shape[0] + list_coarse.shape[0]
    width = ceil_to(list_fine.shape[1], LANES)
    slots, peers = asks_fine.shape[0] + asks_coarse.shape[0], asks_fine.shape[1]
    vmem = pl.BlockSpec(memory_space=pltpu.VMEM)
    return pl.pallas_call(
        functools.partial(plan_kernel, variants, coarse_at),
        out_specs=[vmem, vmem, pl.BlockSpec(memory_space=pltpu.SMEM)],
        out_shape=[
            shape_of((own, width), jnp.int32),
            shape_of((own + peers * slots, LANES), jnp.int32),
            shape_of((1,), jnp.int32),
        ],
        scratch_shapes=[pltpu.VMEM((2, 8, LANES), jnp.float32)],
        compiler_params=pltpu.CompilerParams(vmem_limit_bytes=VMEM_BYTES),
        name="plan",
    )(asks_fine, asks_coarse, list_fine, list_coarse)


def pack_rows(values, table, tile):
    pairs = values.shape[0] // 2
    even = values[pl.ds(0, pairs, stride=2), :].astype(jnp.int32)
    odd = values[pl.ds(1, pairs, stride=2), :].astype(jnp.int32)
    both = odd * 65536 + even
    for block in range(table.shape[0]):
        part = both[8 * block : 8 * block + 8]
        if part.shape[0] < 8:
            part = jnp.concatenate([part, jnp.zeros((8 - part.shape[0], LANES), jnp.int32)], axis=0)
        table[block, :, tile * LANES : (tile + 1) * LANES] = part


def scale_of(values):
    peak = jnp.max(jnp.max(jnp.abs(values), axis=0, keepdims=True), axis=1, keepdims=True)
    power = jnp.floor(jnp.log2(jnp.broadcast_to(jnp.maximum(peak, 1e-30), (8, LANES))))
    return jnp.exp2(13.0 - power)[0:1], jnp.exp2(power - 29.0)


def build_tables(ranges, to_ref, own_ref, arrived, rows_t, table_f, table, unit):
    peers, lines, _ = arrived.shape
    surface = rows_t.shape[0]
    extra = surface - LANES
    came = arrived[...].astype(jnp.float32)
    rest = came[:, lines - 8 :].reshape(peers * 8, LANES).T
    at = 0
    for g in range(lines // 8 - 1):
        part = came[:, 8 * g : 8 * g + 8].reshape(peers * 8, LANES).T
        part = jnp.concatenate([part, rest[g * extra : (g + 1) * extra]], axis=0)
        rows_t[:, at : at + peers * 8] = part.astype(jnp.bfloat16)
        at += peers * 8
    own = own_ref[...].astype(jnp.float32)
    rows_t[:, at : at + own.shape[0]] = own.T.astype(jnp.bfloat16)
    to = to_ref[...]
    tiles = table_f.shape[0]
    lanes = lane_iota(to.shape)
    for k in range(0, tiles, 2):
        size = min(2, tiles - k)
        hot = [(to == lanes + (k + h) * LANES).astype(jnp.float32) for h in range(size)]
        hot = jnp.concatenate([x.astype(jnp.bfloat16) for x in hot], axis=1)
        columns = jnp.dot(rows_t[...], hot, preferred_element_type=jnp.float32)
        for h in range(size):
            table_f[k + h] = columns[:, h * LANES : (h + 1) * LANES]
    for level, (low, high) in enumerate(ranges):
        factor, unit[level] = scale_of(jnp.max(jnp.abs(table_f[low:high]), axis=0))
        for k in range(low, high):
            table_f[k] = jnp.round(table_f[k] * factor)
            pack_rows(table_f.at[k], table, k)


def lay_pieces(surface, offsets, left, group, m_ref, stage, mr_ref):
    width = m_ref.shape[2]
    tiles = width // LANES

    def spread(tile, first):
        inside = lane_iota((8, LANES)) < offsets - tile * LANES
        if group:
            row = lax.broadcasted_iota(jnp.int32, (8, LANES), 0) + group
            inside = inside & (row < left)
        for a in range(first, first + 19):
            part = m_ref[a, group : group + 8, tile * LANES : (tile + 1) * LANES]
            part = part.astype(jnp.float32)
            if group or (tile + 1) * LANES > offsets:
                part = jnp.where(inside, part, 0.0)
            stage[group // 8, tile, pl.ds(STAGE_A * a, 8, stride=STAGE_B), :] = part

    def lay(tile, j):
        rows = stage[group // 8, tile, pl.ds(STAGE_B * j, surface, stride=STAGE_A), :]
        at = (j * tiles + tile) * LANES
        mr_ref[:, at : at + LANES] = rows.astype(jnp.bfloat16)

    for tile in range(tiles):
        for first in range(0, surface, 19):
            yield functools.partial(spread, tile, first)
        for j in range(8):
            yield functools.partial(lay, tile, j)


def product(acc, g_ref, mr_ref):
    acc[...] += lax.dot_general(
        g_ref[...],
        mr_ref[...],
        (((1,), (1,)), ((), ())),
        preferred_element_type=jnp.float32,
    )


def gather_pieces(step, first_pair, levels, idx_ref, table, g_ref):
    width = idx_ref.shape[1]
    for low, high, base, tiles in levels:
        rows = [
            [
                jnp.broadcast_to(
                    table[
                        step,
                        first_pair + q : first_pair + q + 1,
                        (base + k) * LANES : (base + k + 1) * LANES,
                    ],
                    (8, LANES),
                )
                for k in range(tiles)
            ]
            for q in range(PAIRS // 2)
        ]

        def words(rows, tiles, target, first):
            idx = idx_ref[target : target + 8, first : first + LANES]
            at = idx & (LANES - 1)
            later = [idx >= k * LANES for k in range(1, tiles)]
            blank = idx < 0
            values = []
            for q in range(PAIRS // 2):
                value = None
                for k in range(tiles):
                    got = jnp.take_along_axis(rows[q][k], at, axis=1, mode="promise_in_bounds")
                    value = got if k == 0 else jnp.where(later[k - 1], got, value)
                values.append(jnp.where(blank, 0, value))
            return values

        def unit(rows, tiles, target, first):
            upper = words(rows, tiles, target, first)
            lower = words(rows, tiles, target + 8, first)
            for q in range(PAIRS // 2):
                value = jnp.concatenate([upper[q], lower[q]], axis=0)
                low_half = (value << 16).astype(jnp.float32).astype(jnp.bfloat16)
                high_half = value.astype(jnp.float32).astype(jnp.bfloat16)
                to = 2 * q * width + first
                g_ref[target : target + CHUNK, to : to + LANES] = low_half
                to = to + width
                g_ref[target : target + CHUNK, to : to + LANES] = high_half

        for first in range(0, width, LANES):
            for target in range(low, high, CHUNK):
                yield functools.partial(unit, rows, tiles, target, first)


def interleave(main, others):
    done = 0
    for n, piece in enumerate(main):
        piece()
        until = (n + 1) * len(others) // len(main)
        for other in others[done:until]:
            other()
        done = until


def translate_kernel(
    variants,
    coarse_tile,
    offsets,
    pick_ref,
    idx_ref,
    to_ref,
    own_ref,
    arrived_any,
    m_ref,
    of_ref,
    oc_ref,
    rows_t,
    table_f,
    table,
    unit,
    arrived,
    stage,
    acc,
    mr_a,
    mr_b,
    g_a,
    g_b,
    sem,
):
    fine_own, targets = of_ref.shape[0], idx_ref.shape[0]
    step = pl.program_id(0)

    @pl.when(step == 0)
    def _():
        fetch = pltpu.make_async_copy(arrived_any, arrived, sem)
        fetch.start()
        for ref in (acc, mr_b, g_b):
            ref[...] = jnp.zeros_like(ref)
        fetch.wait()
        build_tables(
            ((0, coarse_tile), (coarse_tile, table_f.shape[0])),
            to_ref,
            own_ref,
            arrived,
            rows_t,
            table_f,
            table,
            unit,
        )

    def work(fine_tiles, coarse_tiles):
        levels = (
            (0, fine_own, 0, fine_tiles),
            (fine_own, targets, coarse_tile, coarse_tiles),
        )
        surface = of_ref.shape[1]
        left = surface - step * 2 * PAIRS
        for half, (now, before) in enumerate((((g_a, mr_a), (g_b, mr_b)), ((g_b, mr_b), (g_a, mr_a)))):
            product(acc, *before)
            interleave(
                list(gather_pieces(step, half * PAIRS // 2, levels, idx_ref, table, now[0])),
                list(lay_pieces(surface, offsets, left, half * 8, m_ref, stage, now[1])),
            )

    for at, tiles in enumerate(variants):
        pl.when(pick_ref[0] == at)(functools.partial(work, *tiles))

    @pl.when(step == pl.num_programs(0) - 1)
    def _():
        product(acc, g_b, mr_b)
        of_ref[...] = acc[0:fine_own, :] * unit[0, 0:1, 0:1]
        oc_ref[...] = acc[fine_own:targets, :] * (0.5 * unit[1, 0:1, 0:1])


def translate(
    pick, idx, to, own_rows, arrived, m2l_ops, variants, coarse_tile, tiles, fine_own
):
    surface, _, offsets = m2l_ops.shape
    width = ceil_to(offsets, LANES)
    targets = idx.shape[0]
    coarse_own = targets - fine_own
    blocks = pl.cdiv(surface, 2 * PAIRS)
    return pl.pallas_call(
        functools.partial(translate_kernel, variants, coarse_tile, offsets),
        grid=(blocks,),
        in_specs=[
            pl.BlockSpec(memory_space=pltpu.SMEM),
            whole(idx),
            whole(to),
            whole(own_rows),
            pl.BlockSpec(memory_space=pl.ANY),
            pl.BlockSpec((surface, 2 * PAIRS, width), lambda i: (0, i, 0)),
        ],
        out_specs=[
            pl.BlockSpec((fine_own, surface), lambda i: (0, 0)),
            pl.BlockSpec((coarse_own, surface), lambda i: (0, 0)),
        ],
        out_shape=[
            shape_of((fine_own, surface), jnp.float32),
            shape_of((coarse_own, surface), jnp.float32),
        ],
        scratch_shapes=[
            pltpu.VMEM((surface, to.shape[0]), jnp.bfloat16),
            pltpu.VMEM((tiles, surface, LANES), jnp.float32),
            pltpu.VMEM((blocks, 8, tiles * LANES), jnp.int32),
            pltpu.VMEM((2, 8, LANES), jnp.float32),
            pltpu.VMEM(arrived.shape, jnp.bfloat16),
            pltpu.VMEM(
                (PAIRS // 4, width // LANES, ceil_to(STAGE_A * surface, 8), LANES), jnp.float32
            ),
            pltpu.VMEM((targets, surface), jnp.float32),
            pltpu.VMEM((surface, PAIRS * width), jnp.bfloat16),
            pltpu.VMEM((surface, PAIRS * width), jnp.bfloat16),
            pltpu.VMEM((targets, PAIRS * width), jnp.bfloat16),
            pltpu.VMEM((targets, PAIRS * width), jnp.bfloat16),
            pltpu.SemaphoreType.DMA,
        ],
        compiler_params=pltpu.CompilerParams(vmem_limit_bytes=48 << 20),
        cost_estimate=pl.CostEstimate(
            flops=2 * surface * surface * targets * width,
            bytes_accessed=2 * surface * surface * width,
            transcendentals=0,
        ),
        name="translate",
    )(pick, idx, to, own_rows, arrived, m2l_ops)


def exchange(x):
    return lax.all_to_all(x, AXES, split_axis=0, concat_axis=0, tiled=True)


def body(
    dens_fine, parent, child_code, m2m_ops, m2l_ops, ask_fine, list_fine, ask_coarse, list_coarse
):
    surface, fine_own = dens_fine.shape
    coarse_own = list_coarse.shape[0]
    asks_fine, asks_coarse = ask_fine[0].T, ask_coarse[0].T
    fine_cap, peers = asks_fine.shape
    coarse_cap = asks_coarse.shape[0]
    wanted = exchange(join_asks(asks_fine, asks_coarse, fine_own))

    fine_tiles = ceil_to(fine_own - LOCAL + (peers - 1) * fine_cap, LANES) // LANES
    coarse_tiles = ceil_to(coarse_own + (peers - 1) * coarse_cap, LANES) // LANES
    variants = [(min(n, fine_tiles), min(2, coarse_tiles)) for n in (3, 4)]
    variants = variants + [(fine_tiles, coarse_tiles)]
    idx, to, pick = plan(
        asks_fine, asks_coarse, list_fine, list_coarse, variants, fine_tiles * LANES
    )

    fine_rows = dens_fine.T
    positions = jnp.arange(8, dtype=jnp.int32)
    spread = jnp.where(
        (child_code[:, None] == positions[None, :])[:, :, None],
        fine_rows[:, None, :],
        jnp.zeros((), jnp.bfloat16),
    )
    child_terms = lax.dot_general(
        spread.reshape(fine_own, 8 * surface),
        m2m_ops.reshape(surface, 8 * surface),
        (((1,), (1,)), ((), ())),
        preferred_element_type=jnp.float32,
    )
    local_parent = parent - lax.axis_index(AXES) * coarse_own
    members = (jnp.arange(coarse_own, dtype=jnp.int32)[:, None] == local_parent[None, :]).astype(
        jnp.float32
    )
    coarse_rows = jnp.dot(members, child_terms, precision=lax.Precision.HIGHEST).astype(
        jnp.bfloat16
    )

    own_rows = jnp.concatenate([fine_rows, coarse_rows], axis=0)
    arrived = exchange(answer(wanted, own_rows))
    pot_fine, pot_coarse = translate(
        pick,
        idx,
        to,
        own_rows,
        arrived,
        m2l_ops,
        variants,
        fine_tiles,
        fine_tiles + coarse_tiles,
        fine_own,
    )
    return pot_fine.T, pot_coarse.T


def solution(mesh):
    return jax.shard_map(
        body,
        mesh=mesh,
        in_specs=(
            P(None, AXES),
            P(AXES),
            P(AXES),
            P(),
            P(),
            P(AXES, None, None),
            P(AXES, None),
            P(AXES, None, None),
            P(AXES, None),
        ),
        out_specs=(P(None, AXES), P(None, AXES)),
        check_vma=False,
    )
```

```python
import functools

import jax
import jax.numpy as jnp
from jax import lax
from jax.experimental import pallas as pl
from jax.experimental.pallas import tpu as pltpu
from jax.sharding import PartitionSpec as P

LANES = 128
CHUNK = 16
PAIRS = 8
BLANK = -1
LOCAL = 0
AXES = ("leaf", "oct")
STAGE_A, STAGE_B = 23, 3
VMEM_BYTES = 48 << 20


def ceil_to(n, m):
    return (n + m - 1) // m * m


def lane_iota(shape):
    return lax.broadcasted_iota(jnp.int32, shape, 1)


def whole(x):
    return pl.BlockSpec(x.shape, lambda *i: (0,) * x.ndim)


def shape_of(shape, dtype):
    return jax.ShapeDtypeStruct(shape, dtype)


def asks_kernel(fine_own, f_ref, c_ref, o_ref, scr):
    fine_cap, peers = f_ref.shape
    coarse_cap = c_ref.shape[0]
    scr[...] = jnp.zeros_like(scr)
    scr[0:fine_cap, 0:peers] = f_ref[...]
    coarse = c_ref[...]
    scr[fine_cap : fine_cap + coarse_cap, 0:peers] = jnp.where(coarse < 0, -1, coarse + fine_own)
    o_ref[...] = scr[...].T[0:peers, 0 : fine_cap + coarse_cap]


def join_asks(asks_fine, asks_coarse, fine_own):
    peers = asks_fine.shape[1]
    slots = asks_fine.shape[0] + asks_coarse.shape[0]
    return pl.pallas_call(
        functools.partial(asks_kernel, fine_own),
        out_shape=shape_of((peers, slots), jnp.int32),
        scratch_shapes=[pltpu.VMEM((LANES, LANES), jnp.int32)],
        name="join_asks",
    )(asks_fine, asks_coarse)


def answer_kernel(w_ref, own_ref, o_ref, scr, hot):
    peers, slots = w_ref.shape
    own, surface = own_ref.shape
    scr[0:peers, 0:slots] = w_ref[...]
    columns = scr[...].T[0:slots, :]
    octant = lane_iota((slots, own))
    for e in range(0, peers, 2):
        picked = [
            jnp.broadcast_to(columns[:, d : d + 1], (slots, own)) == octant for d in (e, e + 1)
        ]
        both = jnp.concatenate([p.astype(jnp.float32) for p in picked], axis=0)
        hot[e * slots : (e + 2) * slots, :] = both.astype(jnp.bfloat16)
    found = jnp.dot(hot[...], own_ref[...], preferred_element_type=jnp.float32)
    extra = surface - LANES
    rest = jnp.concatenate(
        [found[:, LANES:], jnp.zeros((peers * slots, LANES - extra), jnp.float32)], axis=1
    ).reshape(peers, slots, LANES)
    line = rest[:, 0:8].reshape(peers * 8, LANES)
    for g in range(1, slots // 8):
        part = rest[:, 8 * g : 8 * g + 8].reshape(peers * 8, LANES)
        line = line + pltpu.roll(part, g * extra, axis=1)
    o_ref[...] = jnp.concatenate(
        [found[:, 0:LANES].reshape(peers, slots, LANES), line.reshape(peers, 8, LANES)], axis=1
    ).astype(jnp.bfloat16)


def answer(wanted, own_rows):
    peers, slots = wanted.shape
    return pl.pallas_call(
        answer_kernel,
        out_shape=shape_of((peers, slots + 8, LANES), jnp.bfloat16),
        scratch_shapes=[
            pltpu.VMEM((LANES, LANES), jnp.int32),
            pltpu.VMEM((peers * slots, own_rows.shape[0]), jnp.bfloat16),
        ],
        compiler_params=pltpu.CompilerParams(vmem_limit_bytes=16 << 20),
        name="answer",
    )(wanted, own_rows)


def remap(entries, own, done, cap, shift):
    slot = jnp.maximum(entries - own, 0)
    peer = slot // cap
    moved = jnp.take_along_axis(
        jnp.broadcast_to(shift, entries.shape), peer, axis=1, mode="promise_in_bounds"
    )
    column = jnp.where(entries < own, entries, entries - moved) - done
    return jnp.where(entries < done, BLANK, column)


def plan_kernel(
    variants,
    coarse_at,
    af_ref,
    ac_ref,
    lf_ref,
    lc_ref,
    idx_ref,
    to_ref,
    pick_ref,
    cnt,
):
    offsets = lf_ref.shape[1]
    body_lanes = offsets // LANES * LANES
    peers = af_ref.shape[1]
    lanes = lane_iota((LANES, LANES))
    earlier = lax.broadcasted_iota(jnp.int32, (LANES, LANES), 0) < lanes
    earlier = earlier.astype(jnp.float32).astype(jnp.bfloat16)
    levels = []
    row = 0
    cnt[...] = jnp.zeros_like(cnt)
    for level, (ask_ref, list_ref) in enumerate(((af_ref, lf_ref), (ac_ref, lc_ref))):
        own, cap = list_ref.shape[0], ask_ref.shape[0]
        done = LOCAL if level == 0 else 0
        valid = (ask_ref[...] >= 0).astype(jnp.float32)
        cnt[level, 0:1, 0:peers] = jnp.sum(valid, axis=0, keepdims=True)
        counts = cnt[level]
        before = jnp.dot(
            counts.astype(jnp.bfloat16), earlier, preferred_element_type=jnp.float32
        ).astype(jnp.int32)[0:1]
        total = jnp.sum(counts).astype(jnp.int32)
        counts = counts.astype(jnp.int32)[0:1]
        shift = lane_iota((1, LANES)) * cap - before
        levels.append((own, cap, counts, before, total))
        lists = [list_ref[:, first : first + LANES] for first in range(0, body_lanes, LANES)]
        lists.append(
            jnp.concatenate(
                [
                    list_ref[:, body_lanes:offsets],
                    jnp.full((own, LANES - (offsets - body_lanes)), -1, jnp.int32),
                ],
                axis=1,
            )
        )
        for k, x in enumerate(lists):
            idx_ref[row : row + own, k * LANES : (k + 1) * LANES] = remap(
                x, own, done, cap, shift
            )
        row += own

    (fine_own, fine_cap, *fine), (coarse_own, coarse_cap, *coarse) = levels
    place = lax.broadcasted_iota(jnp.int32, (8, LANES), 0)
    at = 0
    for level, base in (((fine_cap, *fine), fine_own - LOCAL), ((coarse_cap, *coarse), coarse_at + coarse_own)):
        cap, counts, before, _ = level
        for first in range(0, cap, 8):
            for e in range(peers):
                count = jnp.broadcast_to(counts[:, e : e + 1], (8, LANES))
                start = jnp.broadcast_to(before[:, e : e + 1], (8, LANES)) + base
                k = place + first
                to_ref[at : at + 8, :] = jnp.where(k < count, start + k, -1)
                at += 8
    octant = lax.broadcasted_iota(jnp.int32, (fine_own, LANES), 0)
    to_ref[at : at + fine_own, :] = jnp.maximum(octant - LOCAL, -1)
    octant = lax.broadcasted_iota(jnp.int32, (coarse_own, LANES), 0)
    to_ref[at + fine_own : at + row, :] = octant + coarse_at

    pick = jnp.int32(len(variants) - 1)
    for at in reversed(range(len(variants) - 1)):
        fits = (fine_own - LOCAL + fine[2] <= variants[at][0] * LANES) & (
            coarse_own + coarse[2] <= variants[at][1] * LANES
        )
        pick = jnp.where(fits, at, pick)
    pick_ref[0] = pick


def plan(asks_fine, asks_coarse, list_fine, list_coarse, variants, coarse_at):
    own = list_fine.shape[0] + list_coarse.shape[0]
    width = ceil_to(list_fine.shape[1], LANES)
    slots, peers = asks_fine.shape[0] + asks_coarse.shape[0], asks_fine.shape[1]
    vmem = pl.BlockSpec(memory_space=pltpu.VMEM)
    return pl.pallas_call(
        functools.partial(plan_kernel, variants, coarse_at),
        out_specs=[vmem, vmem, pl.BlockSpec(memory_space=pltpu.SMEM)],
        out_shape=[
            shape_of((own, width), jnp.int32),
            shape_of((own + peers * slots, LANES), jnp.int32),
            shape_of((1,), jnp.int32),
        ],
        scratch_shapes=[pltpu.VMEM((2, 8, LANES), jnp.float32)],
        compiler_params=pltpu.CompilerParams(vmem_limit_bytes=VMEM_BYTES),
        name="plan",
    )(asks_fine, asks_coarse, list_fine, list_coarse)


def pack_rows(values, table, tile):
    pairs = values.shape[0] // 2
    even = values[pl.ds(0, pairs, stride=2), :].astype(jnp.int32)
    odd = values[pl.ds(1, pairs, stride=2), :].astype(jnp.int32)
    both = odd * 65536 + even
    for block in range(table.shape[0]):
        part = both[2 * PAIRS * block : 2 * PAIRS * (block + 1)]
        missing = 2 * PAIRS - part.shape[0]
        if missing:
            part = jnp.concatenate([part, jnp.zeros((missing, LANES), jnp.int32)], axis=0)
        table[block, :, tile * LANES : (tile + 1) * LANES] = part


def scale_of(values):
    peak = jnp.max(jnp.max(jnp.abs(values), axis=0, keepdims=True), axis=1, keepdims=True)
    power = jnp.floor(jnp.log2(jnp.broadcast_to(jnp.maximum(peak, 1e-30), (8, LANES))))
    return jnp.exp2(13.0 - power)[0:1], jnp.exp2(power - 29.0)


def build_tables(ranges, to_ref, own_ref, arrived, rows_t, table_f, table, unit):
    peers, lines, _ = arrived.shape
    surface = rows_t.shape[0]
    extra = surface - LANES
    came = arrived[...].astype(jnp.float32)
    rest = came[:, lines - 8 :].reshape(peers * 8, LANES).T
    at = 0
    for g in range(lines // 8 - 1):
        part = came[:, 8 * g : 8 * g + 8].reshape(peers * 8, LANES).T
        part = jnp.concatenate([part, rest[g * extra : (g + 1) * extra]], axis=0)
        rows_t[:, at : at + peers * 8] = part.astype(jnp.bfloat16)
        at += peers * 8
    own = own_ref[...].astype(jnp.float32)
    rows_t[:, at : at + own.shape[0]] = own.T.astype(jnp.bfloat16)
    to = to_ref[...]
    tiles = table_f.shape[0]
    lanes = lane_iota(to.shape)
    for k in range(0, tiles, 2):
        size = min(2, tiles - k)
        hot = [(to == lanes + (k + h) * LANES).astype(jnp.float32) for h in range(size)]
        hot = jnp.concatenate([x.astype(jnp.bfloat16) for x in hot], axis=1)
        columns = jnp.dot(rows_t[...], hot, preferred_element_type=jnp.float32)
        for h in range(size):
            table_f[k + h] = columns[:, h * LANES : (h + 1) * LANES]
    for level, (low, high) in enumerate(ranges):
        factor, unit[level] = scale_of(jnp.max(jnp.abs(table_f[low:high]), axis=0))
        for k in range(low, high):
            table_f[k] = jnp.round(table_f[k] * factor)
            pack_rows(table_f.at[k], table, k)


def lay_pieces(surface, offsets, half, m_ref, stage, mr_ref):
    _, step_b, width = m_ref.shape
    tiles = width // LANES
    step = pl.program_id(0)
    real = surface - (pl.cdiv(surface, step_b) - 1) * step_b

    def spread(group, tile, first):
        at_b = half * 2 * PAIRS + group * 8
        inside = lane_iota((8, LANES)) < offsets - tile * LANES
        short = at_b + 8 > real
        if short:
            row = lax.broadcasted_iota(jnp.int32, (8, LANES), 0) + at_b
            inside = inside & (row < surface - step * step_b)
        for a in range(first, first + 19):
            part = m_ref[a, at_b : at_b + 8, tile * LANES : (tile + 1) * LANES]
            part = part.astype(jnp.float32)
            if short or (tile + 1) * LANES > offsets:
                part = jnp.where(inside, part, 0.0)
            stage[group, tile, pl.ds(STAGE_A * a, 8, stride=STAGE_B), :] = part

    def lay(group, tile, j):
        rows = stage[group, tile, pl.ds(STAGE_B * j, surface, stride=STAGE_A), :]
        at = ((group * 8 + j) * tiles + tile) * LANES
        mr_ref[:, at : at + LANES] = rows.astype(jnp.bfloat16)

    for group in range(PAIRS // 4):
        for tile in range(tiles):
            for first in range(0, surface, 19):
                yield functools.partial(spread, group, tile, first)
            for j in range(8):
                yield functools.partial(lay, group, tile, j)


def product(acc, g_ref, mr_ref):
    acc[...] += lax.dot_general(
        g_ref[...],
        mr_ref[...],
        (((1,), (1,)), ((), ())),
        preferred_element_type=jnp.float32,
    )


def gather_pieces(step, first_pair, levels, idx_ref, table, g_ref):
    width = idx_ref.shape[1]
    for low, high, base, tiles in levels:
        rows = [
            [
                jnp.broadcast_to(
                    table[
                        step,
                        first_pair + q : first_pair + q + 1,
                        (base + k) * LANES : (base + k + 1) * LANES,
                    ],
                    (8, LANES),
                )
                for k in range(tiles)
            ]
            for q in range(PAIRS)
        ]

        def words(rows, tiles, target, first):
            idx = idx_ref[target : target + 8, first : first + LANES]
            at = idx & (LANES - 1)
            later = [idx >= k * LANES for k in range(1, tiles)]
            blank = idx < 0
            values = []
            for q in range(PAIRS):
                value = None
                for k in range(tiles):
                    got = jnp.take_along_axis(rows[q][k], at, axis=1, mode="promise_in_bounds")
                    value = got if k == 0 else jnp.where(later[k - 1], got, value)
                values.append(jnp.where(blank, 0, value))
            return values

        def unit(rows, tiles, target, first):
            upper = words(rows, tiles, target, first)
            lower = words(rows, tiles, target + 8, first)
            for q in range(PAIRS):
                value = jnp.concatenate([upper[q], lower[q]], axis=0)
                low_half = (value << 16).astype(jnp.float32).astype(jnp.bfloat16)
                high_half = value.astype(jnp.float32).astype(jnp.bfloat16)
                to = 2 * q * width + first
                g_ref[target : target + CHUNK, to : to + LANES] = low_half
                to = to + width
                g_ref[target : target + CHUNK, to : to + LANES] = high_half

        for first in range(0, width, LANES):
            for target in range(low, high, CHUNK):
                yield functools.partial(unit, rows, tiles, target, first)


def interleave(main, others):
    done = 0
    for n, piece in enumerate(main):
        piece()
        until = (n + 1) * len(others) // len(main)
        for other in others[done:until]:
            other()
        done = until


def translate_kernel(
    variants,
    coarse_tile,
    offsets,
    pick_ref,
    idx_ref,
    to_ref,
    own_ref,
    arrived_any,
    m_ref,
    of_ref,
    oc_ref,
    rows_t,
    table_f,
    table,
    unit,
    arrived,
    stage,
    acc,
    mr_a,
    mr_b,
    g_a,
    g_b,
    sem,
):
    fine_own, targets = of_ref.shape[0], idx_ref.shape[0]
    step = pl.program_id(0)

    @pl.when(step == 0)
    def _():
        fetch = pltpu.make_async_copy(arrived_any, arrived, sem)
        fetch.start()
        for ref in (acc, mr_b, g_b):
            ref[...] = jnp.zeros_like(ref)
        fetch.wait()
        build_tables(
            ((0, coarse_tile), (coarse_tile, table_f.shape[0])),
            to_ref,
            own_ref,
            arrived,
            rows_t,
            table_f,
            table,
            unit,
        )

    def work(fine_tiles, coarse_tiles):
        levels = (
            (0, fine_own, 0, fine_tiles),
            (fine_own, targets, coarse_tile, coarse_tiles),
        )
        surface = of_ref.shape[1]
        for half, (now, before) in enumerate((((g_a, mr_a), (g_b, mr_b)), ((g_b, mr_b), (g_a, mr_a)))):
            product(acc, *before)
            interleave(
                list(gather_pieces(step, half * PAIRS, levels, idx_ref, table, now[0])),
                list(lay_pieces(surface, offsets, half, m_ref, stage, now[1])),
            )

    for at, tiles in enumerate(variants):
        pl.when(pick_ref[0] == at)(functools.partial(work, *tiles))

    @pl.when(step == pl.num_programs(0) - 1)
    def _():
        product(acc, g_b, mr_b)
        of_ref[...] = acc[0:fine_own, :] * unit[0, 0:1, 0:1]
        oc_ref[...] = acc[fine_own:targets, :] * (0.5 * unit[1, 0:1, 0:1])


def translate(
    pick, idx, to, own_rows, arrived, m2l_ops, variants, coarse_tile, tiles, fine_own
):
    surface, _, offsets = m2l_ops.shape
    width = ceil_to(offsets, LANES)
    targets = idx.shape[0]
    coarse_own = targets - fine_own
    blocks = pl.cdiv(surface, 4 * PAIRS)
    return pl.pallas_call(
        functools.partial(translate_kernel, variants, coarse_tile, offsets),
        grid=(blocks,),
        in_specs=[
            pl.BlockSpec(memory_space=pltpu.SMEM),
            whole(idx),
            whole(to),
            whole(own_rows),
            pl.BlockSpec(memory_space=pl.ANY),
            pl.BlockSpec((surface, 4 * PAIRS, width), lambda i: (0, i, 0)),
        ],
        out_specs=[
            pl.BlockSpec((fine_own, surface), lambda i: (0, 0)),
            pl.BlockSpec((coarse_own, surface), lambda i: (0, 0)),
        ],
        out_shape=[
            shape_of((fine_own, surface), jnp.float32),
            shape_of((coarse_own, surface), jnp.float32),
        ],
        scratch_shapes=[
            pltpu.VMEM((surface, to.shape[0]), jnp.bfloat16),
            pltpu.VMEM((tiles, surface, LANES), jnp.float32),
            pltpu.VMEM((blocks, 2 * PAIRS, tiles * LANES), jnp.int32),
            pltpu.VMEM((2, 8, LANES), jnp.float32),
            pltpu.VMEM(arrived.shape, jnp.bfloat16),
            pltpu.VMEM(
                (PAIRS // 4, width // LANES, ceil_to(STAGE_A * surface, 8), LANES), jnp.float32
            ),
            pltpu.VMEM((targets, surface), jnp.float32),
            pltpu.VMEM((surface, 2 * PAIRS * width), jnp.bfloat16),
            pltpu.VMEM((surface, 2 * PAIRS * width), jnp.bfloat16),
            pltpu.VMEM((targets, 2 * PAIRS * width), jnp.bfloat16),
            pltpu.VMEM((targets, 2 * PAIRS * width), jnp.bfloat16),
            pltpu.SemaphoreType.DMA,
        ],
        compiler_params=pltpu.CompilerParams(vmem_limit_bytes=48 << 20),
        cost_estimate=pl.CostEstimate(
            flops=2 * surface * surface * targets * width,
            bytes_accessed=2 * surface * surface * width,
            transcendentals=0,
        ),
        name="translate",
    )(pick, idx, to, own_rows, arrived, m2l_ops)


def exchange(x):
    return lax.all_to_all(x, AXES, split_axis=0, concat_axis=0, tiled=True)


def body(
    dens_fine, parent, child_code, m2m_ops, m2l_ops, ask_fine, list_fine, ask_coarse, list_coarse
):
    surface, fine_own = dens_fine.shape
    coarse_own = list_coarse.shape[0]
    asks_fine, asks_coarse = ask_fine[0].T, ask_coarse[0].T
    fine_cap, peers = asks_fine.shape
    coarse_cap = asks_coarse.shape[0]
    wanted = exchange(join_asks(asks_fine, asks_coarse, fine_own))

    fine_tiles = ceil_to(fine_own - LOCAL + (peers - 1) * fine_cap, LANES) // LANES
    coarse_tiles = ceil_to(coarse_own + (peers - 1) * coarse_cap, LANES) // LANES
    variants = [(min(n, fine_tiles), min(2, coarse_tiles)) for n in (3, 4)]
    variants = variants + [(fine_tiles, coarse_tiles)]
    idx, to, pick = plan(
        asks_fine, asks_coarse, list_fine, list_coarse, variants, fine_tiles * LANES
    )

    fine_rows = dens_fine.T
    positions = jnp.arange(8, dtype=jnp.int32)
    spread = jnp.where(
        (child_code[:, None] == positions[None, :])[:, :, None],
        fine_rows[:, None, :],
        jnp.zeros((), jnp.bfloat16),
    )
    child_terms = lax.dot_general(
        spread.reshape(fine_own, 8 * surface),
        m2m_ops.reshape(surface, 8 * surface),
        (((1,), (1,)), ((), ())),
        preferred_element_type=jnp.float32,
    )
    local_parent = parent - lax.axis_index(AXES) * coarse_own
    members = (jnp.arange(coarse_own, dtype=jnp.int32)[:, None] == local_parent[None, :]).astype(
        jnp.float32
    )
    coarse_rows = jnp.dot(members, child_terms, precision=lax.Precision.HIGHEST).astype(
        jnp.bfloat16
    )

    own_rows = jnp.concatenate([fine_rows, coarse_rows], axis=0)
    arrived = exchange(answer(wanted, own_rows))
    pot_fine, pot_coarse = translate(
        pick,
        idx,
        to,
        own_rows,
        arrived,
        m2l_ops,
        variants,
        fine_tiles,
        fine_tiles + coarse_tiles,
        fine_own,
    )
    return pot_fine.T, pot_coarse.T


def solution(mesh):
    return jax.shard_map(
        body,
        mesh=mesh,
        in_specs=(
            P(None, AXES),
            P(AXES),
            P(AXES),
            P(),
            P(),
            P(AXES, None, None),
            P(AXES, None),
            P(AXES, None, None),
            P(AXES, None),
        ),
        out_specs=(P(None, AXES), P(None, AXES)),
        check_vma=False,
    )
```

```python
import functools

import jax
import jax.numpy as jnp
from jax import lax
from jax.experimental import pallas as pl
from jax.experimental.pallas import tpu as pltpu
from jax.sharding import PartitionSpec as P

LANES = 128
CHUNK = 16
PAIRS = 8
BLANK = -1
LOCAL = 0
AXES = ("leaf", "oct")
STAGE_A, STAGE_B = 23, 3
VMEM_BYTES = 48 << 20


def ceil_to(n, m):
    return (n + m - 1) // m * m


def lane_iota(shape):
    return lax.broadcasted_iota(jnp.int32, shape, 1)


def whole(x):
    return pl.BlockSpec(x.shape, lambda *i: (0,) * x.ndim)


def shape_of(shape, dtype):
    return jax.ShapeDtypeStruct(shape, dtype)


def asks_kernel(fine_own, f_ref, c_ref, o_ref, scr):
    fine_cap, peers = f_ref.shape
    coarse_cap = c_ref.shape[0]
    scr[...] = jnp.zeros_like(scr)
    scr[0:fine_cap, 0:peers] = f_ref[...]
    coarse = c_ref[...]
    scr[fine_cap : fine_cap + coarse_cap, 0:peers] = jnp.where(coarse < 0, -1, coarse + fine_own)
    o_ref[...] = scr[...].T[0:peers, 0 : fine_cap + coarse_cap]


def join_asks(asks_fine, asks_coarse, fine_own):
    peers = asks_fine.shape[1]
    slots = asks_fine.shape[0] + asks_coarse.shape[0]
    return pl.pallas_call(
        functools.partial(asks_kernel, fine_own),
        out_shape=shape_of((peers, slots), jnp.int32),
        scratch_shapes=[pltpu.VMEM((LANES, LANES), jnp.int32)],
        name="join_asks",
    )(asks_fine, asks_coarse)


def answer_kernel(w_ref, own_ref, o_ref, scr, hot):
    peers, slots = w_ref.shape
    own, surface = own_ref.shape
    scr[0:peers, 0:slots] = w_ref[...]
    columns = scr[...].T[0:slots, :]
    octant = lane_iota((slots, own))
    for e in range(0, peers, 2):
        picked = [
            jnp.broadcast_to(columns[:, d : d + 1], (slots, own)) == octant for d in (e, e + 1)
        ]
        both = jnp.concatenate([p.astype(jnp.float32) for p in picked], axis=0)
        hot[e * slots : (e + 2) * slots, :] = both.astype(jnp.bfloat16)
    found = jnp.dot(hot[...], own_ref[...], preferred_element_type=jnp.float32)
    extra = surface - LANES
    rest = jnp.concatenate(
        [found[:, LANES:], jnp.zeros((peers * slots, LANES - extra), jnp.float32)], axis=1
    ).reshape(peers, slots, LANES)
    line = rest[:, 0:8].reshape(peers * 8, LANES)
    for g in range(1, slots // 8):
        part = rest[:, 8 * g : 8 * g + 8].reshape(peers * 8, LANES)
        line = line + pltpu.roll(part, g * extra, axis=1)
    o_ref[...] = jnp.concatenate(
        [found[:, 0:LANES].reshape(peers, slots, LANES), line.reshape(peers, 8, LANES)], axis=1
    ).astype(jnp.bfloat16)


def answer(wanted, own_rows):
    peers, slots = wanted.shape
    return pl.pallas_call(
        answer_kernel,
        out_shape=shape_of((peers, slots + 8, LANES), jnp.bfloat16),
        scratch_shapes=[
            pltpu.VMEM((LANES, LANES), jnp.int32),
            pltpu.VMEM((peers * slots, own_rows.shape[0]), jnp.bfloat16),
        ],
        compiler_params=pltpu.CompilerParams(vmem_limit_bytes=16 << 20),
        name="answer",
    )(wanted, own_rows)


def remap(entries, own, done, cap, shift):
    slot = jnp.maximum(entries - own, 0)
    peer = slot // cap
    moved = jnp.take_along_axis(
        jnp.broadcast_to(shift, entries.shape), peer, axis=1, mode="promise_in_bounds"
    )
    column = jnp.where(entries < own, entries, entries - moved) - done
    return jnp.where(entries < done, BLANK, column)


def plan_kernel(
    variants,
    coarse_at,
    af_ref,
    ac_ref,
    lf_ref,
    lc_ref,
    idx_ref,
    to_ref,
    pick_ref,
    cnt,
):
    offsets = lf_ref.shape[1]
    body_lanes = offsets // LANES * LANES
    peers = af_ref.shape[1]
    lanes = lane_iota((LANES, LANES))
    earlier = lax.broadcasted_iota(jnp.int32, (LANES, LANES), 0) < lanes
    earlier = earlier.astype(jnp.float32).astype(jnp.bfloat16)
    levels = []
    row = 0
    cnt[...] = jnp.zeros_like(cnt)
    for level, (ask_ref, list_ref) in enumerate(((af_ref, lf_ref), (ac_ref, lc_ref))):
        own, cap = list_ref.shape[0], ask_ref.shape[0]
        done = LOCAL if level == 0 else 0
        valid = (ask_ref[...] >= 0).astype(jnp.float32)
        cnt[level, 0:1, 0:peers] = jnp.sum(valid, axis=0, keepdims=True)
        counts = cnt[level]
        before = jnp.dot(
            counts.astype(jnp.bfloat16), earlier, preferred_element_type=jnp.float32
        ).astype(jnp.int32)[0:1]
        total = jnp.sum(counts).astype(jnp.int32)
        counts = counts.astype(jnp.int32)[0:1]
        shift = lane_iota((1, LANES)) * cap - before
        levels.append((own, cap, counts, before, total))
        lists = [list_ref[:, first : first + LANES] for first in range(0, body_lanes, LANES)]
        lists.append(
            jnp.concatenate(
                [
                    list_ref[:, body_lanes:offsets],
                    jnp.full((own, LANES - (offsets - body_lanes)), -1, jnp.int32),
                ],
                axis=1,
            )
        )
        for k, x in enumerate(lists):
            idx_ref[row : row + own, k * LANES : (k + 1) * LANES] = remap(
                x, own, done, cap, shift
            )
        row += own

    (fine_own, fine_cap, *fine), (coarse_own, coarse_cap, *coarse) = levels
    place = lax.broadcasted_iota(jnp.int32, (8, LANES), 0)
    at = 0
    for level, base in (((fine_cap, *fine), fine_own - LOCAL), ((coarse_cap, *coarse), coarse_at + coarse_own)):
        cap, counts, before, _ = level
        for first in range(0, cap, 8):
            for e in range(peers):
                count = jnp.broadcast_to(counts[:, e : e + 1], (8, LANES))
                start = jnp.broadcast_to(before[:, e : e + 1], (8, LANES)) + base
                k = place + first
                to_ref[at : at + 8, :] = jnp.where(k < count, start + k, -1)
                at += 8
    octant = lax.broadcasted_iota(jnp.int32, (fine_own, LANES), 0)
    to_ref[at : at + fine_own, :] = jnp.maximum(octant - LOCAL, -1)
    octant = lax.broadcasted_iota(jnp.int32, (coarse_own, LANES), 0)
    to_ref[at + fine_own : at + row, :] = octant + coarse_at

    pick = jnp.int32(len(variants) - 1)
    for at in reversed(range(len(variants) - 1)):
        fits = (fine_own - LOCAL + fine[2] <= variants[at][0] * LANES) & (
            coarse_own + coarse[2] <= variants[at][1] * LANES
        )
        pick = jnp.where(fits, at, pick)
    pick_ref[0] = pick


def plan(asks_fine, asks_coarse, list_fine, list_coarse, variants, coarse_at):
    own = list_fine.shape[0] + list_coarse.shape[0]
    width = ceil_to(list_fine.shape[1], LANES)
    slots, peers = asks_fine.shape[0] + asks_coarse.shape[0], asks_fine.shape[1]
    vmem = pl.BlockSpec(memory_space=pltpu.VMEM)
    return pl.pallas_call(
        functools.partial(plan_kernel, variants, coarse_at),
        out_specs=[vmem, vmem, pl.BlockSpec(memory_space=pltpu.SMEM)],
        out_shape=[
            shape_of((own, width), jnp.int32),
            shape_of((own + peers * slots, LANES), jnp.int32),
            shape_of((1,), jnp.int32),
        ],
        scratch_shapes=[pltpu.VMEM((2, 8, LANES), jnp.float32)],
        compiler_params=pltpu.CompilerParams(vmem_limit_bytes=VMEM_BYTES),
        name="plan",
    )(asks_fine, asks_coarse, list_fine, list_coarse)


def pack_rows(values, table, tile):
    pairs = values.shape[0] // 2
    even = values[pl.ds(0, pairs, stride=2), :].astype(jnp.int32)
    odd = values[pl.ds(1, pairs, stride=2), :].astype(jnp.int32)
    both = odd * 65536 + even
    for block in range(table.shape[0]):
        part = both[8 * block : 8 * block + 8]
        if part.shape[0] < 8:
            part = jnp.concatenate([part, jnp.zeros((8 - part.shape[0], LANES), jnp.int32)], axis=0)
        table[block, :, tile * LANES : (tile + 1) * LANES] = part


def scale_of(values):
    peak = jnp.max(jnp.max(jnp.abs(values), axis=0, keepdims=True), axis=1, keepdims=True)
    power = jnp.floor(jnp.log2(jnp.broadcast_to(jnp.maximum(peak, 1e-30), (8, LANES))))
    return jnp.exp2(13.0 - power)[0:1], jnp.exp2(power - 29.0)


def build_tables(ranges, to_ref, own_ref, arrived, rows_t, table_f, table, unit):
    peers, lines, _ = arrived.shape
    surface = rows_t.shape[0]
    extra = surface - LANES
    came = arrived[...].astype(jnp.float32)
    rest = came[:, lines - 8 :].reshape(peers * 8, LANES).T
    at = 0
    for g in range(lines // 8 - 1):
        part = came[:, 8 * g : 8 * g + 8].reshape(peers * 8, LANES).T
        part = jnp.concatenate([part, rest[g * extra : (g + 1) * extra]], axis=0)
        rows_t[:, at : at + peers * 8] = part.astype(jnp.bfloat16)
        at += peers * 8
    own = own_ref[...].astype(jnp.float32)
    rows_t[:, at : at + own.shape[0]] = own.T.astype(jnp.bfloat16)
    to = to_ref[...]
    tiles = table_f.shape[0]
    lanes = lane_iota(to.shape)
    for k in range(0, tiles, 2):
        size = min(2, tiles - k)
        hot = [(to == lanes + (k + h) * LANES).astype(jnp.float32) for h in range(size)]
        hot = jnp.concatenate([x.astype(jnp.bfloat16) for x in hot], axis=1)
        columns = jnp.dot(rows_t[...], hot, preferred_element_type=jnp.float32)
        for h in range(size):
            table_f[k + h] = columns[:, h * LANES : (h + 1) * LANES]
    for level, (low, high) in enumerate(ranges):
        factor, unit[level] = scale_of(jnp.max(jnp.abs(table_f[low:high]), axis=0))
        for k in range(low, high):
            table_f[k] = jnp.round(table_f[k] * factor)
            pack_rows(table_f.at[k], table, k)


def lay_pieces(surface, offsets, left, m_ref, stage, mr_ref):
    _, step_b, width = m_ref.shape
    tiles = width // LANES

    def spread(group, tile, first):
        inside = lane_iota((8, LANES)) < offsets - tile * LANES
        if group:
            row = lax.broadcasted_iota(jnp.int32, (8, LANES), 0) + group
            inside = inside & (row < left)
        for a in range(first, first + 19):
            part = m_ref[a, group : group + 8, tile * LANES : (tile + 1) * LANES]
            part = part.astype(jnp.float32)
            if group or (tile + 1) * LANES > offsets:
                part = jnp.where(inside, part, 0.0)
            stage[group // 8, tile, pl.ds(STAGE_A * a, 8, stride=STAGE_B), :] = part

    def lay(group, tile, j):
        rows = stage[group // 8, tile, pl.ds(STAGE_B * j, surface, stride=STAGE_A), :]
        at = ((group + j) * tiles + tile) * LANES
        mr_ref[0:surface, at : at + LANES] = rows.astype(jnp.bfloat16)

    for group in range(0, step_b, 8):
        for tile in range(tiles):
            for first in range(0, surface, 19):
                yield functools.partial(spread, group, tile, first)
            for j in range(8):
                yield functools.partial(lay, group, tile, j)


def product(acc, g_ref, mr_ref):
    acc[...] += lax.dot_general(
        g_ref[...],
        mr_ref[...],
        (((1,), (1,)), ((), ())),
        preferred_element_type=jnp.float32,
    )


def gather_pieces(step, levels, idx_ref, table, g_ref):
    width = idx_ref.shape[1]
    for low, high, base, tiles in levels:
        rows = [
            [
                jnp.broadcast_to(
                    table[step, q : q + 1, (base + k) * LANES : (base + k + 1) * LANES],
                    (8, LANES),
                )
                for k in range(tiles)
            ]
            for q in range(PAIRS)
        ]

        def words(rows, tiles, target, first):
            idx = idx_ref[target : target + 8, first : first + LANES]
            at = idx & (LANES - 1)
            later = [idx >= k * LANES for k in range(1, tiles)]
            blank = idx < 0
            values = []
            for q in range(PAIRS):
                value = None
                for k in range(tiles):
                    got = jnp.take_along_axis(rows[q][k], at, axis=1, mode="promise_in_bounds")
                    value = got if k == 0 else jnp.where(later[k - 1], got, value)
                values.append(jnp.where(blank, 0, value))
            return values

        def unit(rows, tiles, target, first):
            upper = words(rows, tiles, target, first)
            lower = words(rows, tiles, target + 8, first)
            for q in range(PAIRS):
                value = jnp.concatenate([upper[q], lower[q]], axis=0)
                low_half = (value << 16).astype(jnp.float32).astype(jnp.bfloat16)
                high_half = value.astype(jnp.float32).astype(jnp.bfloat16)
                to = 2 * q * width + first
                g_ref[target : target + CHUNK, to : to + LANES] = low_half
                to = to + width
                g_ref[target : target + CHUNK, to : to + LANES] = high_half

        for first in range(0, width, LANES):
            for target in range(low, high, CHUNK):
                yield functools.partial(unit, rows, tiles, target, first)


def interleave(main, others):
    done = 0
    for n, piece in enumerate(main):
        piece()
        until = (n + 1) * len(others) // len(main)
        for other in others[done:until]:
            other()
        done = until


def translate_kernel(
    variants,
    coarse_tile,
    offsets,
    pick_ref,
    idx_ref,
    to_ref,
    own_ref,
    arrived_any,
    m_ref,
    of_ref,
    oc_ref,
    rows_t,
    table_f,
    table,
    unit,
    arrived,
    stage,
    acc,
    mr,
    g,
    sem,
):
    fine_own, targets = of_ref.shape[0], idx_ref.shape[0]
    step = pl.program_id(0)

    @pl.when(step == 0)
    def _():
        fetch = pltpu.make_async_copy(arrived_any, arrived, sem)
        fetch.start()
        fetch.wait()
        build_tables(
            ((0, coarse_tile), (coarse_tile, table_f.shape[0])),
            to_ref,
            own_ref,
            arrived,
            rows_t,
            table_f,
            table,
            unit,
        )

    def work(fine_tiles, coarse_tiles):
        levels = (
            (0, fine_own, 0, fine_tiles),
            (fine_own, targets, coarse_tile, coarse_tiles),
        )
        surface = of_ref.shape[1]
        left = surface - step * 2 * PAIRS
        product(acc, g, mr)
        interleave(
            list(gather_pieces(step, levels, idx_ref, table, g)),
            list(lay_pieces(surface, offsets, left, m_ref, stage, mr)),
        )

    for at, tiles in enumerate(variants):
        pl.when(pick_ref[0] == at)(functools.partial(work, *tiles))

    @pl.when(step == 0)
    def _():
        acc[...] = jnp.zeros_like(acc)

    @pl.when(step == pl.num_programs(0) - 1)
    def _():
        product(acc, g, mr)
        of_ref[...] = acc[0:fine_own, 0 : of_ref.shape[1]] * unit[0, 0:1, 0:1]
        oc_ref[...] = acc[fine_own:targets, 0 : of_ref.shape[1]] * (0.5 * unit[1, 0:1, 0:1])


def translate(
    pick, idx, to, own_rows, arrived, m2l_ops, variants, coarse_tile, tiles, fine_own
):
    surface, _, offsets = m2l_ops.shape
    width = ceil_to(offsets, LANES)
    targets = idx.shape[0]
    coarse_own = targets - fine_own
    blocks = pl.cdiv(surface, 2 * PAIRS)
    return pl.pallas_call(
        functools.partial(translate_kernel, variants, coarse_tile, offsets),
        grid=(blocks,),
        in_specs=[
            pl.BlockSpec(memory_space=pltpu.SMEM),
            whole(idx),
            whole(to),
            whole(own_rows),
            pl.BlockSpec(memory_space=pl.ANY),
            pl.BlockSpec((surface, 2 * PAIRS, width), lambda i: (0, i, 0)),
        ],
        out_specs=[
            pl.BlockSpec((fine_own, surface), lambda i: (0, 0)),
            pl.BlockSpec((coarse_own, surface), lambda i: (0, 0)),
        ],
        out_shape=[
            shape_of((fine_own, surface), jnp.float32),
            shape_of((coarse_own, surface), jnp.float32),
        ],
        scratch_shapes=[
            pltpu.VMEM((surface, to.shape[0]), jnp.bfloat16),
            pltpu.VMEM((tiles, surface, LANES), jnp.float32),
            pltpu.VMEM((blocks, 8, tiles * LANES), jnp.int32),
            pltpu.VMEM((2, 8, LANES), jnp.float32),
            pltpu.VMEM(arrived.shape, jnp.bfloat16),
            pltpu.VMEM(
                (PAIRS // 4, width // LANES, ceil_to(STAGE_A * surface, 8), LANES), jnp.float32
            ),
            pltpu.VMEM((targets, ceil_to(surface, 2 * LANES)), jnp.float32),
            pltpu.VMEM((ceil_to(surface, 2 * LANES), 2 * PAIRS * width), jnp.bfloat16),
            pltpu.VMEM((targets, 2 * PAIRS * width), jnp.bfloat16),
            pltpu.SemaphoreType.DMA,
        ],
        compiler_params=pltpu.CompilerParams(vmem_limit_bytes=48 << 20),
        cost_estimate=pl.CostEstimate(
            flops=2 * surface * surface * targets * width,
            bytes_accessed=2 * surface * surface * width,
            transcendentals=0,
        ),
        name="translate",
    )(pick, idx, to, own_rows, arrived, m2l_ops)


def exchange(x):
    return lax.all_to_all(x, AXES, split_axis=0, concat_axis=0, tiled=True)


def body(
    dens_fine, parent, child_code, m2m_ops, m2l_ops, ask_fine, list_fine, ask_coarse, list_coarse
):
    surface, fine_own = dens_fine.shape
    coarse_own = list_coarse.shape[0]
    asks_fine, asks_coarse = ask_fine[0].T, ask_coarse[0].T
    fine_cap, peers = asks_fine.shape
    coarse_cap = asks_coarse.shape[0]
    wanted = exchange(join_asks(asks_fine, asks_coarse, fine_own))

    fine_tiles = ceil_to(fine_own - LOCAL + (peers - 1) * fine_cap, LANES) // LANES
    coarse_tiles = ceil_to(coarse_own + (peers - 1) * coarse_cap, LANES) // LANES
    variants = [(min(n, fine_tiles), min(2, coarse_tiles)) for n in (3, 4)]
    variants = variants + [(fine_tiles, coarse_tiles)]
    idx, to, pick = plan(
        asks_fine, asks_coarse, list_fine, list_coarse, variants, fine_tiles * LANES
    )

    fine_rows = dens_fine.T
    positions = jnp.arange(8, dtype=jnp.int32)
    spread = jnp.where(
        (child_code[:, None] == positions[None, :])[:, :, None],
        fine_rows[:, None, :],
        jnp.zeros((), jnp.bfloat16),
    )
    child_terms = lax.dot_general(
        spread.reshape(fine_own, 8 * surface),
        m2m_ops.reshape(surface, 8 * surface),
        (((1,), (1,)), ((), ())),
        preferred_element_type=jnp.float32,
    )
    local_parent = parent - lax.axis_index(AXES) * coarse_own
    members = (jnp.arange(coarse_own, dtype=jnp.int32)[:, None] == local_parent[None, :]).astype(
        jnp.float32
    )
    coarse_rows = jnp.dot(members, child_terms, precision=lax.Precision.HIGHEST).astype(
        jnp.bfloat16
    )

    own_rows = jnp.concatenate([fine_rows, coarse_rows], axis=0)
    arrived = exchange(answer(wanted, own_rows))
    pot_fine, pot_coarse = translate(
        pick,
        idx,
        to,
        own_rows,
        arrived,
        m2l_ops,
        variants,
        fine_tiles,
        fine_tiles + coarse_tiles,
        fine_own,
    )
    return pot_fine.T, pot_coarse.T


def solution(mesh):
    return jax.shard_map(
        body,
        mesh=mesh,
        in_specs=(
            P(None, AXES),
            P(AXES),
            P(AXES),
            P(),
            P(),
            P(AXES, None, None),
            P(AXES, None),
            P(AXES, None, None),
            P(AXES, None),
        ),
        out_specs=(P(None, AXES), P(None, AXES)),
        check_vma=False,
    )
```
